32 devices in a mesh: groups: 2 (over y), blk: 4 (over z), mpo: 2 (over x), rep: 2 (over core).
Axes of the slice: x: 2, y: 2, z: 4, core: 2. Of those that a mesh axis runs over, the one named last changes fastest.
Arguments:
- wavefunction: bfloat16 [16, 256, 256], P(('groups', 'blk', 'rep')), parts along dimension 0
- env_left: bfloat16 [48, 16, 256, 256], P('mpo', ('groups', 'blk', 'rep')), parts along dimension 1
- env_right: bfloat16 [48, 16, 256, 256], P('mpo', ('groups', 'blk', 'rep')), parts along dimension 1
- channel_class: int32 [48], P('mpo'), may hold values from 0 to 4
Outputs:
- basis: bfloat16 [3, 16, 256, 256], P(None, ('groups', 'blk', 'rep'), 'mpo'), parts along dimension 1
- coeffs: float32 [4, 3], P('groups'), parts along dimension 0
The draws below stay inside these ranges and needn't reach their ends.
There are 2 independent parts, one for each index of `groups`. The reference program is written for one: setup_inputs(seed, part) draws one part's arguments, and reference() takes and returns one part's arrays. A program takes and returns all parts, laid end to end along the dimension named above; an argument that names none is the same for every part. Nothing has to cross between parts.
Inputs may be any that keep to these rules, and one draw needn't show every extreme that they name: `channel_class`: class 0 keeps both quantum numbers; classes 1 and 2 raise the particle number with spin up and down; classes 3 and 4 lower it with spin up and down.
All inputs are finite; a program needn't handle non-finite values.
Results may differ from the reference program's by a relative error of at most 0.018.
Values may be sent and summed in bfloat16 or wider, within the bound.
No kernel may reach another device: no remote copies, remote signals or barrier semaphores. Data moves between devices by JAX's collectives and lax.ppermute only.
A program may use at most 64 MiB of HBM per device.

```python
import jax
import jax.numpy as jnp
from jax import lax

S = 256
K = 48
NS = 4
STEPS = 3
NB = 8


def environment(key, normal_weight):
    keys = jax.random.split(key, 2)
    diagonal = jax.random.uniform(keys[0], (K, NB, S, 1), jnp.float32, 0.3, 0.7)
    identity = jnp.eye(S, dtype=jnp.float32)
    spread = normal_weight * jax.random.normal(keys[1], (K, NB, S, S), jnp.float32)
    return (diagonal * identity + spread / jnp.sqrt(jnp.float32(S))).astype(jnp.bfloat16)


def draw_env_left(key, part):
    key = jax.random.fold_in(key, 23)
    return environment(key, 0.5)


def draw_env_right(key, part):
    key = jax.random.fold_in(key, 37)
    return environment(key, 0.5)


def draw_wavefunction(key, part):
    key = jax.random.fold_in(key, 11)
    sector_scale = jnp.exp(jnp.log(3.0) * jnp.arange(NB, dtype=jnp.float32) / (NB - 1))[:, None, None]
    values = jax.random.normal(key, (NB, S, S), jnp.float32)
    return (values * sector_scale).astype(jnp.bfloat16)


def set_ends(values, key, smallest, top_value):
    dims = values.shape
    spot = [jax.random.randint(jax.random.fold_in(key, axis), (), 0, dims[axis]) for axis in range(len(dims))]
    values = values.at[tuple(spot)].set(smallest)
    longest = dims.index(max(dims))
    spot[longest] = (spot[longest] + 1) % dims[longest]
    return values.at[tuple(spot)].set(top_value)


def setup_inputs(seed: int = 0, part: int = 0) -> dict:
    key_of = jax.random.split(jax.random.key(seed), 5)
    own_keys = jax.random.split(jax.random.fold_in(key_of[4], part), 5)
    wavefunction = draw_wavefunction(jax.random.fold_in(jax.random.fold_in(key_of[4], part), 71), part)
    env_left = draw_env_left(jax.random.fold_in(jax.random.fold_in(key_of[4], part), 71), part)
    env_right = draw_env_right(jax.random.fold_in(jax.random.fold_in(key_of[4], part), 71), part)
    channel_class = set_ends(jax.random.randint(key_of[3], (K,), 0, 5), jax.random.fold_in(key_of[3], 1), 0, 4).astype(jnp.int32)
    return dict(wavefunction=wavefunction, env_left=env_left, env_right=env_right, channel_class=channel_class)


epsilon = 1e-06

def displace(vector, offset):
    blank = jnp.zeros((abs(offset),) + vector.shape[1:], vector.dtype)
    if offset > 0:
        return jnp.concatenate([blank, vector[:-offset]], 0)
    return jnp.concatenate([vector[-offset:], blank], 0)

def sources(vector):
    spin_index = jnp.arange(NB) % NS
    keep_low = (spin_index >= 1).astype(jnp.bfloat16)[:, None, None]
    keep_high = (spin_index <= NS - 2).astype(jnp.bfloat16)[:, None, None]
    return jnp.stack([vector, displace(vector, NS + 1) * keep_low, displace(vector, NS - 1) * keep_high, displace(vector, -(NS + 1)) * keep_high, displace(vector, -(NS - 1)) * keep_low])

def apply_hamiltonian(vector, env_left, env_right, channel_class):
    candidates = sources(vector)

    def add_channel(running, channel_data):
        left_piece, right_piece, kind = channel_data
        picked = lax.dynamic_index_in_dim(candidates, kind, 0, keepdims=False)
        partial_value = jnp.einsum('nij,njl->nil', left_piece.astype(jnp.float32), picked.astype(jnp.float32)).astype(jnp.bfloat16)
        return (running + jnp.einsum('nij,nlj->nil', partial_value.astype(jnp.float32), right_piece.astype(jnp.float32)), None)
    running, _ = lax.scan(add_channel, jnp.zeros(vector.shape, jnp.float32), (env_left, env_right, channel_class))
    return running

def reference(wavefunction, env_left, env_right, channel_class):
    entries = NB * S * S
    initial = wavefunction.astype(jnp.float32)
    start_value = jnp.sqrt(jnp.sum(initial * initial) / entries + epsilon)
    vector = (initial / start_value).astype(jnp.bfloat16)
    previous = jnp.zeros(wavefunction.shape, jnp.float32)
    beta_prev = jnp.zeros((), jnp.float32)
    basis_list, alphas, beta_list = ([], [], [])
    for iteration in range(STEPS):
        product = apply_hamiltonian(vector, env_left, env_right, channel_class)
        current = vector.astype(jnp.float32)
        alpha_now = jnp.sum(current * product) / entries
        residue = product - alpha_now * current - beta_prev * previous
        beta_now = jnp.sqrt(jnp.sum(residue * residue) / entries + epsilon)
        upcoming = (residue / beta_now).astype(jnp.bfloat16)
        basis_list.append(upcoming)
        alphas.append(alpha_now)
        beta_list.append(beta_now)
        previous = current
        beta_prev = beta_now
        vector = upcoming
    return (jnp.stack(basis_list), jnp.stack([jnp.stack(alphas), jnp.stack(beta_list)]))
```

```python
import functools

import jax
import jax.numpy as jnp
from jax import lax
from jax.experimental import pallas as pl
from jax.experimental.pallas import tpu as pltpu
from jax.sharding import PartitionSpec as P

NS = 4
STEPS = 3
OFFSETS = (0, NS + 1, NS - 1, -(NS + 1), -(NS - 1))
EPSILON = 1e-06
UNROLL = 2
VMEM = pl.BlockSpec(memory_space=pltpu.VMEM)
SMEM = pl.BlockSpec(memory_space=pltpu.SMEM)
ANY = pl.BlockSpec(memory_space=pl.ANY)


def reaches(kind, sector, blocks):
    source = sector - OFFSETS[kind]
    spin = sector % NS
    inside = (source >= 0) & (source < blocks)
    if kind in (1, 4):
        return inside & (spin >= 1)
    if kind in (2, 3):
        return inside & (spin <= NS - 2)
    return inside


def routes(blocks):
    lists = {}
    for kind in range(1, 5):
        lists[kind] = [
            (k - OFFSETS[kind], k) for k in range(blocks) if bool(reaches(kind, k, blocks))
        ]
    permutes, place = [], {}
    for up, down in ((1, 3), (2, 4)):
        both = lists[up] + lists[down]
        disjoint = len({a for a, _ in both}) == len(both) == len({b for _, b in both})
        groups = ((up, down),) if disjoint else ((up,), (down,))
        for group in groups:
            for kind in group:
                place[kind] = len(permutes)
            permutes.append([pair for kind in group for pair in lists[kind]])
    return permutes, place


def lane_of(rows, lane):
    return rows[:, lane : lane + 1]


def pack(values, shape):
    lanes = lax.broadcasted_iota(jnp.int32, shape, 1)
    out = jnp.zeros(shape, jnp.float32)
    for place, value in enumerate(values):
        out = jnp.where(lanes == place, value, out)
    return out


def total(x):
    return jnp.sum(jnp.sum(x, axis=0, keepdims=True), axis=1, keepdims=True)


def norm_kernel(psi_ref, rows_ref):
    psi = psi_ref[0].astype(jnp.float32)
    rows_ref[...] = pack([total(psi * psi)], rows_ref.shape)


def sum_parts(parts_ref):
    w = parts_ref[0].astype(jnp.float32)
    for part in range(1, parts_ref.shape[0]):
        w += parts_ref[part].astype(jnp.float32)
    return w


def middle_kernel(first, last, *refs):
    parts, (v_ref, vp_ref, scal_ref, w_ref, rows_ref) = refs[:-5], refs[-5:]
    w = parts[0][...].astype(jnp.float32)
    for part in parts[1:]:
        w += part[...].astype(jnp.float32)
    if not last:
        w_ref[...] = w.astype(jnp.bfloat16)
    v = v_ref[0].astype(jnp.float32)
    a = total(v * w)
    d = total(v * v)
    local = a / jnp.maximum(d, 1e-30)
    r = w - local * v
    if not first:
        r -= lane_of(scal_ref[0:1, :], 1) * vp_ref[0].astype(jnp.float32)
    if last:
        w_ref[...] = w
    rows_ref[...] = pack([a, d, local, total(r * v), total(r * r)], rows_ref.shape)


def coefficients(rows, entries):
    a, d, local, p, q = (lane_of(rows, lane) for lane in range(5))
    alpha = jnp.sum(a, axis=0, keepdims=True) / entries
    off = local - alpha
    square = jnp.sum(q + off * (2.0 * p + off * d), axis=0, keepdims=True)
    beta = jnp.sqrt(jnp.maximum(square, 0.0) / entries + EPSILON)
    return alpha, beta


def product_kernel(step, slots, place, blocks, entries, *refs):
    refs = list(refs)
    kinds_ref, left_hbm, right_hbm, rows_ref = refs[:4]
    refs = refs[4:]
    fresh, refs = refs[:slots], refs[slots:]
    if step >= 1:
        v_ref, refs = refs[0], refs[1:]
    if step >= 2:
        vp_ref, scal_ref, refs = refs[0], refs[1], refs[2:]
    t_ref, v_out, scal_out, left, right, acc, order, slot_of, sems = refs
    channels = left_hbm.shape[0]
    sector = lax.axis_index("blk") * lax.axis_size("rep") + lax.axis_index("rep")

    def list_channel(b, count):
        kind = kinds_ref[b]
        live = kind == 0
        slot = jnp.int32(0)
        for c in range(1, 5):
            live = live | ((kind == c) & reaches(c, sector, blocks))
            slot = jnp.where(kind == c, 1 + place[c], slot)

        @pl.when(live)
        def _():
            order[count] = b
            slot_of[count] = slot
            pltpu.make_async_copy(left_hbm.at[b], left.at[count], sems.at[0, count]).start()
            pltpu.make_async_copy(right_hbm.at[b], right.at[count], sems.at[1, count]).start()

        return count + live.astype(jnp.int32)

    count = lax.fori_loop(0, channels, list_channel, jnp.int32(0))
    for extra in range(UNROLL - 1):
        order[count + extra] = 0
        slot_of[count + extra] = slots

    rows = rows_ref[...]
    if step == 0:
        beta = jnp.sqrt(jnp.sum(lane_of(rows, 0), axis=0, keepdims=True) / entries + EPSILON)
        alpha = jnp.zeros_like(beta)
    else:
        alpha, beta = coefficients(rows, entries)
    scal_out[...] = pack([alpha, beta], scal_out.shape)
    for slot in range(slots):
        block = fresh[slot][0] if step == 0 else fresh[slot][...]
        r = block.astype(jnp.float32)
        if step >= 1:
            r -= alpha * v_ref[slot].astype(jnp.float32)
        if step >= 2:
            r -= lane_of(scal_ref[0:1, :], 1) * vp_ref[slot].astype(jnp.float32)
        v_out[slot] = (r / beta).astype(jnp.bfloat16)
    v_out[slots] = jnp.zeros(v_out.shape[1:], jnp.bfloat16)
    acc[...] = jnp.zeros_like(acc)

    def multiply(group, carry):
        result = None
        for inner in range(UNROLL):
            at = group * UNROLL + inner
            live = at < count

            @pl.when(live)
            def _():
                pltpu.make_async_copy(left_hbm.at[0], left.at[at], sems.at[0, at]).wait()
                pltpu.make_async_copy(right_hbm.at[0], right.at[at], sems.at[1, at]).wait()

        for inner in range(UNROLL):
            at = group * UNROLL + inner
            held = jnp.where(at < count, at, 0)
            piece = jnp.dot(
                left[held], v_out[slot_of[at]], preferred_element_type=jnp.float32
            ).astype(jnp.bfloat16)
            term = lax.dot_general(
                piece, right[held], (((1,), (1,)), ((), ())), preferred_element_type=jnp.float32
            )
            result = term if result is None else result + term
        acc[...] += result
        return carry

    lax.fori_loop(0, (count + UNROLL - 1) // UNROLL, multiply, 0)
    t_ref[...] = acc[...].astype(jnp.bfloat16)


def final_kernel(entries, rows_ref, w_ref, v3_ref, v2_ref, scal1_ref, scal2_ref, basis_ref, coef_ref):
    share = basis_ref.shape[2]
    start = pl.multiple_of(lax.axis_index("mpo") * share, share)
    mine = pl.ds(start, share)
    alpha, beta = coefficients(rows_ref[...], entries)
    v3, v2 = v3_ref[0, mine, :], v2_ref[0, mine, :]
    r = w_ref[mine, :] - alpha * v3.astype(jnp.float32)
    r -= lane_of(scal2_ref[0:1, :], 1) * v2.astype(jnp.float32)
    basis_ref[0, 0] = v2
    basis_ref[1, 0] = v3
    basis_ref[2, 0] = (r / beta).astype(jnp.bfloat16)
    row = lax.broadcasted_iota(jnp.int32, coef_ref.shape, 0)
    column = lax.broadcasted_iota(jnp.int32, coef_ref.shape, 1)
    out = jnp.zeros(coef_ref.shape, jnp.float32)
    pairs = [(lane_of(s[0:1, :], 0), lane_of(s[0:1, :], 1)) for s in (scal1_ref, scal2_ref)]
    for step, (a, b) in enumerate(pairs + [(alpha, beta)]):
        out = jnp.where(column == step, jnp.where(row == 0, a, b), out)
    coef_ref[...] = out


def shards(wavefunction, env_left, env_right, channel_class):
    width = wavefunction.shape[1]
    ring = ("blk", "rep")
    parts = lax.axis_size("mpo")
    blocks = lax.axis_size("blk") * lax.axis_size("rep")
    entries = blocks * width * width
    permutes, place = routes(blocks)
    slots = 1 + len(permutes)
    channels = channel_class.shape[0]
    left, right = env_left[:, 0], env_right[:, 0]
    rows_shape = jax.ShapeDtypeStruct((blocks, 128), jnp.float32)
    block_f32 = jax.ShapeDtypeStruct((width, width), jnp.float32)
    block_bf16 = jax.ShapeDtypeStruct((width, width), jnp.bfloat16)

    def exchange(rows):
        return lax.all_to_all(rows, ring, 0, 0, tiled=True)

    def gather_parts(t):
        if parts == 2:
            return [t, lax.ppermute(t, "mpo", [(0, 1), (1, 0)])]
        held = lax.all_gather(t, "mpo")
        return [held[i] for i in range(parts)]

    def product(step, fresh, rows, *old):
        return pl.pallas_call(
            functools.partial(product_kernel, step, slots, place, blocks, entries),
            out_shape=(
                block_bf16,
                jax.ShapeDtypeStruct((slots + 1, width, width), jnp.bfloat16),
                jax.ShapeDtypeStruct((8, 128), jnp.float32),
            ),
            in_specs=[SMEM, ANY, ANY] + [VMEM] * (1 + len(fresh) + len(old)),
            out_specs=(VMEM,) * 3,
            scratch_shapes=[
                pltpu.VMEM((channels, width, width), jnp.bfloat16),
                pltpu.VMEM((channels, width, width), jnp.bfloat16),
                pltpu.VMEM((width, width), jnp.float32),
                pltpu.SMEM((channels + UNROLL,), jnp.int32),
                pltpu.SMEM((channels + UNROLL,), jnp.int32),
                pltpu.SemaphoreType.DMA((2, channels)),
            ],
            compiler_params=pltpu.CompilerParams(vmem_limit_bytes=32 * 1024 * 1024),
            name="product",
        )(channel_class, left, right, rows, *fresh, *old)

    def middle(first, last, t, v, vp, scal):
        pieces = gather_parts(t)
        return pl.pallas_call(
            functools.partial(middle_kernel, first, last),
            out_shape=(block_f32 if last else block_bf16, rows_shape),
            in_specs=[VMEM] * (len(pieces) + 3),
            out_specs=(VMEM, VMEM),
            name="middle",
        )(*pieces, v, vp, scal)

    def spread(block):
        return [block] + [lax.ppermute(block, ring, pairs) for pairs in permutes]

    fresh = spread(wavefunction)
    rows = pl.pallas_call(norm_kernel, out_shape=rows_shape, in_specs=[VMEM], out_specs=VMEM, name="norm")(
        wavefunction
    )
    t, v1, scal0 = product(0, fresh, exchange(rows))
    w, rows = middle(True, False, t, v1, v1, scal0)
    fresh = spread(w)
    t, v2, scal1 = product(1, fresh, exchange(rows), v1)
    w, rows = middle(False, False, t, v2, v1, scal1)
    fresh = spread(w)
    t, v3, scal2 = product(2, fresh, exchange(rows), v2, v1, scal1)
    w, rows = middle(False, True, t, v3, v2, scal2)
    basis, coefs = pl.pallas_call(
        functools.partial(final_kernel, entries),
        out_shape=(
            jax.ShapeDtypeStruct((STEPS, 1, width // parts, width), jnp.bfloat16),
            jax.ShapeDtypeStruct((2, STEPS), jnp.float32),
        ),
        in_specs=[VMEM] * 6,
        out_specs=(VMEM, VMEM),
        name="final",
    )(exchange(rows), w, v3, v2, scal1, scal2)
    return basis, coefs


def solution(mesh):
    return jax.shard_map(
        shards,
        mesh=mesh,
        in_specs=(
            P(("groups", "blk", "rep"), None, None),
            P("mpo", ("groups", "blk", "rep"), None, None),
            P("mpo", ("groups", "blk", "rep"), None, None),
            P("mpo"),
        ),
        out_specs=(P(None, ("groups", "blk", "rep"), "mpo", None), P("groups", None)),
        check_vma=False,
    )
```

```python
import functools

import jax
import jax.numpy as jnp
from jax import lax
from jax.experimental import pallas as pl
from jax.experimental.pallas import tpu as pltpu
from jax.sharding import PartitionSpec as P

NS = 4
STEPS = 3
OFFSETS = (0, NS + 1, NS - 1, -(NS + 1), -(NS - 1))
EPSILON = 1e-06
WIDE = 8
VMEM = pl.BlockSpec(memory_space=pltpu.VMEM)
SMEM = pl.BlockSpec(memory_space=pltpu.SMEM)
MIB = 1024 * 1024


def reaches(kind, sector, blocks):
    source = sector - OFFSETS[kind]
    spin = sector % NS
    inside = (source >= 0) & (source < blocks)
    if kind in (1, 4):
        return inside & (spin >= 1)
    if kind in (2, 3):
        return inside & (spin <= NS - 2)
    return inside


def routes(blocks):
    lists = {}
    for kind in range(1, 5):
        lists[kind] = [
            (k - OFFSETS[kind], k) for k in range(blocks) if bool(reaches(kind, k, blocks))
        ]
    permutes, place = [], {}
    for up, down in ((1, 3), (2, 4)):
        both = lists[up] + lists[down]
        disjoint = len({a for a, _ in both}) == len(both) == len({b for _, b in both})
        groups = ((up, down),) if disjoint else ((up,), (down,))
        for group in groups:
            for kind in group:
                place[kind] = len(permutes)
            permutes.append([pair for kind in group for pair in lists[kind]])
    return permutes, place


def lane_of(rows, lane):
    return rows[:, lane : lane + 1]


def pack(values, shape):
    lanes = lax.broadcasted_iota(jnp.int32, shape, 1)
    out = jnp.zeros(shape, jnp.float32)
    for place, value in enumerate(values):
        out = jnp.where(lanes == place, value, out)
    return out


def total(x):
    return jnp.sum(jnp.sum(x, axis=0, keepdims=True), axis=1, keepdims=True)


def norm_kernel(psi_ref, rows_ref):
    psi = psi_ref[0].astype(jnp.float32)
    rows_ref[...] = pack([total(psi * psi)], rows_ref.shape)


def sum_parts(parts_ref):
    w = parts_ref[0].astype(jnp.float32)
    for part in range(1, parts_ref.shape[0]):
        w += parts_ref[part].astype(jnp.float32)
    return w


def middle_kernel(first, last, *refs):
    parts, (v_ref, vp_ref, scal_ref, w_ref, rows_ref) = refs[:-5], refs[-5:]
    w = parts[0][...].astype(jnp.float32)
    for part in parts[1:]:
        w += part[...].astype(jnp.float32)
    if not last:
        w_ref[...] = w.astype(jnp.bfloat16)
    v = v_ref[0].astype(jnp.float32)
    a = total(v * w)
    d = total(v * v)
    local = a / jnp.maximum(d, 1e-30)
    r = w - local * v
    if not first:
        r -= lane_of(scal_ref[0:1, :], 1) * vp_ref[0].astype(jnp.float32)
    if last:
        w_ref[...] = w
    rows_ref[...] = pack([a, d, local, total(r * v), total(r * r)], rows_ref.shape)


def coefficients(rows, entries):
    a, d, local, p, q = (lane_of(rows, lane) for lane in range(5))
    alpha = jnp.sum(a, axis=0, keepdims=True) / entries
    off = local - alpha
    square = jnp.sum(q + off * (2.0 * p + off * d), axis=0, keepdims=True)
    beta = jnp.sqrt(jnp.maximum(square, 0.0) / entries + EPSILON)
    return alpha, beta


def product_kernel(step, slots, place, blocks, entries, *refs):
    refs = list(refs)
    kinds_ref, left_ref, right_ref, rows_ref = refs[:4]
    refs = refs[4:]
    fresh, refs = refs[:slots], refs[slots:]
    if step >= 1:
        v_ref, refs = refs[0], refs[1:]
    if step >= 2:
        vp_ref, scal_ref, refs = refs[0], refs[1], refs[2:]
    t_ref, v_out, scal_out, acc, order, slot_of = refs
    channels = kinds_ref.shape[0]
    sector = lax.axis_index("blk") * lax.axis_size("rep") + lax.axis_index("rep")
    reached = [jnp.int32(1)] + [reaches(c, sector, blocks).astype(jnp.int32) for c in range(1, 5)]

    def list_channel(b, count):
        kind = kinds_ref[b]
        live, slot = reached[0], jnp.int32(0)
        for c in range(1, 5):
            live = jnp.where(kind == c, reached[c], live)
            slot = jnp.where(kind == c, 1 + place[c], slot)
        order[count] = b
        slot_of[count] = slot
        return count + live

    count = lax.fori_loop(0, channels, list_channel, jnp.int32(0))
    for extra in range(WIDE):
        order[count + extra] = 0
        slot_of[count + extra] = slots

    rows = rows_ref[...]
    if step == 0:
        beta = jnp.sqrt(jnp.sum(lane_of(rows, 0), axis=0, keepdims=True) / entries + EPSILON)
        alpha = jnp.zeros_like(beta)
    else:
        alpha, beta = coefficients(rows, entries)
    scal_out[...] = pack([alpha, beta], scal_out.shape)
    inverse = 1.0 / beta
    for slot in range(slots):
        block = fresh[slot][0] if step == 0 else fresh[slot][...]
        r = block.astype(jnp.float32)
        if step >= 1:
            r -= alpha * v_ref[slot].astype(jnp.float32)
        if step >= 2:
            r -= lane_of(scal_ref[0:1, :], 1) * vp_ref[slot].astype(jnp.float32)
        v_out[slot] = (r * inverse).astype(jnp.bfloat16)
    v_out[slots] = jnp.zeros(v_out.shape[1:], jnp.bfloat16)
    acc[...] = jnp.zeros_like(acc)

    def multiply(start, wide):
        held = [order[start + inner] for inner in range(wide)]
        pieces = [
            jnp.dot(
                left_ref[b], v_out[slot_of[start + inner]], preferred_element_type=jnp.float32
            ).astype(jnp.bfloat16)
            for inner, b in enumerate(held)
        ]
        acc[...] += lax.dot_general(
            jnp.concatenate(pieces, axis=1),
            jnp.concatenate([right_ref[b] for b in held], axis=1),
            (((1,), (1,)), ((), ())),
            preferred_element_type=jnp.float32,
        )

    def full(group, carry):
        multiply(group * WIDE, WIDE)
        return carry

    groups = count // WIDE
    lax.fori_loop(0, groups, full, 0)
    rest = count - groups * WIDE
    for low, wide in ((0, 2), (2, 4), (4, WIDE)):

        @pl.when((rest > low) & (rest <= wide))
        def _():
            multiply(groups * WIDE, wide)

    t_ref[...] = acc[...].astype(jnp.bfloat16)


def final_kernel(entries, rows_ref, w_ref, v3_ref, v2_ref, scal1_ref, scal2_ref, basis_ref, coef_ref):
    share = basis_ref.shape[2]
    start = pl.multiple_of(lax.axis_index("mpo") * share, share)
    mine = pl.ds(start, share)
    alpha, beta = coefficients(rows_ref[...], entries)
    v3, v2 = v3_ref[0, mine, :], v2_ref[0, mine, :]
    r = w_ref[mine, :] - alpha * v3.astype(jnp.float32)
    r -= lane_of(scal2_ref[0:1, :], 1) * v2.astype(jnp.float32)
    basis_ref[0, 0] = v2
    basis_ref[1, 0] = v3
    basis_ref[2, 0] = (r / beta).astype(jnp.bfloat16)
    row = lax.broadcasted_iota(jnp.int32, coef_ref.shape, 0)
    column = lax.broadcasted_iota(jnp.int32, coef_ref.shape, 1)
    out = jnp.zeros(coef_ref.shape, jnp.float32)
    pairs = [(lane_of(s[0:1, :], 0), lane_of(s[0:1, :], 1)) for s in (scal1_ref, scal2_ref)]
    for step, (a, b) in enumerate(pairs + [(alpha, beta)]):
        out = jnp.where(column == step, jnp.where(row == 0, a, b), out)
    coef_ref[...] = out


def shards(wavefunction, env_left, env_right, channel_class):
    width = wavefunction.shape[1]
    ring = ("blk", "rep")
    parts = lax.axis_size("mpo")
    blocks = lax.axis_size("blk") * lax.axis_size("rep")
    entries = blocks * width * width
    permutes, place = routes(blocks)
    slots = 1 + len(permutes)
    channels = channel_class.shape[0]
    left, right = env_left[:, 0], env_right[:, 0]
    rows_shape = jax.ShapeDtypeStruct((blocks, 128), jnp.float32)
    block_f32 = jax.ShapeDtypeStruct((width, width), jnp.float32)
    block_bf16 = jax.ShapeDtypeStruct((width, width), jnp.bfloat16)

    def exchange(rows):
        return lax.all_to_all(rows, ring, 0, 0, tiled=True)

    def gather_parts(t):
        if parts == 2:
            return [t, lax.ppermute(t, "mpo", [(0, 1), (1, 0)])]
        held = lax.all_gather(t, "mpo")
        return [held[i] for i in range(parts)]

    def product(step, fresh, rows, *old):
        return pl.pallas_call(
            functools.partial(product_kernel, step, slots, place, blocks, entries),
            out_shape=(
                block_bf16,
                jax.ShapeDtypeStruct((slots + 1, width, width), jnp.bfloat16),
                jax.ShapeDtypeStruct((8, 128), jnp.float32),
            ),
            in_specs=[SMEM] + [VMEM] * (3 + len(fresh) + len(old)),
            out_specs=(VMEM,) * 3,
            scratch_shapes=[
                pltpu.VMEM((width, width), jnp.float32),
                pltpu.SMEM((channels + WIDE,), jnp.int32),
                pltpu.SMEM((channels + WIDE,), jnp.int32),
            ],
            compiler_params=pltpu.CompilerParams(vmem_limit_bytes=16 * MIB),
            name="product",
        )(channel_class, left, right, rows, *fresh, *old)

    def middle(first, last, t, v, vp, scal):
        pieces = gather_parts(t)
        return pl.pallas_call(
            functools.partial(middle_kernel, first, last),
            out_shape=(block_f32 if last else block_bf16, rows_shape),
            in_specs=[VMEM] * (len(pieces) + 3),
            out_specs=(VMEM, VMEM),
            compiler_params=pltpu.CompilerParams(vmem_limit_bytes=4 * MIB),
            name="middle",
        )(*pieces, v, vp, scal)

    def spread(block):
        return [block] + [lax.ppermute(block, ring, pairs) for pairs in permutes]

    fresh = spread(wavefunction)
    rows = pl.pallas_call(
        norm_kernel,
        out_shape=rows_shape,
        in_specs=[VMEM],
        out_specs=VMEM,
        compiler_params=pltpu.CompilerParams(vmem_limit_bytes=4 * MIB),
        name="norm",
    )(wavefunction)
    t, v1, scal0 = product(0, fresh, exchange(rows))
    w, rows = middle(True, False, t, v1, v1, scal0)
    fresh = spread(w)
    t, v2, scal1 = product(1, fresh, exchange(rows), v1)
    w, rows = middle(False, False, t, v2, v1, scal1)
    fresh = spread(w)
    t, v3, scal2 = product(2, fresh, exchange(rows), v2, v1, scal1)
    w, rows = middle(False, True, t, v3, v2, scal2)
    basis, coefs = pl.pallas_call(
        functools.partial(final_kernel, entries),
        out_shape=(
            jax.ShapeDtypeStruct((STEPS, 1, width // parts, width), jnp.bfloat16),
            jax.ShapeDtypeStruct((2, STEPS), jnp.float32),
        ),
        in_specs=[VMEM] * 6,
        out_specs=(VMEM, VMEM),
        compiler_params=pltpu.CompilerParams(vmem_limit_bytes=4 * MIB),
        name="final",
    )(exchange(rows), w, v3, v2, scal1, scal2)
    return basis, coefs


def solution(mesh):
    return jax.shard_map(
        shards,
        mesh=mesh,
        in_specs=(
            P(("groups", "blk", "rep"), None, None),
            P("mpo", ("groups", "blk", "rep"), None, None),
            P("mpo", ("groups", "blk", "rep"), None, None),
            P("mpo"),
        ),
        out_specs=(P(None, ("groups", "blk", "rep"), "mpo", None), P("groups", None)),
        check_vma=False,
    )
```

```python
import functools

import jax
import jax.numpy as jnp
from jax import lax
from jax.experimental import pallas as pl
from jax.experimental.pallas import tpu as pltpu
from jax.sharding import PartitionSpec as P

NS = 4
STEPS = 3
OFFSETS = (0, NS + 1, NS - 1, -(NS + 1), -(NS - 1))
EPSILON = 1e-06
WIDE = 8
SMALLEST = 1e-30
MIB = 1024 * 1024
VMEM = pl.BlockSpec(memory_space=pltpu.VMEM)
SMEM = pl.BlockSpec(memory_space=pltpu.SMEM)


def reaches(kind, sector, blocks):
    source = sector - OFFSETS[kind]
    spin = sector % NS
    inside = (source >= 0) & (source < blocks)
    if kind in (1, 4):
        return inside & (spin >= 1)
    if kind in (2, 3):
        return inside & (spin <= NS - 2)
    return inside


def routes(blocks):
    lists = {}
    for kind in range(1, 5):
        lists[kind] = [
            (k - OFFSETS[kind], k) for k in range(blocks) if bool(reaches(kind, k, blocks))
        ]
    permutes, place = [], {}
    for up, down in ((1, 3), (2, 4)):
        both = lists[up] + lists[down]
        disjoint = len({a for a, _ in both}) == len(both) == len({b for _, b in both})
        groups = ((up, down),) if disjoint else ((up,), (down,))
        for group in groups:
            for kind in group:
                place[kind] = len(permutes)
            permutes.append([pair for kind in group for pair in lists[kind]])
    return permutes, place


def here():
    return lax.axis_index("blk") * lax.axis_size("rep") + lax.axis_index("rep")


def lane_of(rows, lane):
    return rows[:, lane : lane + 1]


def pack(values, shape):
    lanes = lax.broadcasted_iota(jnp.int32, shape, 1)
    out = jnp.zeros(shape, jnp.float32)
    for place, value in enumerate(values):
        out = jnp.where(lanes == place, value, out)
    return out


def total(x):
    return jnp.sum(jnp.sum(x, axis=0, keepdims=True), axis=1, keepdims=True)


def column_sum(x):
    return jnp.sum(x, axis=0, keepdims=True)


def peak(x):
    return jnp.max(jnp.max(jnp.abs(x), axis=0, keepdims=True), axis=1, keepdims=True)


def wide_float(ref):
    return ref[...].astype(jnp.float32)


def sum_parts(parts):
    w = wide_float(parts[0])
    for part in parts[1:]:
        w += wide_float(part)
    return w


def first_row(ref):
    return ref[0:1, :]


def list_channels(which, place, blocks, kinds_ref, order, slot_of, idle):
    sector = here()
    use_own = 0 if which == "rest" else 1
    reached = [jnp.int32(use_own)]
    for c in range(1, 5):
        reach = reaches(c, sector, blocks).astype(jnp.int32)
        reached.append(reach if which != "own" else jnp.int32(0))

    def list_channel(b, count):
        kind = kinds_ref[b]
        live, slot = reached[0], jnp.int32(0)
        for c in range(1, 5):
            live = jnp.where(kind == c, reached[c], live)
            slot = jnp.where(kind == c, 1 + place[c], slot)
        order[count] = b
        slot_of[count] = slot
        return count + live

    count = lax.fori_loop(0, kinds_ref.shape[0], list_channel, jnp.int32(0))
    for extra in range(WIDE):
        order[count + extra] = 0
        slot_of[count + extra] = idle
    return count


def multiply_listed(count, left_ref, right_ref, source, acc, order, slot_of):
    def multiply(start, wide):
        held = [order[start + inner] for inner in range(wide)]
        pieces = [
            jnp.dot(
                left_ref[b], source[slot_of[start + inner]], preferred_element_type=jnp.float32
            ).astype(jnp.bfloat16)
            for inner, b in enumerate(held)
        ]
        acc[...] += lax.dot_general(
            jnp.concatenate(pieces, axis=1),
            jnp.concatenate([right_ref[b] for b in held], axis=1),
            (((1,), (1,)), ((), ())),
            preferred_element_type=jnp.float32,
        )

    def full(group, carry):
        multiply(group * WIDE, WIDE)
        return carry

    groups = count // WIDE
    lax.fori_loop(0, groups, full, 0)
    rest = count - groups * WIDE
    for low, wide in ((0, 2), (2, 4), (4, WIDE)):

        @pl.when((rest > low) & (rest <= wide))
        def _():
            multiply(groups * WIDE, wide)


def own_kernel(scaled, place, blocks, kinds_ref, left_ref, right_ref, block_ref, acc, source, order, slot_of):
    count = list_channels("own", place, blocks, kinds_ref, order, slot_of, 1)
    if scaled:
        block = wide_float(block_ref)
        inverse = 1.0 / jnp.maximum(peak(block), SMALLEST)
        source[0] = (block * inverse).astype(jnp.bfloat16)
    else:
        source[0] = block_ref[...]
    source[1] = jnp.zeros(source.shape[1:], jnp.bfloat16)
    acc[...] = jnp.zeros_like(acc)
    multiply_listed(count, left_ref, right_ref, source, acc, order, slot_of)


def rest_kernel(scaled, slots, place, blocks, *refs):
    kinds_ref, left_ref, right_ref, own_ref = refs[:4]
    held, refs = refs[4 : 4 + slots], refs[4 + slots :]
    if scaled:
        t_ref, unit_ref, acc, source, order, slot_of = refs
    else:
        t_ref, acc, source, order, slot_of = refs
    count = list_channels("rest", place, blocks, kinds_ref, order, slot_of, slots)
    if scaled:
        peaks = [jnp.maximum(peak(wide_float(block)), SMALLEST) for block in held]
        unit = functools.reduce(jnp.maximum, peaks)
        unit_ref[...] = jnp.broadcast_to(unit, unit_ref.shape)
        inverse = 1.0 / unit
        for slot in range(1, slots):
            source[slot] = (wide_float(held[slot]) * inverse).astype(jnp.bfloat16)
        acc[...] = own_ref[...] * (peaks[0] * inverse)
    else:
        for slot in range(1, slots):
            source[slot] = held[slot][...]
        acc[...] = own_ref[...]
    source[slots] = jnp.zeros(source.shape[1:], jnp.bfloat16)
    multiply_listed(count, left_ref, right_ref, source, acc, order, slot_of)
    t_ref[...] = acc[...].astype(jnp.bfloat16)


def second_kernel(slots, place, blocks, entries, *refs):
    kinds_ref, left_ref, right_ref, rows_ref = refs[:4]
    products, psis = refs[4 : 4 + slots], refs[4 + slots : 4 + 2 * slots]
    t_ref, v_ref, scal_ref, acc, source, order, slot_of = refs[4 + 2 * slots :]
    count = list_channels("all", place, blocks, kinds_ref, order, slot_of, slots)
    rows = rows_ref[...]
    a, d, local, p, q, unit = (lane_of(rows, lane) for lane in range(6))
    beta_0 = jnp.sqrt(column_sum(unit * unit * d) / entries + EPSILON)
    start_inverse = 1.0 / beta_0
    gain = unit * start_inverse
    alpha = column_sum(gain * (gain * a)) / entries
    off = local - alpha
    square = column_sum(gain * (gain * (q + off * (2.0 * p + off * d))))
    beta = jnp.sqrt(jnp.maximum(square, 0.0) / entries + EPSILON)
    inverse = 1.0 / beta
    sector = here()
    row_of = lax.broadcasted_iota(jnp.int32, gain.shape, 0)
    for slot in range(slots):
        origin = sector
        for kind in range(1, 5):
            if 1 + place[kind] == slot:
                origin = jnp.where(reaches(kind, sector, blocks), sector - OFFSETS[kind], origin)
        gain_here = column_sum(jnp.where(row_of == origin, gain, 0.0))
        r = gain_here * wide_float(products[slot]) - (alpha * start_inverse) * wide_float(psis[slot])
        source[slot] = (r * inverse).astype(jnp.bfloat16)
        if slot == 0:
            scal_ref[...] = pack([alpha, beta, start_inverse, gain_here], scal_ref.shape)
            v_ref[...] = source[0]
    source[slots] = jnp.zeros(source.shape[1:], jnp.bfloat16)
    acc[...] = jnp.zeros_like(acc)
    multiply_listed(count, left_ref, right_ref, source, acc, order, slot_of)
    t_ref[...] = acc[...].astype(jnp.bfloat16)


def first_sums_kernel(*refs):
    parts, (psi_ref, unit_ref, w_ref, rows_ref) = refs[:-4], refs[-4:]
    w = sum_parts(parts)
    w_ref[...] = w.astype(jnp.bfloat16)
    unit = lane_of(first_row(unit_ref), 0)
    v = wide_float(psi_ref) * (1.0 / unit)
    a = total(v * w)
    d = total(v * v)
    local = a / jnp.maximum(d, SMALLEST)
    r = w - local * v
    rows_ref[...] = pack([a, d, local, total(r * v), total(r * r), unit], rows_ref.shape)


def shrink(scal):
    return 1.0 / (jnp.abs(lane_of(scal, 0)) + lane_of(scal, 1))


def second_sums_kernel(*refs):
    parts, (scal_ref, wide_ref, w_ref) = refs[:-3], refs[-3:]
    w = sum_parts(parts) * shrink(first_row(scal_ref))
    wide_ref[...] = w
    w_ref[...] = w.astype(jnp.bfloat16)


def third_sums_kernel(*refs):
    parts, refs = refs[:-8], refs[-8:]
    psi_ref, first_ref, v_ref, w_ref, scal_ref, r_ref, z_ref, rows_ref = refs
    scal = first_row(scal_ref)
    beta, start_inverse, gain = (lane_of(scal, lane) for lane in range(1, 4))
    scale = shrink(scal)
    v, w = wide_float(v_ref), w_ref[...]
    vv, vw = total(v * v), total(v * w)
    local = vw / jnp.maximum(vv, SMALLEST)
    r = w - local * v - (scale * beta * start_inverse) * wide_float(psi_ref)
    z = sum_parts(parts) - (local / scale) * w - (scale * beta * gain) * wide_float(first_ref)
    r_ref[...] = r
    z_ref[...] = z
    sums = [total(r * r), total(r * v), total(r * z), total(r * w)]
    sums += [total(z * v), total(z * w), total(z * z), total(w * w)]
    rows_ref[...] = pack([vv, vw, local] + sums, rows_ref.shape)


def final_kernel(entries, rows_ref, r_ref, z_ref, w_ref, v_ref, scal_ref, basis_ref, coef_ref):
    share = basis_ref.shape[2]
    mine = pl.ds(pl.multiple_of(lax.axis_index("mpo") * share, share), share)
    vv, vw, local, rr, rv, rz, rw, zv, zw, zz, ww = (lane_of(rows_ref[...], i) for i in range(11))
    scal = first_row(scal_ref)
    scale = shrink(scal)
    inverse_scale = 1.0 / scale
    alpha_scaled = column_sum(vw) / entries
    off = local - alpha_scaled
    lift = off * inverse_scale
    square = column_sum(rr + off * (2.0 * rv + off * vv)) / entries
    beta_scaled = jnp.sqrt(jnp.maximum(square, 0.0) + scale * scale * EPSILON)
    inverse = 1.0 / beta_scaled
    mixed = column_sum(rz + lift * rw + off * (zv + lift * vw)) / entries
    alpha_3 = mixed * inverse * inverse
    r_v = column_sum(rv + off * vv) / entries
    z_v = column_sum(zv + lift * vw) / entries
    z_z = column_sum(zz + lift * (2.0 * zw + lift * ww)) / entries
    v_v = column_sum(vv) / entries
    beta_2 = beta_scaled * inverse_scale
    third = (z_z - 2.0 * alpha_3 * mixed + alpha_3 * alpha_3 * square) * inverse * inverse
    third += beta_2 * (beta_2 * v_v - 2.0 * inverse * (z_v - alpha_3 * r_v))
    beta_3 = jnp.sqrt(jnp.maximum(third, 0.0) + EPSILON)

    sector = here()
    row_of = lax.broadcasted_iota(jnp.int32, off.shape, 0)
    off_here = column_sum(jnp.where(row_of == sector, off, 0.0))
    v = v_ref[mine, :]
    v_wide = v.astype(jnp.float32)
    v_3 = (r_ref[mine, :] + off_here * v_wide) * inverse
    image = (z_ref[mine, :] + (off_here * inverse_scale) * w_ref[mine, :]) * inverse
    basis_ref[0, 0] = v
    basis_ref[1, 0] = v_3.astype(jnp.bfloat16)
    residual = image - alpha_3 * v_3 - beta_2 * v_wide
    basis_ref[2, 0] = (residual * (1.0 / beta_3)).astype(jnp.bfloat16)

    row = lax.broadcasted_iota(jnp.int32, coef_ref.shape, 0)
    column = lax.broadcasted_iota(jnp.int32, coef_ref.shape, 1)
    out = jnp.zeros(coef_ref.shape, jnp.float32)
    pairs = [(lane_of(scal, 0), lane_of(scal, 1)), (alpha_scaled * inverse_scale, beta_2), (alpha_3, beta_3)]
    for step, (a, b) in enumerate(pairs):
        out = jnp.where(column == step, jnp.where(row == 0, a, b), out)
    coef_ref[...] = out


def shards(wavefunction, env_left, env_right, channel_class):
    width = wavefunction.shape[1]
    ring = ("blk", "rep")
    parts = lax.axis_size("mpo")
    blocks = lax.axis_size("blk") * lax.axis_size("rep")
    entries = blocks * width * width
    permutes, place = routes(blocks)
    slots = 1 + len(permutes)
    channels = channel_class.shape[0]
    psi, left, right = wavefunction[0], env_left[:, 0], env_right[:, 0]
    rows_shape = jax.ShapeDtypeStruct((blocks, 128), jnp.float32)
    scalars = jax.ShapeDtypeStruct((8, 128), jnp.float32)
    wide = jax.ShapeDtypeStruct((width, width), jnp.float32)
    narrow = jax.ShapeDtypeStruct((width, width), jnp.bfloat16)
    lists = [pltpu.SMEM((channels + WIDE,), jnp.int32)] * 2

    def call(kernel, name, outs, args, scratch=(), share=0, limit=4):
        flops = int(4 * channels * share * width**3)
        cost = pl.CostEstimate(flops=flops, bytes_accessed=4 * width * width, transcendentals=0)
        listed = outs if isinstance(outs, tuple) else (outs,)
        first = SMEM if share else VMEM
        return pl.pallas_call(
            kernel,
            out_shape=outs,
            in_specs=[first] + [VMEM] * (len(args) - 1),
            out_specs=tuple(VMEM for _ in listed) if isinstance(outs, tuple) else VMEM,
            scratch_shapes=list(scratch),
            compiler_params=pltpu.CompilerParams(vmem_limit_bytes=limit * MIB),
            cost_estimate=cost,
            name=name,
        )(*args)

    def sources(count):
        return pltpu.VMEM((count + 1, width, width), jnp.bfloat16)

    def own(scaled, block):
        return call(
            functools.partial(own_kernel, scaled, place, blocks),
            "own",
            wide,
            (channel_class, left, right, block),
            [sources(1)] + lists,
            0.2,
            16,
        )

    def rest(scaled, mine, held):
        return call(
            functools.partial(rest_kernel, scaled, slots, place, blocks),
            "rest",
            (narrow, scalars) if scaled else narrow,
            (channel_class, left, right, mine, *held),
            [pltpu.VMEM((width, width), jnp.float32), sources(slots)] + lists,
            0.4,
            16,
        )

    def spread(block):
        return [block] + [lax.ppermute(block, ring, pairs) for pairs in permutes]

    def gather_parts(t):
        if parts == 2:
            return [t, lax.ppermute(t, "mpo", [(0, 1), (1, 0)])]
        held = lax.all_gather(t, "mpo")
        return [held[i] for i in range(parts)]

    def exchange(rows):
        return lax.all_to_all(rows, ring, 0, 0, tiled=True)

    psis = spread(psi)
    t, unit = rest(True, own(True, psi), psis)
    w_1, rows = call(first_sums_kernel, "sums", (narrow, rows_shape), (*gather_parts(t), psi, unit))
    products = spread(w_1)
    t, v_2, scal = call(
        functools.partial(second_kernel, slots, place, blocks, entries),
        "second",
        (narrow, narrow, scalars),
        (channel_class, left, right, exchange(rows), *products, *psis),
        [pltpu.VMEM((width, width), jnp.float32), sources(slots)] + lists,
        0.6,
        16,
    )
    w_wide, w_2 = call(second_sums_kernel, "sums", (wide, narrow), (*gather_parts(t), scal))
    t = rest(False, own(False, w_2), spread(w_2))
    r, z, rows = call(
        third_sums_kernel,
        "sums",
        (wide, wide, rows_shape),
        (*gather_parts(t), psi, w_1, v_2, w_wide, scal),
        limit=8,
    )
    return call(
        functools.partial(final_kernel, entries),
        "final",
        (
            jax.ShapeDtypeStruct((STEPS, 1, width // parts, width), jnp.bfloat16),
            jax.ShapeDtypeStruct((2, STEPS), jnp.float32),
        ),
        (exchange(rows), r, z, w_wide, v_2, scal),
    )


def solution(mesh):
    return jax.shard_map(
        shards,
        mesh=mesh,
        in_specs=(
            P(("groups", "blk", "rep"), None, None),
            P("mpo", ("groups", "blk", "rep"), None, None),
            P("mpo", ("groups", "blk", "rep"), None, None),
            P("mpo"),
        ),
        out_specs=(P(None, ("groups", "blk", "rep"), "mpo", None), P("groups", None)),
        check_vma=False,
    )
```

```python
import functools

import jax
import jax.numpy as jnp
from jax import lax
from jax.experimental import pallas as pl
from jax.experimental.pallas import tpu as pltpu
from jax.sharding import PartitionSpec as P

NS = 4
STEPS = 3
OFFSETS = (0, NS + 1, NS - 1, -(NS + 1), -(NS - 1))
EPSILON = 1e-06
PAD = 4
SMALLEST = 1e-30
MIB = 1024 * 1024
VMEM = pl.BlockSpec(memory_space=pltpu.VMEM)
SMEM = pl.BlockSpec(memory_space=pltpu.SMEM)


def reaches(kind, sector, blocks):
    source = sector - OFFSETS[kind]
    spin = sector % NS
    inside = (source >= 0) & (source < blocks)
    if kind in (1, 4):
        return inside & (spin >= 1)
    if kind in (2, 3):
        return inside & (spin <= NS - 2)
    return inside


def routes(blocks):
    lists = {}
    for kind in range(1, 5):
        lists[kind] = [
            (k - OFFSETS[kind], k) for k in range(blocks) if bool(reaches(kind, k, blocks))
        ]
    permutes, place = [], {}
    for up, down in ((1, 3), (2, 4)):
        both = lists[up] + lists[down]
        disjoint = len({a for a, _ in both}) == len(both) == len({b for _, b in both})
        groups = ((up, down),) if disjoint else ((up,), (down,))
        for group in groups:
            for kind in group:
                place[kind] = len(permutes)
            permutes.append([pair for kind in group for pair in lists[kind]])
    return permutes, place


def here():
    return lax.axis_index("blk") * lax.axis_size("rep") + lax.axis_index("rep")


def lane_of(rows, lane):
    return rows[:, lane : lane + 1]


def pack(values, shape):
    lanes = lax.broadcasted_iota(jnp.int32, shape, 1)
    out = jnp.zeros(shape, jnp.float32)
    for place, value in enumerate(values):
        out = jnp.where(lanes == place, value, out)
    return out


def total(x):
    return jnp.sum(jnp.sum(x, axis=0, keepdims=True), axis=1, keepdims=True)


def column_sum(x):
    return jnp.sum(x, axis=0, keepdims=True)


def peak(x):
    return jnp.max(jnp.max(jnp.abs(x), axis=0, keepdims=True), axis=1, keepdims=True)


def wide_float(ref):
    return ref[...].astype(jnp.float32)


def sum_parts(parts):
    w = wide_float(parts[0])
    for part in parts[1:]:
        w += wide_float(part)
    return w


def first_row(ref):
    return ref[0:1, :]


def list_channels(which, place, blocks, kinds_ref, order, slot_of, idle):
    sector = here()
    reached = [jnp.int32(0 if which == "rest" else 1)]
    for c in range(1, 5):
        reach = reaches(c, sector, blocks).astype(jnp.int32)
        reached.append(reach if which != "own" else jnp.int32(0))
    count = jnp.int32(0)
    for b in range(kinds_ref.shape[0]):
        kind = kinds_ref[b]
        live, slot = reached[0], jnp.int32(0)
        for c in range(1, 5):
            live = jnp.where(kind == c, reached[c], live)
            slot = jnp.where(kind == c, 1 + place[c], slot)
        order[count] = jnp.int32(b)
        slot_of[count] = slot
        count += live
    for extra in range(PAD):
        order[count + extra] = jnp.int32(0)
        slot_of[count + extra] = jnp.int32(idle)
    return count


def multiply_listed(count, left_ref, right_ref, source, order, slot_of, store):
    channels = left_ref.shape[0]
    sizes = [*range(4, min(channels, 20), 2), *range(20, channels, PAD), channels]
    for low, size in zip([-1] + sizes[:-1], sizes):

        @pl.when((count > low) & (count <= size))
        def _():
            held = [order[at] for at in range(size)]
            pieces = [
                jnp.dot(left_ref[b], source[slot_of[at]], preferred_element_type=jnp.float32).astype(
                    jnp.bfloat16
                )
                for at, b in enumerate(held)
            ]
            store(
                lax.dot_general(
                    jnp.concatenate(pieces, axis=1),
                    jnp.concatenate([right_ref[b] for b in held], axis=1),
                    (((1,), (1,)), ((), ())),
                    preferred_element_type=jnp.float32,
                )
            )


def own_kernel(scaled, place, blocks, kinds_ref, left_ref, right_ref, block_ref, own_ref, source, order, slot_of):
    count = list_channels("own", place, blocks, kinds_ref, order, slot_of, 1)
    if scaled:
        block = wide_float(block_ref)
        inverse = 1.0 / jnp.maximum(peak(block), SMALLEST)
        source[0] = (block * inverse).astype(jnp.bfloat16)
    else:
        source[0] = block_ref[...]
    source[1] = jnp.zeros(source.shape[1:], jnp.bfloat16)

    def store(result):
        own_ref[...] = result

    multiply_listed(count, left_ref, right_ref, source, order, slot_of, store)


def rest_kernel(scaled, slots, place, blocks, *refs):
    kinds_ref, left_ref, right_ref, own_ref = refs[:4]
    held, refs = refs[4 : 4 + slots], refs[4 + slots :]
    if scaled:
        t_ref, unit_ref, source, order, slot_of = refs
    else:
        t_ref, source, order, slot_of = refs
    count = list_channels("rest", place, blocks, kinds_ref, order, slot_of, slots)
    if scaled:
        peaks = [jnp.maximum(peak(wide_float(block)), SMALLEST) for block in held]
        unit = functools.reduce(jnp.maximum, peaks)
        unit_ref[...] = jnp.broadcast_to(unit, unit_ref.shape)
        inverse = 1.0 / unit
        ratio = peaks[0] * inverse
        for slot in range(1, slots):
            source[slot] = (wide_float(held[slot]) * inverse).astype(jnp.bfloat16)
    else:
        for slot in range(1, slots):
            source[slot] = held[slot][...]
    source[slots] = jnp.zeros(source.shape[1:], jnp.bfloat16)

    def store(result):
        mine = own_ref[...] * ratio if scaled else own_ref[...]
        t_ref[...] = (mine + result).astype(jnp.bfloat16)

    multiply_listed(count, left_ref, right_ref, source, order, slot_of, store)


def second_kernel(slots, place, blocks, entries, *refs):
    kinds_ref, left_ref, right_ref, rows_ref = refs[:4]
    products, psis = refs[4 : 4 + slots], refs[4 + slots : 4 + 2 * slots]
    t_ref, v_ref, scal_ref, source, order, slot_of = refs[4 + 2 * slots :]
    count = list_channels("all", place, blocks, kinds_ref, order, slot_of, slots)
    rows = rows_ref[...]
    a, d, local, p, q, unit = (lane_of(rows, lane) for lane in range(6))
    beta_0 = jnp.sqrt(column_sum(unit * unit * d) / entries + EPSILON)
    start_inverse = 1.0 / beta_0
    gain = unit * start_inverse
    alpha = column_sum(gain * (gain * a)) / entries
    off = local - alpha
    square = column_sum(gain * (gain * (q + off * (2.0 * p + off * d))))
    beta = jnp.sqrt(jnp.maximum(square, 0.0) / entries + EPSILON)
    inverse = 1.0 / beta
    sector = here()
    row_of = lax.broadcasted_iota(jnp.int32, gain.shape, 0)
    for slot in range(slots):
        origin = sector
        for kind in range(1, 5):
            if 1 + place[kind] == slot:
                origin = jnp.where(reaches(kind, sector, blocks), sector - OFFSETS[kind], origin)
        gain_here = column_sum(jnp.where(row_of == origin, gain, 0.0))
        r = gain_here * wide_float(products[slot]) - (alpha * start_inverse) * wide_float(psis[slot])
        source[slot] = (r * inverse).astype(jnp.bfloat16)
        if slot == 0:
            scal_ref[...] = pack([alpha, beta, start_inverse, gain_here], scal_ref.shape)
            v_ref[...] = source[0]
    source[slots] = jnp.zeros(source.shape[1:], jnp.bfloat16)

    def store(result):
        t_ref[...] = result.astype(jnp.bfloat16)

    multiply_listed(count, left_ref, right_ref, source, order, slot_of, store)


def first_sums_kernel(*refs):
    parts, (psi_ref, unit_ref, w_ref, rows_ref) = refs[:-4], refs[-4:]
    w = sum_parts(parts)
    w_ref[...] = w.astype(jnp.bfloat16)
    unit = lane_of(first_row(unit_ref), 0)
    v = wide_float(psi_ref) * (1.0 / unit)
    a = total(v * w)
    d = total(v * v)
    local = a / jnp.maximum(d, SMALLEST)
    r = w - local * v
    rows_ref[...] = pack([a, d, local, total(r * v), total(r * r), unit], rows_ref.shape)


def shrink(scal):
    return 1.0 / (jnp.abs(lane_of(scal, 0)) + lane_of(scal, 1))


def second_sums_kernel(*refs):
    parts, (scal_ref, wide_ref, w_ref) = refs[:-3], refs[-3:]
    w = sum_parts(parts) * shrink(first_row(scal_ref))
    wide_ref[...] = w
    w_ref[...] = w.astype(jnp.bfloat16)


def third_sums_kernel(*refs):
    parts, refs = refs[:-8], refs[-8:]
    psi_ref, first_ref, v_ref, w_ref, scal_ref, r_ref, z_ref, rows_ref = refs
    scal = first_row(scal_ref)
    beta, start_inverse, gain = (lane_of(scal, lane) for lane in range(1, 4))
    scale = shrink(scal)
    v, w = wide_float(v_ref), w_ref[...]
    vv, vw = total(v * v), total(v * w)
    local = vw / jnp.maximum(vv, SMALLEST)
    r = w - local * v - (scale * beta * start_inverse) * wide_float(psi_ref)
    z = sum_parts(parts) - (local / scale) * w - (scale * beta * gain) * wide_float(first_ref)
    r_ref[...] = r
    z_ref[...] = z
    sums = [total(r * r), total(r * v), total(r * z), total(r * w)]
    sums += [total(z * v), total(z * w), total(z * z), total(w * w)]
    rows_ref[...] = pack([vv, vw, local] + sums, rows_ref.shape)


def final_kernel(entries, rows_ref, r_ref, z_ref, w_ref, v_ref, scal_ref, basis_ref, coef_ref):
    share = basis_ref.shape[2]
    mine = pl.ds(pl.multiple_of(lax.axis_index("mpo") * share, share), share)
    vv, vw, local, rr, rv, rz, rw, zv, zw, zz, ww = (lane_of(rows_ref[...], i) for i in range(11))
    scal = first_row(scal_ref)
    scale = shrink(scal)
    inverse_scale = 1.0 / scale
    alpha_scaled = column_sum(vw) / entries
    off = local - alpha_scaled
    lift = off * inverse_scale
    square = column_sum(rr + off * (2.0 * rv + off * vv)) / entries
    beta_scaled = jnp.sqrt(jnp.maximum(square, 0.0) + scale * scale * EPSILON)
    inverse = 1.0 / beta_scaled
    mixed = column_sum(rz + lift * rw + off * (zv + lift * vw)) / entries
    alpha_3 = mixed * inverse * inverse
    r_v = column_sum(rv + off * vv) / entries
    z_v = column_sum(zv + lift * vw) / entries
    z_z = column_sum(zz + lift * (2.0 * zw + lift * ww)) / entries
    v_v = column_sum(vv) / entries
    beta_2 = beta_scaled * inverse_scale
    third = (z_z - 2.0 * alpha_3 * mixed + alpha_3 * alpha_3 * square) * inverse * inverse
    third += beta_2 * (beta_2 * v_v - 2.0 * inverse * (z_v - alpha_3 * r_v))
    beta_3 = jnp.sqrt(jnp.maximum(third, 0.0) + EPSILON)

    sector = here()
    row_of = lax.broadcasted_iota(jnp.int32, off.shape, 0)
    off_here = column_sum(jnp.where(row_of == sector, off, 0.0))
    v = v_ref[mine, :]
    v_wide = v.astype(jnp.float32)
    v_3 = (r_ref[mine, :] + off_here * v_wide) * inverse
    image = (z_ref[mine, :] + (off_here * inverse_scale) * w_ref[mine, :]) * inverse
    basis_ref[0, 0] = v
    basis_ref[1, 0] = v_3.astype(jnp.bfloat16)
    residual = image - alpha_3 * v_3 - beta_2 * v_wide
    basis_ref[2, 0] = (residual * (1.0 / beta_3)).astype(jnp.bfloat16)

    row = lax.broadcasted_iota(jnp.int32, coef_ref.shape, 0)
    column = lax.broadcasted_iota(jnp.int32, coef_ref.shape, 1)
    out = jnp.zeros(coef_ref.shape, jnp.float32)
    pairs = [(lane_of(scal, 0), lane_of(scal, 1)), (alpha_scaled * inverse_scale, beta_2), (alpha_3, beta_3)]
    for step, (a, b) in enumerate(pairs):
        out = jnp.where(column == step, jnp.where(row == 0, a, b), out)
    coef_ref[...] = out


def shards(wavefunction, env_left, env_right, channel_class):
    width = wavefunction.shape[1]
    ring = ("blk", "rep")
    parts = lax.axis_size("mpo")
    blocks = lax.axis_size("blk") * lax.axis_size("rep")
    entries = blocks * width * width
    permutes, place = routes(blocks)
    slots = 1 + len(permutes)
    channels = channel_class.shape[0]
    psi, left, right = wavefunction[0], env_left[:, 0], env_right[:, 0]
    rows_shape = jax.ShapeDtypeStruct((blocks, 128), jnp.float32)
    scalars = jax.ShapeDtypeStruct((8, 128), jnp.float32)
    wide = jax.ShapeDtypeStruct((width, width), jnp.float32)
    narrow = jax.ShapeDtypeStruct((width, width), jnp.bfloat16)
    lists = [pltpu.SMEM((channels + PAD,), jnp.int32)] * 2

    def call(kernel, name, outs, args, scratch=(), share=0, limit=4):
        flops = int(4 * channels * share * width**3)
        cost = pl.CostEstimate(flops=flops, bytes_accessed=4 * width * width, transcendentals=0)
        listed = outs if isinstance(outs, tuple) else (outs,)
        first = SMEM if share else VMEM
        return pl.pallas_call(
            kernel,
            out_shape=outs,
            in_specs=[first] + [VMEM] * (len(args) - 1),
            out_specs=tuple(VMEM for _ in listed) if isinstance(outs, tuple) else VMEM,
            scratch_shapes=list(scratch),
            compiler_params=pltpu.CompilerParams(vmem_limit_bytes=limit * MIB),
            cost_estimate=cost,
            name=name,
        )(*args)

    def sources(count):
        return pltpu.VMEM((count + 1, width, width), jnp.bfloat16)

    def own(scaled, block):
        return call(
            functools.partial(own_kernel, scaled, place, blocks),
            "own",
            wide,
            (channel_class, left, right, block),
            [sources(1)] + lists,
            0.2,
            16,
        )

    def rest(scaled, mine, held):
        return call(
            functools.partial(rest_kernel, scaled, slots, place, blocks),
            "rest",
            (narrow, scalars) if scaled else narrow,
            (channel_class, left, right, mine, *held),
            [sources(slots)] + lists,
            0.4,
            16,
        )

    def spread(block):
        return [block] + [lax.ppermute(block, ring, pairs) for pairs in permutes]

    def gather_parts(t):
        if parts == 2:
            return [t, lax.ppermute(t, "mpo", [(0, 1), (1, 0)])]
        held = lax.all_gather(t, "mpo")
        return [held[i] for i in range(parts)]

    def exchange(rows):
        return lax.all_to_all(rows, ring, 0, 0, tiled=True)

    psis = spread(psi)
    t, unit = rest(True, own(True, psi), psis)
    w_1, rows = call(first_sums_kernel, "sums", (narrow, rows_shape), (*gather_parts(t), psi, unit))
    products = spread(w_1)
    t, v_2, scal = call(
        functools.partial(second_kernel, slots, place, blocks, entries),
        "second",
        (narrow, narrow, scalars),
        (channel_class, left, right, exchange(rows), *products, *psis),
        [sources(slots)] + lists,
        0.6,
        16,
    )
    w_wide, w_2 = call(second_sums_kernel, "sums", (wide, narrow), (*gather_parts(t), scal))
    t = rest(False, own(False, w_2), spread(w_2))
    r, z, rows = call(
        third_sums_kernel,
        "sums",
        (wide, wide, rows_shape),
        (*gather_parts(t), psi, w_1, v_2, w_wide, scal),
        limit=8,
    )
    return call(
        functools.partial(final_kernel, entries),
        "final",
        (
            jax.ShapeDtypeStruct((STEPS, 1, width // parts, width), jnp.bfloat16),
            jax.ShapeDtypeStruct((2, STEPS), jnp.float32),
        ),
        (exchange(rows), r, z, w_wide, v_2, scal),
    )


def solution(mesh):
    return jax.shard_map(
        shards,
        mesh=mesh,
        in_specs=(
            P(("groups", "blk", "rep"), None, None),
            P("mpo", ("groups", "blk", "rep"), None, None),
            P("mpo", ("groups", "blk", "rep"), None, None),
            P("mpo"),
        ),
        out_specs=(P(None, ("groups", "blk", "rep"), "mpo", None), P("groups", None)),
        check_vma=False,
    )
```

```python
import functools

import jax
import jax.numpy as jnp
from jax import lax
from jax.experimental import pallas as pl
from jax.experimental.pallas import tpu as pltpu
from jax.sharding import PartitionSpec as P

NS = 4
STEPS = 3
OFFSETS = (0, NS + 1, NS - 1, -(NS + 1), -(NS - 1))
EPSILON = 1e-06
WIDE = 8
SMALLEST = 1e-30
MIB = 1024 * 1024
VMEM = pl.BlockSpec(memory_space=pltpu.VMEM)
SMEM = pl.BlockSpec(memory_space=pltpu.SMEM)


def reaches(kind, sector, blocks):
    source = sector - OFFSETS[kind]
    spin = sector % NS
    inside = (source >= 0) & (source < blocks)
    if kind in (1, 4):
        return inside & (spin >= 1)
    if kind in (2, 3):
        return inside & (spin <= NS - 2)
    return inside


def routes(blocks):
    lists = {}
    for kind in range(1, 5):
        lists[kind] = [
            (k - OFFSETS[kind], k) for k in range(blocks) if bool(reaches(kind, k, blocks))
        ]
    permutes, place = [], {}
    for up, down in ((1, 3), (2, 4)):
        both = lists[up] + lists[down]
        disjoint = len({a for a, _ in both}) == len(both) == len({b for _, b in both})
        groups = ((up, down),) if disjoint else ((up,), (down,))
        for group in groups:
            for kind in group:
                place[kind] = len(permutes)
            permutes.append([pair for kind in group for pair in lists[kind]])
    return permutes, place


def here():
    return lax.axis_index("blk") * lax.axis_size("rep") + lax.axis_index("rep")


def lane_of(rows, lane):
    return rows[:, lane : lane + 1]


def pack(values, shape):
    lanes = lax.broadcasted_iota(jnp.int32, shape, 1)
    out = jnp.zeros(shape, jnp.float32)
    for place, value in enumerate(values):
        out = jnp.where(lanes == place, value, out)
    return out


def total(x):
    return jnp.sum(jnp.sum(x, axis=0, keepdims=True), axis=1, keepdims=True)


def column_sum(x):
    return jnp.sum(x, axis=0, keepdims=True)


def peak(x):
    return jnp.max(jnp.max(jnp.abs(x), axis=0, keepdims=True), axis=1, keepdims=True)


def wide_float(ref):
    return ref[...].astype(jnp.float32)


def sum_parts(parts):
    w = wide_float(parts[0])
    for part in parts[1:]:
        w += wide_float(part)
    return w


def first_row(ref):
    return ref[0:1, :]


def list_channels(which, place, blocks, kinds_ref, order, slot_of, idle):
    sector = here()
    use_own = 0 if which == "rest" else 1
    reached = [jnp.int32(use_own)]
    for c in range(1, 5):
        reach = reaches(c, sector, blocks).astype(jnp.int32)
        reached.append(reach if which != "own" else jnp.int32(0))

    count = jnp.int32(0)
    for b in range(kinds_ref.shape[0]):
        kind = kinds_ref[b]
        live, slot = reached[0], jnp.int32(0)
        for c in range(1, 5):
            live = jnp.where(kind == c, reached[c], live)
            slot = jnp.where(kind == c, 1 + place[c], slot)
        order[count] = jnp.int32(b)
        slot_of[count] = slot
        count += live
    for extra in range(WIDE):
        order[count + extra] = jnp.int32(0)
        slot_of[count + extra] = jnp.int32(idle)
    return count


def multiply_listed(count, left_ref, right_ref, source, acc, order, slot_of):
    def multiply(start, wide):
        held = [order[start + inner] for inner in range(wide)]
        pieces = [
            jnp.dot(
                left_ref[b], source[slot_of[start + inner]], preferred_element_type=jnp.float32
            ).astype(jnp.bfloat16)
            for inner, b in enumerate(held)
        ]
        acc[...] += lax.dot_general(
            jnp.concatenate(pieces, axis=1),
            jnp.concatenate([right_ref[b] for b in held], axis=1),
            (((1,), (1,)), ((), ())),
            preferred_element_type=jnp.float32,
        )

    def full(group, carry):
        multiply(group * WIDE, WIDE)
        return carry

    groups = (count + WIDE // 2 - 1) // WIDE
    lax.fori_loop(0, groups, full, 0)
    rest = count - groups * WIDE
    for low, wide in ((0, 2), (2, 4)):

        @pl.when((rest > low) & (rest <= wide))
        def _():
            multiply(groups * WIDE, wide)


def own_kernel(scaled, place, blocks, kinds_ref, left_ref, right_ref, block_ref, acc, source, order, slot_of):
    count = list_channels("own", place, blocks, kinds_ref, order, slot_of, 1)
    if scaled:
        block = wide_float(block_ref)
        inverse = 1.0 / jnp.maximum(peak(block), SMALLEST)
        source[0] = (block * inverse).astype(jnp.bfloat16)
    else:
        source[0] = block_ref[...]
    source[1] = jnp.zeros(source.shape[1:], jnp.bfloat16)
    acc[...] = jnp.zeros_like(acc)
    multiply_listed(count, left_ref, right_ref, source, acc, order, slot_of)


def rest_kernel(scaled, slots, place, blocks, *refs):
    kinds_ref, left_ref, right_ref, own_ref = refs[:4]
    held, refs = refs[4 : 4 + slots], refs[4 + slots :]
    if scaled:
        t_ref, unit_ref, acc, source, order, slot_of = refs
    else:
        t_ref, acc, source, order, slot_of = refs
    count = list_channels("rest", place, blocks, kinds_ref, order, slot_of, slots)
    if scaled:
        peaks = [jnp.maximum(peak(wide_float(block)), SMALLEST) for block in held]
        unit = functools.reduce(jnp.maximum, peaks)
        unit_ref[...] = jnp.broadcast_to(unit, unit_ref.shape)
        inverse = 1.0 / unit
        for slot in range(1, slots):
            source[slot] = (wide_float(held[slot]) * inverse).astype(jnp.bfloat16)
        acc[...] = own_ref[...] * (peaks[0] * inverse)
    else:
        for slot in range(1, slots):
            source[slot] = held[slot][...]
        acc[...] = own_ref[...]
    source[slots] = jnp.zeros(source.shape[1:], jnp.bfloat16)
    multiply_listed(count, left_ref, right_ref, source, acc, order, slot_of)
    t_ref[...] = acc[...].astype(jnp.bfloat16)


def second_kernel(slots, place, blocks, entries, *refs):
    kinds_ref, left_ref, right_ref, rows_ref = refs[:4]
    products, psis = refs[4 : 4 + slots], refs[4 + slots : 4 + 2 * slots]
    t_ref, v_ref, scal_ref, acc, source, order, slot_of = refs[4 + 2 * slots :]
    count = list_channels("all", place, blocks, kinds_ref, order, slot_of, slots)
    rows = rows_ref[...]
    a, d, local, p, q, unit = (lane_of(rows, lane) for lane in range(6))
    beta_0 = jnp.sqrt(column_sum(unit * unit * d) / entries + EPSILON)
    start_inverse = 1.0 / beta_0
    gain = unit * start_inverse
    alpha = column_sum(gain * (gain * a)) / entries
    off = local - alpha
    square = column_sum(gain * (gain * (q + off * (2.0 * p + off * d))))
    beta = jnp.sqrt(jnp.maximum(square, 0.0) / entries + EPSILON)
    inverse = 1.0 / beta
    sector = here()
    row_of = lax.broadcasted_iota(jnp.int32, gain.shape, 0)
    for slot in range(slots):
        origin = sector
        for kind in range(1, 5):
            if 1 + place[kind] == slot:
                origin = jnp.where(reaches(kind, sector, blocks), sector - OFFSETS[kind], origin)
        gain_here = column_sum(jnp.where(row_of == origin, gain, 0.0))
        r = gain_here * wide_float(products[slot]) - (alpha * start_inverse) * wide_float(psis[slot])
        source[slot] = (r * inverse).astype(jnp.bfloat16)
        if slot == 0:
            scal_ref[...] = pack([alpha, beta, start_inverse, gain_here], scal_ref.shape)
            v_ref[...] = source[0]
    source[slots] = jnp.zeros(source.shape[1:], jnp.bfloat16)
    acc[...] = jnp.zeros_like(acc)
    multiply_listed(count, left_ref, right_ref, source, acc, order, slot_of)
    t_ref[...] = acc[...].astype(jnp.bfloat16)


def first_sums_kernel(*refs):
    parts, (psi_ref, unit_ref, w_ref, rows_ref) = refs[:-4], refs[-4:]
    w = sum_parts(parts)
    w_ref[...] = w.astype(jnp.bfloat16)
    unit = lane_of(first_row(unit_ref), 0)
    v = wide_float(psi_ref) * (1.0 / unit)
    a = total(v * w)
    d = total(v * v)
    local = a / jnp.maximum(d, SMALLEST)
    r = w - local * v
    rows_ref[...] = pack([a, d, local, total(r * v), total(r * r), unit], rows_ref.shape)


def shrink(scal):
    return 1.0 / (jnp.abs(lane_of(scal, 0)) + lane_of(scal, 1))


def second_sums_kernel(*refs):
    parts, (scal_ref, wide_ref, w_ref) = refs[:-3], refs[-3:]
    w = sum_parts(parts) * shrink(first_row(scal_ref))
    wide_ref[...] = w
    w_ref[...] = w.astype(jnp.bfloat16)


def third_sums_kernel(*refs):
    parts, refs = refs[:-8], refs[-8:]
    psi_ref, first_ref, v_ref, w_ref, scal_ref, r_ref, z_ref, rows_ref = refs
    scal = first_row(scal_ref)
    beta, start_inverse, gain = (lane_of(scal, lane) for lane in range(1, 4))
    scale = shrink(scal)
    v, w = wide_float(v_ref), w_ref[...]
    vv, vw = total(v * v), total(v * w)
    local = vw / jnp.maximum(vv, SMALLEST)
    r = w - local * v - (scale * beta * start_inverse) * wide_float(psi_ref)
    z = sum_parts(parts) - (local / scale) * w - (scale * beta * gain) * wide_float(first_ref)
    r_ref[...] = r
    z_ref[...] = z
    sums = [total(r * r), total(r * v), total(r * z), total(r * w)]
    sums += [total(z * v), total(z * w), total(z * z), total(w * w)]
    rows_ref[...] = pack([vv, vw, local] + sums, rows_ref.shape)


def final_kernel(entries, rows_ref, r_ref, z_ref, w_ref, v_ref, scal_ref, basis_ref, coef_ref):
    share = basis_ref.shape[2]
    mine = pl.ds(pl.multiple_of(lax.axis_index("mpo") * share, share), share)
    vv, vw, local, rr, rv, rz, rw, zv, zw, zz, ww = (lane_of(rows_ref[...], i) for i in range(11))
    scal = first_row(scal_ref)
    scale = shrink(scal)
    inverse_scale = 1.0 / scale
    alpha_scaled = column_sum(vw) / entries
    off = local - alpha_scaled
    lift = off * inverse_scale
    square = column_sum(rr + off * (2.0 * rv + off * vv)) / entries
    beta_scaled = jnp.sqrt(jnp.maximum(square, 0.0) + scale * scale * EPSILON)
    inverse = 1.0 / beta_scaled
    mixed = column_sum(rz + lift * rw + off * (zv + lift * vw)) / entries
    alpha_3 = mixed * inverse * inverse
    r_v = column_sum(rv + off * vv) / entries
    z_v = column_sum(zv + lift * vw) / entries
    z_z = column_sum(zz + lift * (2.0 * zw + lift * ww)) / entries
    v_v = column_sum(vv) / entries
    beta_2 = beta_scaled * inverse_scale
    third = (z_z - 2.0 * alpha_3 * mixed + alpha_3 * alpha_3 * square) * inverse * inverse
    third += beta_2 * (beta_2 * v_v - 2.0 * inverse * (z_v - alpha_3 * r_v))
    beta_3 = jnp.sqrt(jnp.maximum(third, 0.0) + EPSILON)

    sector = here()
    row_of = lax.broadcasted_iota(jnp.int32, off.shape, 0)
    off_here = column_sum(jnp.where(row_of == sector, off, 0.0))
    v = v_ref[mine, :]
    v_wide = v.astype(jnp.float32)
    v_3 = (r_ref[mine, :] + off_here * v_wide) * inverse
    image = (z_ref[mine, :] + (off_here * inverse_scale) * w_ref[mine, :]) * inverse
    basis_ref[0, 0] = v
    basis_ref[1, 0] = v_3.astype(jnp.bfloat16)
    residual = image - alpha_3 * v_3 - beta_2 * v_wide
    basis_ref[2, 0] = (residual * (1.0 / beta_3)).astype(jnp.bfloat16)

    row = lax.broadcasted_iota(jnp.int32, coef_ref.shape, 0)
    column = lax.broadcasted_iota(jnp.int32, coef_ref.shape, 1)
    out = jnp.zeros(coef_ref.shape, jnp.float32)
    pairs = [(lane_of(scal, 0), lane_of(scal, 1)), (alpha_scaled * inverse_scale, beta_2), (alpha_3, beta_3)]
    for step, (a, b) in enumerate(pairs):
        out = jnp.where(column == step, jnp.where(row == 0, a, b), out)
    coef_ref[...] = out


def shards(wavefunction, env_left, env_right, channel_class):
    width = wavefunction.shape[1]
    ring = ("blk", "rep")
    parts = lax.axis_size("mpo")
    blocks = lax.axis_size("blk") * lax.axis_size("rep")
    entries = blocks * width * width
    permutes, place = routes(blocks)
    slots = 1 + len(permutes)
    channels = channel_class.shape[0]
    psi, left, right = wavefunction[0], env_left[:, 0], env_right[:, 0]
    rows_shape = jax.ShapeDtypeStruct((blocks, 128), jnp.float32)
    scalars = jax.ShapeDtypeStruct((8, 128), jnp.float32)
    wide = jax.ShapeDtypeStruct((width, width), jnp.float32)
    narrow = jax.ShapeDtypeStruct((width, width), jnp.bfloat16)
    lists = [pltpu.SMEM((channels + WIDE,), jnp.int32)] * 2

    def call(kernel, name, outs, args, scratch=(), share=0, limit=4):
        flops = int(4 * channels * share * width**3)
        cost = pl.CostEstimate(flops=flops, bytes_accessed=4 * width * width, transcendentals=0)
        listed = outs if isinstance(outs, tuple) else (outs,)
        first = SMEM if share else VMEM
        return pl.pallas_call(
            kernel,
            out_shape=outs,
            in_specs=[first] + [VMEM] * (len(args) - 1),
            out_specs=tuple(VMEM for _ in listed) if isinstance(outs, tuple) else VMEM,
            scratch_shapes=list(scratch),
            compiler_params=pltpu.CompilerParams(vmem_limit_bytes=limit * MIB),
            cost_estimate=cost,
            name=name,
        )(*args)

    def sources(count):
        return pltpu.VMEM((count + 1, width, width), jnp.bfloat16)

    def own(scaled, block):
        return call(
            functools.partial(own_kernel, scaled, place, blocks),
            "own",
            wide,
            (channel_class, left, right, block),
            [sources(1)] + lists,
            0.2,
            16,
        )

    def rest(scaled, mine, held):
        return call(
            functools.partial(rest_kernel, scaled, slots, place, blocks),
            "rest",
            (narrow, scalars) if scaled else narrow,
            (channel_class, left, right, mine, *held),
            [pltpu.VMEM((width, width), jnp.float32), sources(slots)] + lists,
            0.4,
            16,
        )

    def spread(block):
        return [block] + [lax.ppermute(block, ring, pairs) for pairs in permutes]

    def gather_parts(t):
        if parts == 2:
            return [t, lax.ppermute(t, "mpo", [(0, 1), (1, 0)])]
        held = lax.all_gather(t, "mpo")
        return [held[i] for i in range(parts)]

    def exchange(rows):
        return lax.all_to_all(rows, ring, 0, 0, tiled=True)

    psis = spread(psi)
    t, unit = rest(True, own(True, psi), psis)
    w_1, rows = call(first_sums_kernel, "sums", (narrow, rows_shape), (*gather_parts(t), psi, unit))
    products = spread(w_1)
    t, v_2, scal = call(
        functools.partial(second_kernel, slots, place, blocks, entries),
        "second",
        (narrow, narrow, scalars),
        (channel_class, left, right, exchange(rows), *products, *psis),
        [pltpu.VMEM((width, width), jnp.float32), sources(slots)] + lists,
        0.6,
        16,
    )
    w_wide, w_2 = call(second_sums_kernel, "sums", (wide, narrow), (*gather_parts(t), scal))
    t = rest(False, own(False, w_2), spread(w_2))
    r, z, rows = call(
        third_sums_kernel,
        "sums",
        (wide, wide, rows_shape),
        (*gather_parts(t), psi, w_1, v_2, w_wide, scal),
        limit=8,
    )
    return call(
        functools.partial(final_kernel, entries),
        "final",
        (
            jax.ShapeDtypeStruct((STEPS, 1, width // parts, width), jnp.bfloat16),
            jax.ShapeDtypeStruct((2, STEPS), jnp.float32),
        ),
        (exchange(rows), r, z, w_wide, v_2, scal),
    )


def solution(mesh):
    return jax.shard_map(
        shards,
        mesh=mesh,
        in_specs=(
            P(("groups", "blk", "rep"), None, None),
            P("mpo", ("groups", "blk", "rep"), None, None),
            P("mpo", ("groups", "blk", "rep"), None, None),
            P("mpo"),
        ),
        out_specs=(P(None, ("groups", "blk", "rep"), "mpo", None), P("groups", None)),
        check_vma=False,
    )
```

```python
import functools

import jax
import jax.numpy as jnp
from jax import lax
from jax.experimental import pallas as pl
from jax.experimental.pallas import tpu as pltpu
from jax.sharding import PartitionSpec as P

NS = 4
STEPS = 3
OFFSETS = (0, NS + 1, NS - 1, -(NS + 1), -(NS - 1))
EPSILON = 1e-06
WIDE = 8
SMALLEST = 1e-30
MIB = 1024 * 1024
VMEM = pl.BlockSpec(memory_space=pltpu.VMEM)
SMEM = pl.BlockSpec(memory_space=pltpu.SMEM)


def reaches(kind, sector, blocks):
    source = sector - OFFSETS[kind]
    spin = sector % NS
    inside = (source >= 0) & (source < blocks)
    if kind in (1, 4):
        return inside & (spin >= 1)
    if kind in (2, 3):
        return inside & (spin <= NS - 2)
    return inside


def routes(blocks):
    degree, edges = [0] * blocks, []
    for kind in (1, 2):
        for k in range(blocks):
            if reaches(kind, k, blocks):
                edges.append((k - OFFSETS[kind], k))
                degree[k - OFFSETS[kind]] += 1
                degree[k] += 1
    edges.sort(key=lambda edge: degree[edge[0]] + degree[edge[1]])
    partner = [{} for _ in range(blocks)]

    def lowest(block):
        return next(c for c in range(len(edges)) if c not in partner[block])

    for a, b in edges:
        here_free, there_free = lowest(a), lowest(b)
        if here_free in partner[b]:
            path, block, colour = [b], b, here_free
            while colour in partner[block]:
                block = partner[block][colour]
                path.append(block)
                colour = there_free if colour == here_free else here_free
            for block in path:
                moved = {}
                for old, new in ((here_free, there_free), (there_free, here_free)):
                    if old in partner[block]:
                        moved[new] = partner[block].pop(old)
                partner[block].update(moved)
        partner[a][here_free], partner[b][here_free] = b, a
    colours = sorted({c for held in partner for c in held})
    permutes = [[(held[c], k) for k, held in enumerate(partner) if c in held] for c in colours]
    return sorted(permutes, key=len, reverse=True)


def slot_tables(permutes, blocks):
    origins = [{k: k for k in range(blocks)}] + [{k: s for s, k in pairs} for pairs in permutes]
    places = []
    for kind in range(5):
        place = {}
        for slot, origin in enumerate(origins):
            for k, source in origin.items():
                if source == k - OFFSETS[kind] and reaches(kind, k, blocks):
                    place[k] = slot
        places.append(place)
    return places, origins


def look_up(table, sector, default):
    out = jnp.int32(default)
    for k, value in table.items():
        if value != default:
            out = jnp.where(sector == k, jnp.int32(value), out)
    return out


def here():
    return lax.axis_index("blk") * lax.axis_size("rep") + lax.axis_index("rep")


def lane_of(rows, lane):
    return rows[:, lane : lane + 1]


def pack(values, shape):
    lanes = lax.broadcasted_iota(jnp.int32, shape, 1)
    out = jnp.zeros(shape, jnp.float32)
    for place, value in enumerate(values):
        out = jnp.where(lanes == place, value, out)
    return out


def total(x):
    return jnp.sum(jnp.sum(x, axis=0, keepdims=True), axis=1, keepdims=True)


def column_sum(x):
    return jnp.sum(x, axis=0, keepdims=True)


def peak(x):
    return jnp.max(jnp.max(jnp.abs(x), axis=0, keepdims=True), axis=1, keepdims=True)


def wide_float(ref):
    return ref[...].astype(jnp.float32)


def sum_parts(parts):
    w = wide_float(parts[0])
    for part in parts[1:]:
        w += wide_float(part)
    return w


def first_row(ref):
    return ref[0:1, :]


def list_channels(which, places, kinds_ref, order, slot_of, idle):
    sector = here()
    slots = [jnp.int32(-1 if which == "rest" else 0)]
    slots += [look_up(places[c], sector, -1) if which != "own" else jnp.int32(-1) for c in range(1, 5)]
    count = jnp.int32(0)
    for b in range(kinds_ref.shape[0]):
        kind = kinds_ref[b]
        slot = slots[0]
        for c in range(1, 5):
            slot = jnp.where(kind == c, slots[c], slot)
        order[count] = jnp.int32(b)
        slot_of[count] = slot
        count += jnp.where(slot >= 0, 1, 0)
    for extra in range(WIDE):
        order[count + extra] = jnp.int32(0)
        slot_of[count + extra] = jnp.int32(idle)
    return count


def multiply_listed(count, left_ref, right_ref, source, acc, order, slot_of):
    def multiply(start, wide):
        held = [order[start + inner] for inner in range(wide)]
        pieces = [
            jnp.dot(
                left_ref[b], source[slot_of[start + inner]], preferred_element_type=jnp.float32
            ).astype(jnp.bfloat16)
            for inner, b in enumerate(held)
        ]
        acc[...] += lax.dot_general(
            jnp.concatenate(pieces, axis=1),
            jnp.concatenate([right_ref[b] for b in held], axis=1),
            (((1,), (1,)), ((), ())),
            preferred_element_type=jnp.float32,
        )

    def full(group, carry):
        multiply(group * WIDE, WIDE)
        return carry

    groups = (count + WIDE // 2 - 1) // WIDE
    lax.fori_loop(0, groups, full, 0)
    rest = count - groups * WIDE
    for low, wide in ((0, 2), (2, 4)):

        @pl.when((rest > low) & (rest <= wide))
        def _():
            multiply(groups * WIDE, wide)


def own_kernel(scaled, places, kinds_ref, left_ref, right_ref, block_ref, acc, source, order, slot_of):
    count = list_channels("own", places, kinds_ref, order, slot_of, 1)
    if scaled:
        block = wide_float(block_ref)
        inverse = 1.0 / jnp.maximum(peak(block), SMALLEST)
        source[0] = (block * inverse).astype(jnp.bfloat16)
    else:
        source[0] = block_ref[...]
    source[1] = jnp.zeros(source.shape[1:], jnp.bfloat16)
    acc[...] = jnp.zeros_like(acc)
    multiply_listed(count, left_ref, right_ref, source, acc, order, slot_of)


def scaled_rest_kernel(slots, places, *refs):
    kinds_ref, left_ref, right_ref, own_ref = refs[:4]
    held, (t_ref, unit_ref, acc, source, order, slot_of) = refs[4 : 4 + slots], refs[4 + slots :]
    count = list_channels("rest", places, kinds_ref, order, slot_of, slots)
    peaks = [jnp.maximum(peak(wide_float(block)), SMALLEST) for block in held]
    unit = functools.reduce(jnp.maximum, peaks)
    unit_ref[...] = jnp.broadcast_to(unit, unit_ref.shape)
    inverse = 1.0 / unit
    for slot in range(1, slots):
        source[slot] = (wide_float(held[slot]) * inverse).astype(jnp.bfloat16)
    acc[...] = own_ref[...] * (peaks[0] * inverse)
    source[slots] = jnp.zeros(source.shape[1:], jnp.bfloat16)
    multiply_listed(count, left_ref, right_ref, source, acc, order, slot_of)
    t_ref[...] = acc[...].astype(jnp.bfloat16)


def rest_kernel(slots, places, *refs):
    kinds_ref, left_ref, right_ref, own_ref = refs[:4]
    t_ref, acc, source, order, slot_of = refs[-5:]
    shares, held = refs[4 : -5 - (slots - 2)], refs[-5 - (slots - 2) : -5]
    count = list_channels("rest", places, kinds_ref, order, slot_of, slots)
    share = source.shape[1] // lax.axis_size("mpo")
    for step, block in enumerate(shares):
        if len(shares) == 1:
            source[1] = block[...]
        else:
            at = lax.axis_index("mpo") if step == 0 else 1 - lax.axis_index("mpo")
            source[1, pl.ds(pl.multiple_of(at * share, share), share), :] = block[...]
    for slot in range(2, slots):
        source[slot] = held[slot - 2][...]
    acc[...] = own_ref[...]
    source[slots] = jnp.zeros(source.shape[1:], jnp.bfloat16)
    multiply_listed(count, left_ref, right_ref, source, acc, order, slot_of)
    t_ref[...] = acc[...].astype(jnp.bfloat16)


def second_kernel(slots, places, origins, entries, *refs):
    kinds_ref, left_ref, right_ref, rows_ref = refs[:4]
    products, psis = refs[4 : 4 + slots], refs[4 + slots : 4 + 2 * slots]
    t_ref, v_ref, scal_ref, acc, source, order, slot_of = refs[4 + 2 * slots :]
    count = list_channels("all", places, kinds_ref, order, slot_of, slots)
    rows = rows_ref[...]
    a, d, local, p, q, unit = (lane_of(rows, lane) for lane in range(6))
    beta_0 = jnp.sqrt(column_sum(unit * unit * d) / entries + EPSILON)
    start_inverse = 1.0 / beta_0
    gain = unit * start_inverse
    alpha = column_sum(gain * (gain * a)) / entries
    off = local - alpha
    square = column_sum(gain * (gain * (q + off * (2.0 * p + off * d))))
    beta = jnp.sqrt(jnp.maximum(square, 0.0) / entries + EPSILON)
    inverse = 1.0 / beta
    sector = here()
    row_of = lax.broadcasted_iota(jnp.int32, gain.shape, 0)
    for slot in range(slots):
        origin = sector if slot == 0 else look_up(origins[slot], sector, 0)
        gain_here = column_sum(jnp.where(row_of == origin, gain, 0.0))
        r = gain_here * wide_float(products[slot]) - (alpha * start_inverse) * wide_float(psis[slot])
        source[slot] = (r * inverse).astype(jnp.bfloat16)
        if slot == 0:
            scal_ref[...] = pack([alpha, beta, start_inverse, gain_here], scal_ref.shape)
            v_ref[...] = source[0]
    source[slots] = jnp.zeros(source.shape[1:], jnp.bfloat16)
    acc[...] = jnp.zeros_like(acc)
    multiply_listed(count, left_ref, right_ref, source, acc, order, slot_of)
    t_ref[...] = acc[...].astype(jnp.bfloat16)


def first_sums_kernel(*refs):
    parts, (psi_ref, unit_ref, w_ref, rows_ref) = refs[:-4], refs[-4:]
    w = sum_parts(parts)
    w_ref[...] = w.astype(jnp.bfloat16)
    unit = lane_of(first_row(unit_ref), 0)
    v = wide_float(psi_ref) * (1.0 / unit)
    a = total(v * w)
    d = total(v * v)
    local = a / jnp.maximum(d, SMALLEST)
    r = w - local * v
    rows_ref[...] = pack([a, d, local, total(r * v), total(r * r), unit], rows_ref.shape)


def shrink(scal):
    return 1.0 / (jnp.abs(lane_of(scal, 0)) + lane_of(scal, 1))


def second_sums_kernel(*refs):
    parts, (scal_ref, wide_ref, w_ref, share_ref) = refs[:-4], refs[-4:]
    w = sum_parts(parts) * shrink(first_row(scal_ref))
    wide_ref[...] = w
    w_ref[...] = w.astype(jnp.bfloat16)
    share = share_ref.shape[0]
    mine = pl.ds(pl.multiple_of(lax.axis_index("mpo") * share, share), share)
    share_ref[...] = wide_ref[mine, :].astype(jnp.bfloat16)


def third_sums_kernel(*refs):
    parts, refs = refs[:-8], refs[-8:]
    psi_ref, first_ref, v_ref, w_ref, scal_ref, r_ref, z_ref, rows_ref = refs
    scal = first_row(scal_ref)
    beta, start_inverse, gain = (lane_of(scal, lane) for lane in range(1, 4))
    scale = shrink(scal)
    v, w = wide_float(v_ref), w_ref[...]
    vv, vw = total(v * v), total(v * w)
    local = vw / jnp.maximum(vv, SMALLEST)
    r = w - local * v - (scale * beta * start_inverse) * wide_float(psi_ref)
    z = sum_parts(parts) - (local / scale) * w - (scale * beta * gain) * wide_float(first_ref)
    r_ref[...] = r
    z_ref[...] = z
    sums = [total(r * r), total(r * v), total(r * z), total(r * w)]
    sums += [total(z * v), total(z * w), total(z * z), total(w * w)]
    rows_ref[...] = pack([vv, vw, local] + sums, rows_ref.shape)


def final_kernel(entries, rows_ref, r_ref, z_ref, w_ref, v_ref, scal_ref, basis_ref, coef_ref):
    share = basis_ref.shape[2]
    mine = pl.ds(pl.multiple_of(lax.axis_index("mpo") * share, share), share)
    vv, vw, local, rr, rv, rz, rw, zv, zw, zz, ww = (lane_of(rows_ref[...], i) for i in range(11))
    scal = first_row(scal_ref)
    scale = shrink(scal)
    inverse_scale = 1.0 / scale
    alpha_scaled = column_sum(vw) / entries
    off = local - alpha_scaled
    lift = off * inverse_scale
    square = column_sum(rr + off * (2.0 * rv + off * vv)) / entries
    beta_scaled = jnp.sqrt(jnp.maximum(square, 0.0) + scale * scale * EPSILON)
    inverse = 1.0 / beta_scaled
    mixed = column_sum(rz + lift * rw + off * (zv + lift * vw)) / entries
    alpha_3 = mixed * inverse * inverse
    r_v = column_sum(rv + off * vv) / entries
    z_v = column_sum(zv + lift * vw) / entries
    z_z = column_sum(zz + lift * (2.0 * zw + lift * ww)) / entries
    v_v = column_sum(vv) / entries
    beta_2 = beta_scaled * inverse_scale
    third = (z_z - 2.0 * alpha_3 * mixed + alpha_3 * alpha_3 * square) * inverse * inverse
    third += beta_2 * (beta_2 * v_v - 2.0 * inverse * (z_v - alpha_3 * r_v))
    beta_3 = jnp.sqrt(jnp.maximum(third, 0.0) + EPSILON)

    sector = here()
    row_of = lax.broadcasted_iota(jnp.int32, off.shape, 0)
    off_here = column_sum(jnp.where(row_of == sector, off, 0.0))
    v = v_ref[mine, :]
    v_wide = v.astype(jnp.float32)
    v_3 = (r_ref[mine, :] + off_here * v_wide) * inverse
    image = (z_ref[mine, :] + (off_here * inverse_scale) * w_ref[mine, :]) * inverse
    basis_ref[0, 0] = v
    basis_ref[1, 0] = v_3.astype(jnp.bfloat16)
    residual = image - alpha_3 * v_3 - beta_2 * v_wide
    basis_ref[2, 0] = (residual * (1.0 / beta_3)).astype(jnp.bfloat16)

    row = lax.broadcasted_iota(jnp.int32, coef_ref.shape, 0)
    column = lax.broadcasted_iota(jnp.int32, coef_ref.shape, 1)
    out = jnp.zeros(coef_ref.shape, jnp.float32)
    pairs = [(lane_of(scal, 0), lane_of(scal, 1)), (alpha_scaled * inverse_scale, beta_2), (alpha_3, beta_3)]
    for step, (a, b) in enumerate(pairs):
        out = jnp.where(column == step, jnp.where(row == 0, a, b), out)
    coef_ref[...] = out


def shards(wavefunction, env_left, env_right, channel_class):
    width = wavefunction.shape[1]
    ring = ("blk", "rep")
    parts = lax.axis_size("mpo")
    blocks = lax.axis_size("blk") * lax.axis_size("rep")
    entries = blocks * width * width
    permutes = routes(blocks)
    places, origins = slot_tables(permutes, blocks)
    slots = 1 + len(permutes)
    channels = channel_class.shape[0]
    psi, left, right = wavefunction[0], env_left[:, 0], env_right[:, 0]
    rows_shape = jax.ShapeDtypeStruct((blocks, 128), jnp.float32)
    scalars = jax.ShapeDtypeStruct((8, 128), jnp.float32)
    wide = jax.ShapeDtypeStruct((width, width), jnp.float32)
    narrow = jax.ShapeDtypeStruct((width, width), jnp.bfloat16)
    lists = [pltpu.SMEM((channels + WIDE,), jnp.int32)] * 2

    def call(kernel, name, outs, args, scratch=(), share=0, limit=4):
        flops = int(4 * channels * share * width**3)
        cost = pl.CostEstimate(flops=flops, bytes_accessed=4 * width * width, transcendentals=0)
        listed = outs if isinstance(outs, tuple) else (outs,)
        first = SMEM if share else VMEM
        return pl.pallas_call(
            kernel,
            out_shape=outs,
            in_specs=[first] + [VMEM] * (len(args) - 1),
            out_specs=tuple(VMEM for _ in listed) if isinstance(outs, tuple) else VMEM,
            scratch_shapes=list(scratch),
            compiler_params=pltpu.CompilerParams(vmem_limit_bytes=limit * MIB),
            cost_estimate=cost,
            name=name,
        )(*args)

    def sources(count):
        return pltpu.VMEM((count + 1, width, width), jnp.bfloat16)

    def own(scaled, block):
        return call(
            functools.partial(own_kernel, scaled, places),
            "own",
            wide,
            (channel_class, left, right, block),
            [sources(1)] + lists,
            0.2,
            16,
        )

    def rest(scaled, mine, *held):
        return call(
            functools.partial(scaled_rest_kernel if scaled else rest_kernel, slots, places),
            "rest",
            (narrow, scalars) if scaled else narrow,
            (channel_class, left, right, mine, *held),
            [pltpu.VMEM((width, width), jnp.float32), sources(slots)] + lists,
            0.4,
            16,
        )

    def shift(block, pairs):
        return lax.ppermute(block, ring, pairs)

    def spread(block):
        return [block] + [shift(block, pairs) for pairs in permutes]

    def spread_shared(block, share):
        piece = shift(share, permutes[0])
        if parts == 2:
            first = [piece, lax.ppermute(piece, "mpo", [(0, 1), (1, 0)])]
        else:
            first = [lax.all_gather(piece, "mpo", axis=0, tiled=True)]
        return first + [shift(block, pairs) for pairs in permutes[1:]]

    def gather_parts(t):
        if parts == 2:
            return [t, lax.ppermute(t, "mpo", [(0, 1), (1, 0)])]
        held = lax.all_gather(t, "mpo")
        return [held[i] for i in range(parts)]

    def exchange(rows):
        return lax.all_to_all(rows, ring, 0, 0, tiled=True)

    psis = spread(psi)
    t, unit = rest(True, own(True, psi), *psis)
    w_1, rows = call(first_sums_kernel, "sums", (narrow, rows_shape), (*gather_parts(t), psi, unit))
    products = spread(w_1)
    t, v_2, scal = call(
        functools.partial(second_kernel, slots, places, origins, entries),
        "second",
        (narrow, narrow, scalars),
        (channel_class, left, right, exchange(rows), *products, *psis),
        [pltpu.VMEM((width, width), jnp.float32), sources(slots)] + lists,
        0.6,
        16,
    )
    share = jax.ShapeDtypeStruct((width // parts, width), jnp.bfloat16)
    w_wide, w_2, share_2 = call(
        second_sums_kernel, "sums", (wide, narrow, share), (*gather_parts(t), scal)
    )
    t = rest(False, own(False, w_2), *spread_shared(w_2, share_2))
    r, z, rows = call(
        third_sums_kernel,
        "sums",
        (wide, wide, rows_shape),
        (*gather_parts(t), psi, w_1, v_2, w_wide, scal),
        limit=8,
    )
    return call(
        functools.partial(final_kernel, entries),
        "final",
        (
            jax.ShapeDtypeStruct((STEPS, 1, width // parts, width), jnp.bfloat16),
            jax.ShapeDtypeStruct((2, STEPS), jnp.float32),
        ),
        (exchange(rows), r, z, w_wide, v_2, scal),
    )


def solution(mesh):
    return jax.shard_map(
        shards,
        mesh=mesh,
        in_specs=(
            P(("groups", "blk", "rep"), None, None),
            P("mpo", ("groups", "blk", "rep"), None, None),
            P("mpo", ("groups", "blk", "rep"), None, None),
            P("mpo"),
        ),
        out_specs=(P(None, ("groups", "blk", "rep"), "mpo", None), P("groups", None)),
        check_vma=False,
    )
```

```python
import functools

import jax
import jax.numpy as jnp
from jax import lax
from jax.experimental import pallas as pl
from jax.experimental.pallas import tpu as pltpu
from jax.sharding import PartitionSpec as P

NS = 4
STEPS = 3
OFFSETS = (0, NS + 1, NS - 1, -(NS + 1), -(NS - 1))
EPSILON = 1e-06
WIDE = 8
SMALLEST = 1e-30
MIB = 1024 * 1024
VMEM = pl.BlockSpec(memory_space=pltpu.VMEM)
SMEM = pl.BlockSpec(memory_space=pltpu.SMEM)


def reaches(kind, sector, blocks):
    source = sector - OFFSETS[kind]
    spin = sector % NS
    inside = (source >= 0) & (source < blocks)
    if kind in (1, 4):
        return inside & (spin >= 1)
    if kind in (2, 3):
        return inside & (spin <= NS - 2)
    return inside


def routes(blocks):
    degree, edges = [0] * blocks, []
    for kind in (1, 2):
        for k in range(blocks):
            if reaches(kind, k, blocks):
                edges.append((k - OFFSETS[kind], k))
                degree[k - OFFSETS[kind]] += 1
                degree[k] += 1
    edges.sort(key=lambda edge: degree[edge[0]] + degree[edge[1]])
    partner = [{} for _ in range(blocks)]

    def lowest(block):
        return next(c for c in range(len(edges)) if c not in partner[block])

    for a, b in edges:
        here_free, there_free = lowest(a), lowest(b)
        if here_free in partner[b]:
            path, block, colour = [b], b, here_free
            while colour in partner[block]:
                block = partner[block][colour]
                path.append(block)
                colour = there_free if colour == here_free else here_free
            for block in path:
                moved = {}
                for old, new in ((here_free, there_free), (there_free, here_free)):
                    if old in partner[block]:
                        moved[new] = partner[block].pop(old)
                partner[block].update(moved)
        partner[a][here_free], partner[b][here_free] = b, a
    colours = sorted({c for held in partner for c in held})
    permutes = [[(held[c], k) for k, held in enumerate(partner) if c in held] for c in colours]
    return sorted(permutes, key=len, reverse=True)


def slot_tables(permutes, blocks):
    origins = [{k: k for k in range(blocks)}] + [{k: s for s, k in pairs} for pairs in permutes]
    places = []
    for kind in range(5):
        place = {}
        for slot, origin in enumerate(origins):
            for k, source in origin.items():
                if source == k - OFFSETS[kind] and reaches(kind, k, blocks):
                    place[k] = slot
        places.append(place)
    return places, origins


def look_up(table, sector, default):
    out = jnp.int32(default)
    for k, value in table.items():
        if value != default:
            out = jnp.where(sector == k, jnp.int32(value), out)
    return out


def here():
    return lax.axis_index("blk") * lax.axis_size("rep") + lax.axis_index("rep")


def lane_of(rows, lane):
    return rows[:, lane : lane + 1]


def pack(values, shape):
    lanes = lax.broadcasted_iota(jnp.int32, shape, 1)
    out = jnp.zeros(shape, jnp.float32)
    for place, value in enumerate(values):
        out = jnp.where(lanes == place, value, out)
    return out


def total(x):
    return jnp.sum(jnp.sum(x, axis=0, keepdims=True), axis=1, keepdims=True)


def column_sum(x):
    return jnp.sum(x, axis=0, keepdims=True)


def peak(x):
    return jnp.max(jnp.max(jnp.abs(x), axis=0, keepdims=True), axis=1, keepdims=True)


def wide_float(ref):
    return ref[...].astype(jnp.float32)


def sum_parts(parts):
    w = wide_float(parts[0])
    for part in parts[1:]:
        w += wide_float(part)
    return w


def first_row(ref):
    return ref[0:1, :]


def list_channels(which, places, kinds_ref, order, slot_of, idle):
    sector = here()
    slots = [jnp.int32(-1 if which == "rest" else 0)]
    slots += [look_up(places[c], sector, -1) if which != "own" else jnp.int32(-1) for c in range(1, 5)]
    count = jnp.int32(0)
    for b in range(kinds_ref.shape[0]):
        kind = kinds_ref[b]
        slot = slots[0]
        for c in range(1, 5):
            slot = jnp.where(kind == c, slots[c], slot)
        order[count] = jnp.int32(b)
        slot_of[count] = slot
        count += jnp.where(slot >= 0, 1, 0)
    for extra in range(WIDE):
        order[count + extra] = jnp.int32(0)
        slot_of[count + extra] = jnp.int32(idle)
    return count


def multiply_listed(count, left_ref, right_ref, source, acc, order, slot_of):
    def multiply(start, wide):
        held = [order[start + inner] for inner in range(wide)]
        pieces = [
            jnp.dot(
                left_ref[b], source[slot_of[start + inner]], preferred_element_type=jnp.float32
            ).astype(jnp.bfloat16)
            for inner, b in enumerate(held)
        ]
        acc[...] += lax.dot_general(
            jnp.concatenate(pieces, axis=1),
            jnp.concatenate([right_ref[b] for b in held], axis=1),
            (((1,), (1,)), ((), ())),
            preferred_element_type=jnp.float32,
        )

    def full(group, carry):
        multiply(group * WIDE, WIDE)
        return carry

    groups = (count + WIDE // 2 - 1) // WIDE
    lax.fori_loop(0, groups, full, 0)
    rest = count - groups * WIDE
    for low, wide in ((0, 2), (2, 4)):

        @pl.when((rest > low) & (rest <= wide))
        def _():
            multiply(groups * WIDE, wide)


def own_kernel(scaled, places, kinds_ref, left_ref, right_ref, block_ref, acc, source, order, slot_of):
    count = list_channels("own", places, kinds_ref, order, slot_of, 1)
    if scaled:
        block = wide_float(block_ref)
        inverse = 1.0 / jnp.maximum(peak(block), SMALLEST)
        source[0] = (block * inverse).astype(jnp.bfloat16)
    else:
        source[0] = block_ref[...]
    source[1] = jnp.zeros(source.shape[1:], jnp.bfloat16)
    acc[...] = jnp.zeros_like(acc)
    multiply_listed(count, left_ref, right_ref, source, acc, order, slot_of)


def rest_kernel(scaled, passes, shares, slots, places, *refs):
    kinds_ref, left_ref, right_ref, own_ref = refs[:4]
    refs = refs[4:]
    if scaled:
        block_ref, refs = refs[0], refs[1:]
    first, refs = refs[:shares], refs[shares:]
    others, refs = refs[: slots - 2], refs[slots - 2 :]
    if passes:
        rows_ref, refs = refs[0], refs[1:]
    t_ref, refs = refs[0], refs[1:]
    if scaled:
        unit_ref, refs = refs[0], refs[1:]
    if passes:
        refs[0][...] = rows_ref[...]
        refs = refs[1:]
    acc, source, order, slot_of = refs
    count = list_channels("rest", places, kinds_ref, order, slot_of, slots)
    if scaled:
        mine = jnp.maximum(peak(wide_float(block_ref)), SMALLEST)
        unit = mine
        for block in (*first, *others):
            unit = jnp.maximum(unit, peak(wide_float(block)))
        unit_ref[...] = jnp.broadcast_to(unit, unit_ref.shape)
        inverse = 1.0 / unit

    def scale(block):
        return (wide_float(block) * inverse).astype(jnp.bfloat16) if scaled else block[...]

    share = source.shape[1] // shares
    for step, block in enumerate(first):
        at = 0 if shares == 1 else jnp.abs(step - lax.axis_index("mpo"))
        source[1, pl.ds(pl.multiple_of(at * share, share), share), :] = scale(block)
    for slot, block in enumerate(others, 2):
        source[slot] = scale(block)
    source[slots] = jnp.zeros(source.shape[1:], jnp.bfloat16)
    acc[...] = own_ref[...] * (mine * inverse) if scaled else own_ref[...]
    multiply_listed(count, left_ref, right_ref, source, acc, order, slot_of)
    t_ref[...] = acc[...].astype(jnp.bfloat16)


def my_rows(share):
    return pl.ds(pl.multiple_of(lax.axis_index("mpo") * share, share), share)


def first_sums_kernel(*refs):
    parts, (psi_ref, unit_ref, w_ref, share_ref, rows_ref) = refs[:-5], refs[-5:]
    w = sum_parts(parts)
    unit = lane_of(first_row(unit_ref), 0)
    w_ref[...] = (w * unit).astype(jnp.bfloat16)
    share_ref[...] = w_ref[my_rows(share_ref.shape[0]), :]
    v = wide_float(psi_ref) * (1.0 / unit)
    a = total(v * w)
    d = total(v * v)
    local = a / jnp.maximum(d, SMALLEST)
    r = w - local * v
    sums = pack([a, d, local, total(r * v), total(r * r), unit], rows_ref.shape)
    row = lax.broadcasted_iota(jnp.int32, rows_ref.shape, 0)
    rows_ref[...] = jnp.where(row == here(), sums, 0.0)


def shrink(scal):
    return 1.0 / (jnp.abs(lane_of(scal, 0)) + lane_of(scal, 1))


def second_sums_kernel(entries, *refs):
    parts, refs = refs[:-9], refs[-9:]
    rows_ref, psi_ref, first_ref, unit_ref, wide_ref, w_ref, share_ref, v_ref, scal_ref = refs
    rows = rows_ref[...]
    a, d, local, p, q, unit = (lane_of(rows, lane) for lane in range(6))
    beta_0 = jnp.sqrt(column_sum(unit * unit * d) / entries + EPSILON)
    start_inverse = 1.0 / beta_0
    gain = unit * start_inverse
    alpha = column_sum(gain * (gain * a)) / entries
    off = local - alpha
    square = column_sum(gain * (gain * (q + off * (2.0 * p + off * d))))
    beta = jnp.sqrt(jnp.maximum(square, 0.0) / entries + EPSILON)
    inverse = 1.0 / beta
    scal = pack([alpha, beta, start_inverse], scal_ref.shape)
    scal_ref[...] = scal
    image = wide_float(first_ref) * start_inverse
    v_ref[...] = ((image - (alpha * start_inverse) * wide_float(psi_ref)) * inverse).astype(jnp.bfloat16)
    lift = lane_of(first_row(unit_ref), 0) * start_inverse
    w = (sum_parts(parts) * lift - alpha * image) * (inverse * shrink(first_row(scal)))
    wide_ref[...] = w
    w_ref[...] = w.astype(jnp.bfloat16)
    share_ref[...] = w_ref[my_rows(share_ref.shape[0]), :]


def third_sums_kernel(*refs):
    parts, refs = refs[:-8], refs[-8:]
    psi_ref, first_ref, v_ref, w_ref, scal_ref, r_ref, z_ref, rows_ref = refs
    scal = first_row(scal_ref)
    scale = shrink(scal)
    push = scale * lane_of(scal, 1) * lane_of(scal, 2)
    v, w = wide_float(v_ref), w_ref[...]
    vv, vw = total(v * v), total(v * w)
    local = vw / jnp.maximum(vv, SMALLEST)
    r = w - local * v - push * wide_float(psi_ref)
    z = sum_parts(parts) - (local / scale) * w - push * wide_float(first_ref)
    r_ref[...] = r
    z_ref[...] = z
    sums = [total(r * r), total(r * v), total(r * z), total(r * w)]
    sums += [total(z * v), total(z * w), total(z * z), total(w * w)]
    rows_ref[...] = pack([vv, vw, local] + sums, rows_ref.shape)


def final_kernel(entries, rows_ref, r_ref, z_ref, w_ref, v_ref, scal_ref, basis_ref, coef_ref):
    share = basis_ref.shape[2]
    mine = my_rows(share)
    vv, vw, local, rr, rv, rz, rw, zv, zw, zz, ww = (lane_of(rows_ref[...], i) for i in range(11))
    scal = first_row(scal_ref)
    scale = shrink(scal)
    inverse_scale = 1.0 / scale
    alpha_scaled = column_sum(vw) / entries
    off = local - alpha_scaled
    lift = off * inverse_scale
    square = column_sum(rr + off * (2.0 * rv + off * vv)) / entries
    beta_scaled = jnp.sqrt(jnp.maximum(square, 0.0) + scale * scale * EPSILON)
    inverse = 1.0 / beta_scaled
    mixed = column_sum(rz + lift * rw + off * (zv + lift * vw)) / entries
    alpha_3 = mixed * inverse * inverse
    r_v = column_sum(rv + off * vv) / entries
    z_v = column_sum(zv + lift * vw) / entries
    z_z = column_sum(zz + lift * (2.0 * zw + lift * ww)) / entries
    v_v = column_sum(vv) / entries
    beta_2 = beta_scaled * inverse_scale
    third = (z_z - 2.0 * alpha_3 * mixed + alpha_3 * alpha_3 * square) * inverse * inverse
    third += beta_2 * (beta_2 * v_v - 2.0 * inverse * (z_v - alpha_3 * r_v))
    beta_3 = jnp.sqrt(jnp.maximum(third, 0.0) + EPSILON)

    sector = here()
    row_of = lax.broadcasted_iota(jnp.int32, off.shape, 0)
    off_here = column_sum(jnp.where(row_of == sector, off, 0.0))
    v = v_ref[mine, :]
    v_wide = v.astype(jnp.float32)
    v_3 = (r_ref[mine, :] + off_here * v_wide) * inverse
    image = (z_ref[mine, :] + (off_here * inverse_scale) * w_ref[mine, :]) * inverse
    basis_ref[0, 0] = v
    basis_ref[1, 0] = v_3.astype(jnp.bfloat16)
    residual = image - alpha_3 * v_3 - beta_2 * v_wide
    basis_ref[2, 0] = (residual * (1.0 / beta_3)).astype(jnp.bfloat16)

    row = lax.broadcasted_iota(jnp.int32, coef_ref.shape, 0)
    column = lax.broadcasted_iota(jnp.int32, coef_ref.shape, 1)
    out = jnp.zeros(coef_ref.shape, jnp.float32)
    pairs = [(lane_of(scal, 0), lane_of(scal, 1)), (alpha_scaled * inverse_scale, beta_2), (alpha_3, beta_3)]
    for step, (a, b) in enumerate(pairs):
        out = jnp.where(column == step, jnp.where(row == 0, a, b), out)
    coef_ref[...] = out


def shards(wavefunction, env_left, env_right, channel_class):
    width = wavefunction.shape[1]
    ring = ("blk", "rep")
    parts = lax.axis_size("mpo")
    blocks = lax.axis_size("blk") * lax.axis_size("rep")
    entries = blocks * width * width
    permutes = routes(blocks)
    places, origins = slot_tables(permutes, blocks)
    slots = 1 + len(permutes)
    channels = channel_class.shape[0]
    psi, left, right = wavefunction[0], env_left[:, 0], env_right[:, 0]
    rows_shape = jax.ShapeDtypeStruct((blocks, 128), jnp.float32)
    scalars = jax.ShapeDtypeStruct((8, 128), jnp.float32)
    wide = jax.ShapeDtypeStruct((width, width), jnp.float32)
    narrow = jax.ShapeDtypeStruct((width, width), jnp.bfloat16)
    lists = [pltpu.SMEM((channels + WIDE,), jnp.int32)] * 2

    def call(kernel, name, outs, args, scratch=(), share=0, limit=4):
        flops = int(4 * channels * share * width**3)
        cost = pl.CostEstimate(flops=flops, bytes_accessed=4 * width * width, transcendentals=0)
        listed = outs if isinstance(outs, tuple) else (outs,)
        first = SMEM if share else VMEM
        return pl.pallas_call(
            kernel,
            out_shape=outs,
            in_specs=[first] + [VMEM] * (len(args) - 1),
            out_specs=tuple(VMEM for _ in listed) if isinstance(outs, tuple) else VMEM,
            scratch_shapes=list(scratch),
            compiler_params=pltpu.CompilerParams(vmem_limit_bytes=limit * MIB),
            cost_estimate=cost,
            name=name,
        )(*args)

    def sources(count):
        return pltpu.VMEM((count + 1, width, width), jnp.bfloat16)

    def own(scaled, block):
        return call(
            functools.partial(own_kernel, scaled, places),
            "own",
            wide,
            (channel_class, left, right, block),
            [sources(1)] + lists,
            0.2,
            16,
        )

    def rest(mine, first, others, block=None, rows=None):
        scaled, passes = block is not None, rows is not None
        outs = (narrow,) + (scalars,) * scaled + (rows_shape,) * passes
        args = [channel_class, left, right, mine] + [block] * scaled + first + others + [rows] * passes
        return call(
            functools.partial(rest_kernel, scaled, passes, len(first), slots, places),
            "rest",
            outs,
            args,
            [pltpu.VMEM((width, width), jnp.float32), sources(slots)] + lists,
            0.4,
            16,
        )

    def shift(block, pairs):
        return lax.ppermute(block, ring, pairs)

    def spread(block, share):
        piece = shift(share, permutes[0])
        if parts == 2:
            first = [piece, lax.ppermute(piece, "mpo", [(0, 1), (1, 0)])]
        else:
            first = [lax.all_gather(piece, "mpo", axis=0, tiled=True)]
        return first, [shift(block, pairs) for pairs in permutes[1:]]

    def gather_parts(t):
        if parts == 2:
            return [t, lax.ppermute(t, "mpo", [(0, 1), (1, 0)])]
        held = lax.all_gather(t, "mpo")
        return [held[i] for i in range(parts)]

    def exchange(rows):
        return lax.all_to_all(rows, ring, 0, 0, tiled=True)

    rounds = []
    for axis in ("rep", "blk"):
        size = lax.axis_size(axis)
        bits = [1 << i for i in range(size.bit_length() - 1)]
        if sum(bits) == size - 1:
            rounds += [(axis, [(i, i ^ bit) for i in range(size)]) for bit in bits]
        else:
            rounds += [(axis, None)]

    def add_round(rows, axis, pairs):
        if pairs is None:
            return lax.psum(rows, axis)
        return rows + lax.ppermute(rows, axis, pairs)

    share = jax.ShapeDtypeStruct((width // parts, width), jnp.bfloat16)
    held = [shift(psi, pairs) for pairs in permutes]
    t, unit = rest(own(True, psi), held[:1], held[1:], psi)
    w_1, share_1, rows = call(
        first_sums_kernel, "sums", (narrow, share, rows_shape), (*gather_parts(t), psi, unit)
    )
    held = spread(w_1, share_1)
    for step in rounds[:-1]:
        rows = add_round(rows, *step)
    t, unit, rows = rest(own(True, w_1), *held, w_1, rows)
    rows = add_round(rows, *rounds[-1])
    w_wide, w_2, share_2, v_2, scal = call(
        functools.partial(second_sums_kernel, entries),
        "sums",
        (wide, narrow, share, narrow, scalars),
        (*gather_parts(t), rows, psi, w_1, unit),
    )
    (t,) = rest(own(False, w_2), *spread(w_2, share_2))
    r, z, rows = call(
        third_sums_kernel,
        "sums",
        (wide, wide, rows_shape),
        (*gather_parts(t), psi, w_1, v_2, w_wide, scal),
        limit=8,
    )
    return call(
        functools.partial(final_kernel, entries),
        "final",
        (
            jax.ShapeDtypeStruct((STEPS, 1, width // parts, width), jnp.bfloat16),
            jax.ShapeDtypeStruct((2, STEPS), jnp.float32),
        ),
        (exchange(rows), r, z, w_wide, v_2, scal),
    )


def solution(mesh):
    return jax.shard_map(
        shards,
        mesh=mesh,
        in_specs=(
            P(("groups", "blk", "rep"), None, None),
            P("mpo", ("groups", "blk", "rep"), None, None),
            P("mpo", ("groups", "blk", "rep"), None, None),
            P("mpo"),
        ),
        out_specs=(P(None, ("groups", "blk", "rep"), "mpo", None), P("groups", None)),
        check_vma=False,
    )
```

```python
import functools

import jax
import jax.numpy as jnp
from jax import lax
from jax.experimental import pallas as pl
from jax.experimental.pallas import tpu as pltpu
from jax.sharding import PartitionSpec as P

NS = 4
STEPS = 3
OFFSETS = (0, NS + 1, NS - 1, -(NS + 1), -(NS - 1))
EPSILON = 1e-06
WIDE = 8
SMALLEST = 1e-30
MIB = 1024 * 1024
VMEM = pl.BlockSpec(memory_space=pltpu.VMEM)
SMEM = pl.BlockSpec(memory_space=pltpu.SMEM)


def reaches(kind, sector, blocks):
    source = sector - OFFSETS[kind]
    spin = sector % NS
    inside = (source >= 0) & (source < blocks)
    if kind in (1, 4):
        return inside & (spin >= 1)
    if kind in (2, 3):
        return inside & (spin <= NS - 2)
    return inside


def routes(blocks):
    degree, edges = [0] * blocks, []
    for kind in (1, 2):
        for k in range(blocks):
            if reaches(kind, k, blocks):
                edges.append((k - OFFSETS[kind], k))
                degree[k - OFFSETS[kind]] += 1
                degree[k] += 1
    edges.sort(key=lambda edge: degree[edge[0]] + degree[edge[1]])
    partner = [{} for _ in range(blocks)]

    def lowest(block):
        return next(c for c in range(len(edges)) if c not in partner[block])

    for a, b in edges:
        here_free, there_free = lowest(a), lowest(b)
        if here_free in partner[b]:
            path, block, colour = [b], b, here_free
            while colour in partner[block]:
                block = partner[block][colour]
                path.append(block)
                colour = there_free if colour == here_free else here_free
            for block in path:
                moved = {}
                for old, new in ((here_free, there_free), (there_free, here_free)):
                    if old in partner[block]:
                        moved[new] = partner[block].pop(old)
                partner[block].update(moved)
        partner[a][here_free], partner[b][here_free] = b, a
    colours = sorted({c for held in partner for c in held})
    permutes = [[(held[c], k) for k, held in enumerate(partner) if c in held] for c in colours]
    return sorted(permutes, key=len, reverse=True)


def slot_tables(permutes, blocks):
    origins = [{k: k for k in range(blocks)}] + [{k: s for s, k in pairs} for pairs in permutes]
    places = []
    for kind in range(5):
        place = {}
        for slot, origin in enumerate(origins):
            for k, source in origin.items():
                if source == k - OFFSETS[kind] and reaches(kind, k, blocks):
                    place[k] = slot
        places.append(place)
    return places, origins


def look_up(table, sector, default):
    out = jnp.int32(default)
    for k, value in table.items():
        if value != default:
            out = jnp.where(sector == k, jnp.int32(value), out)
    return out


def here():
    return lax.axis_index("blk") * lax.axis_size("rep") + lax.axis_index("rep")


def lane_of(rows, lane):
    return rows[:, lane : lane + 1]


def pack(values, shape):
    lanes = lax.broadcasted_iota(jnp.int32, shape, 1)
    out = jnp.zeros(shape, jnp.float32)
    for place, value in enumerate(values):
        out = jnp.where(lanes == place, value, out)
    return out


def total(x):
    return jnp.sum(jnp.sum(x, axis=0, keepdims=True), axis=1, keepdims=True)


def column_sum(x):
    return jnp.sum(x, axis=0, keepdims=True)


def peak(x):
    return jnp.max(jnp.max(jnp.abs(x), axis=0, keepdims=True), axis=1, keepdims=True)


def wide_float(ref):
    return ref[...].astype(jnp.float32)


def sum_parts(parts):
    w = wide_float(parts[0])
    for part in parts[1:]:
        w += wide_float(part)
    return w


def first_row(ref):
    return ref[0:1, :]


def list_channels(which, places, kinds_ref, order, slot_of, idle):
    sector = here()
    slots = [jnp.int32(-1 if which == "rest" else 0)]
    slots += [look_up(places[c], sector, -1) if which != "own" else jnp.int32(-1) for c in range(1, 5)]
    count = jnp.int32(0)
    for b in range(kinds_ref.shape[0]):
        kind = kinds_ref[b]
        slot = slots[0]
        for c in range(1, 5):
            slot = jnp.where(kind == c, slots[c], slot)
        order[count] = jnp.int32(b)
        slot_of[count] = slot
        count += jnp.where(slot >= 0, 1, 0)
    for extra in range(WIDE):
        order[count + extra] = jnp.int32(0)
        slot_of[count + extra] = jnp.int32(idle)
    return count


def multiply_listed(count, left_ref, right_ref, source, acc, order, slot_of):
    def multiply(start, wide):
        held = [order[start + inner] for inner in range(wide)]
        pieces = [
            jnp.dot(
                left_ref[b], source[slot_of[start + inner]], preferred_element_type=jnp.float32
            ).astype(jnp.bfloat16)
            for inner, b in enumerate(held)
        ]
        acc[...] += lax.dot_general(
            jnp.concatenate(pieces, axis=1),
            jnp.concatenate([right_ref[b] for b in held], axis=1),
            (((1,), (1,)), ((), ())),
            preferred_element_type=jnp.float32,
        )

    def full(group, carry):
        multiply(group * WIDE, WIDE)
        return carry

    groups = (count + WIDE // 2 - 1) // WIDE
    lax.fori_loop(0, groups, full, 0)
    rest = count - groups * WIDE
    for low, wide in ((0, 2), (2, 4)):

        @pl.when((rest > low) & (rest <= wide))
        def _():
            multiply(groups * WIDE, wide)


def own_kernel(scaled, places, kinds_ref, left_ref, right_ref, block_ref, acc, source, order, slot_of):
    count = list_channels("own", places, kinds_ref, order, slot_of, 1)
    if scaled:
        block = wide_float(block_ref)
        inverse = 1.0 / jnp.maximum(peak(block), SMALLEST)
        source[0] = (block * inverse).astype(jnp.bfloat16)
    else:
        source[0] = block_ref[...]
    source[1] = jnp.zeros(source.shape[1:], jnp.bfloat16)
    acc[...] = jnp.zeros_like(acc)
    multiply_listed(count, left_ref, right_ref, source, acc, order, slot_of)


def rest_kernel(scaled, passes, shares, slots, places, *refs):
    kinds_ref, left_ref, right_ref, own_ref = refs[:4]
    refs = refs[4:]
    if scaled:
        block_ref, refs = refs[0], refs[1:]
    first, refs = refs[:shares], refs[shares:]
    others, refs = refs[: slots - 2], refs[slots - 2 :]
    if passes:
        rows_ref, refs = refs[0], refs[1:]
    t_ref, refs = refs[0], refs[1:]
    if scaled:
        unit_ref, refs = refs[0], refs[1:]
    if passes:
        refs[0][...] = rows_ref[...]
        refs = refs[1:]
    acc, source, order, slot_of = refs
    count = list_channels("rest", places, kinds_ref, order, slot_of, slots)
    if scaled:
        mine = jnp.maximum(peak(wide_float(block_ref)), SMALLEST)
        unit = mine
        for block in (*first, *others):
            unit = jnp.maximum(unit, peak(wide_float(block)))
        unit_ref[...] = jnp.broadcast_to(unit, unit_ref.shape)
        inverse = 1.0 / unit

    def scale(block):
        return (wide_float(block) * inverse).astype(jnp.bfloat16) if scaled else block[...]

    share = source.shape[1] // shares
    for step, block in enumerate(first):
        at = 0 if shares == 1 else jnp.abs(step - lax.axis_index("mpo"))
        source[1, pl.ds(pl.multiple_of(at * share, share), share), :] = scale(block)
    for slot, block in enumerate(others, 2):
        source[slot] = scale(block)
    source[slots] = jnp.zeros(source.shape[1:], jnp.bfloat16)
    acc[...] = own_ref[...] * (mine * inverse) if scaled else own_ref[...]
    multiply_listed(count, left_ref, right_ref, source, acc, order, slot_of)
    t_ref[...] = acc[...].astype(jnp.bfloat16)


def pass_kernel(block_ref, rows_ref, out_ref):
    out_ref[...] = block_ref[...]


def my_rows(share):
    return pl.ds(pl.multiple_of(lax.axis_index("mpo") * share, share), share)


def first_sums_kernel(*refs):
    parts, (psi_ref, unit_ref, w_ref, share_ref, rows_ref) = refs[:-5], refs[-5:]
    w = sum_parts(parts)
    unit = lane_of(first_row(unit_ref), 0)
    w_ref[...] = (w * unit).astype(jnp.bfloat16)
    share_ref[...] = w_ref[my_rows(share_ref.shape[0]), :]
    v = wide_float(psi_ref) * (1.0 / unit)
    a = total(v * w)
    d = total(v * v)
    local = a / jnp.maximum(d, SMALLEST)
    r = w - local * v
    sums = pack([a, d, local, total(r * v), total(r * r), unit], rows_ref.shape)
    row = lax.broadcasted_iota(jnp.int32, rows_ref.shape, 0)
    rows_ref[...] = jnp.where(row == here(), sums, 0.0)


def shrink(scal):
    return 1.0 / (jnp.abs(lane_of(scal, 0)) + lane_of(scal, 1))


def second_sums_kernel(entries, *refs):
    parts, refs = refs[:-9], refs[-9:]
    rows_ref, psi_ref, first_ref, unit_ref, wide_ref, w_ref, share_ref, v_ref, scal_ref = refs
    rows = rows_ref[...]
    a, d, local, p, q, unit = (lane_of(rows, lane) for lane in range(6))
    beta_0 = jnp.sqrt(column_sum(unit * unit * d) / entries + EPSILON)
    start_inverse = 1.0 / beta_0
    gain = unit * start_inverse
    alpha = column_sum(gain * (gain * a)) / entries
    off = local - alpha
    square = column_sum(gain * (gain * (q + off * (2.0 * p + off * d))))
    beta = jnp.sqrt(jnp.maximum(square, 0.0) / entries + EPSILON)
    inverse = 1.0 / beta
    scal = pack([alpha, beta, start_inverse], scal_ref.shape)
    scal_ref[...] = scal
    image = wide_float(first_ref) * start_inverse
    v_ref[...] = ((image - (alpha * start_inverse) * wide_float(psi_ref)) * inverse).astype(jnp.bfloat16)
    lift = lane_of(first_row(unit_ref), 0) * start_inverse
    w = (sum_parts(parts) * lift - alpha * image) * (inverse * shrink(first_row(scal)))
    wide_ref[...] = w
    w_ref[...] = w.astype(jnp.bfloat16)
    share_ref[...] = w_ref[my_rows(share_ref.shape[0]), :]


def third_sums_kernel(*refs):
    parts, refs = refs[:-8], refs[-8:]
    psi_ref, first_ref, v_ref, w_ref, scal_ref, r_ref, z_ref, rows_ref = refs
    scal = first_row(scal_ref)
    scale = shrink(scal)
    push = scale * lane_of(scal, 1) * lane_of(scal, 2)
    v, w = wide_float(v_ref), w_ref[...]
    vv, vw = total(v * v), total(v * w)
    local = vw / jnp.maximum(vv, SMALLEST)
    r = w - local * v - push * wide_float(psi_ref)
    z = sum_parts(parts) - (local / scale) * w - push * wide_float(first_ref)
    r_ref[...] = r
    z_ref[...] = z
    sums = [total(r * r), total(r * v), total(r * z), total(r * w)]
    sums += [total(z * v), total(z * w), total(z * z), total(w * w)]
    rows_ref[...] = pack([vv, vw, local] + sums, rows_ref.shape)


def final_kernel(entries, rows_ref, r_ref, z_ref, w_ref, v_ref, scal_ref, basis_ref, coef_ref):
    share = basis_ref.shape[2]
    mine = my_rows(share)
    vv, vw, local, rr, rv, rz, rw, zv, zw, zz, ww = (lane_of(rows_ref[...], i) for i in range(11))
    scal = first_row(scal_ref)
    scale = shrink(scal)
    inverse_scale = 1.0 / scale
    alpha_scaled = column_sum(vw) / entries
    off = local - alpha_scaled
    lift = off * inverse_scale
    square = column_sum(rr + off * (2.0 * rv + off * vv)) / entries
    beta_scaled = jnp.sqrt(jnp.maximum(square, 0.0) + scale * scale * EPSILON)
    inverse = 1.0 / beta_scaled
    mixed = column_sum(rz + lift * rw + off * (zv + lift * vw)) / entries
    alpha_3 = mixed * inverse * inverse
    r_v = column_sum(rv + off * vv) / entries
    z_v = column_sum(zv + lift * vw) / entries
    z_z = column_sum(zz + lift * (2.0 * zw + lift * ww)) / entries
    v_v = column_sum(vv) / entries
    beta_2 = beta_scaled * inverse_scale
    third = (z_z - 2.0 * alpha_3 * mixed + alpha_3 * alpha_3 * square) * inverse * inverse
    third += beta_2 * (beta_2 * v_v - 2.0 * inverse * (z_v - alpha_3 * r_v))
    beta_3 = jnp.sqrt(jnp.maximum(third, 0.0) + EPSILON)

    sector = here()
    row_of = lax.broadcasted_iota(jnp.int32, off.shape, 0)
    off_here = column_sum(jnp.where(row_of == sector, off, 0.0))
    v = v_ref[mine, :]
    v_wide = v.astype(jnp.float32)
    v_3 = (r_ref[mine, :] + off_here * v_wide) * inverse
    image = (z_ref[mine, :] + (off_here * inverse_scale) * w_ref[mine, :]) * inverse
    basis_ref[0, 0] = v
    basis_ref[1, 0] = v_3.astype(jnp.bfloat16)
    residual = image - alpha_3 * v_3 - beta_2 * v_wide
    basis_ref[2, 0] = (residual * (1.0 / beta_3)).astype(jnp.bfloat16)

    row = lax.broadcasted_iota(jnp.int32, coef_ref.shape, 0)
    column = lax.broadcasted_iota(jnp.int32, coef_ref.shape, 1)
    out = jnp.zeros(coef_ref.shape, jnp.float32)
    pairs = [(lane_of(scal, 0), lane_of(scal, 1)), (alpha_scaled * inverse_scale, beta_2), (alpha_3, beta_3)]
    for step, (a, b) in enumerate(pairs):
        out = jnp.where(column == step, jnp.where(row == 0, a, b), out)
    coef_ref[...] = out


def shards(wavefunction, env_left, env_right, channel_class):
    width = wavefunction.shape[1]
    ring = ("blk", "rep")
    parts = lax.axis_size("mpo")
    blocks = lax.axis_size("blk") * lax.axis_size("rep")
    entries = blocks * width * width
    permutes = routes(blocks)
    places, origins = slot_tables(permutes, blocks)
    slots = 1 + len(permutes)
    channels = channel_class.shape[0]
    psi, left, right = wavefunction[0], env_left[:, 0], env_right[:, 0]
    rows_shape = jax.ShapeDtypeStruct((blocks, 128), jnp.float32)
    scalars = jax.ShapeDtypeStruct((8, 128), jnp.float32)
    wide = jax.ShapeDtypeStruct((width, width), jnp.float32)
    narrow = jax.ShapeDtypeStruct((width, width), jnp.bfloat16)
    share_shape = jax.ShapeDtypeStruct((width // parts, width), jnp.bfloat16)
    lists = [pltpu.SMEM((channels + WIDE,), jnp.int32)] * 2

    def call(kernel, name, outs, args, scratch=(), share=0, limit=4):
        flops = int(4 * channels * share * width**3)
        cost = pl.CostEstimate(flops=flops, bytes_accessed=4 * width * width, transcendentals=0)
        listed = outs if isinstance(outs, tuple) else (outs,)
        first = SMEM if share else VMEM
        return pl.pallas_call(
            kernel,
            out_shape=outs,
            in_specs=[first] + [VMEM] * (len(args) - 1),
            out_specs=tuple(VMEM for _ in listed) if isinstance(outs, tuple) else VMEM,
            scratch_shapes=list(scratch),
            compiler_params=pltpu.CompilerParams(vmem_limit_bytes=limit * MIB),
            cost_estimate=cost,
            name=name,
        )(*args)

    def sources(count):
        return pltpu.VMEM((count + 1, width, width), jnp.bfloat16)

    def own(scaled, block):
        return call(
            functools.partial(own_kernel, scaled, places),
            "own",
            wide,
            (channel_class, left, right, block),
            [sources(1)] + lists,
            0.2,
            16,
        )

    def rest(mine, first, others, block=None, rows=None):
        scaled, passes = block is not None, rows is not None
        outs = (narrow,) + (scalars,) * scaled + (rows_shape,) * passes
        args = [channel_class, left, right, mine] + [block] * scaled + first + others + [rows] * passes
        return call(
            functools.partial(rest_kernel, scaled, passes, len(first), slots, places),
            "rest",
            outs,
            args,
            [pltpu.VMEM((width, width), jnp.float32), sources(slots)] + lists,
            0.4,
            16,
        )

    def shift(block, pairs):
        return lax.ppermute(block, ring, pairs)

    rounds = []
    for axis in ("rep", "blk"):
        size = lax.axis_size(axis)
        bits = [1 << i for i in range(size.bit_length() - 1)]
        if sum(bits) == size - 1:
            rounds += [(axis, [(i, i ^ bit) for i in range(size)]) for bit in bits]
        else:
            rounds += [(axis, None)]

    def add_round(rows, axis, pairs):
        if pairs is None:
            return lax.psum(rows, axis)
        return rows + lax.ppermute(rows, axis, pairs)

    def spread(block, share, rows=None):
        piece = shift(share, permutes[0])
        if rows is not None:
            for step in rounds[:-1]:
                rows = add_round(rows, *step)
            piece = call(pass_kernel, "hold", share_shape, (piece, rows))
        if parts == 2:
            first = [piece, lax.ppermute(piece, "mpo", [(0, 1), (1, 0)])]
        else:
            first = [lax.all_gather(piece, "mpo", axis=0, tiled=True)]
        return first, [shift(block, pairs) for pairs in permutes[1:]], rows

    def gather_parts(t):
        if parts == 2:
            return [t, lax.ppermute(t, "mpo", [(0, 1), (1, 0)])]
        held = lax.all_gather(t, "mpo")
        return [held[i] for i in range(parts)]

    def exchange(rows):
        return lax.all_to_all(rows, ring, 0, 0, tiled=True)

    held = [shift(psi, pairs) for pairs in permutes]
    t, unit = rest(own(True, psi), held[:1], held[1:], psi)
    w_1, share_1, rows = call(
        first_sums_kernel, "sums", (narrow, share_shape, rows_shape), (*gather_parts(t), psi, unit)
    )
    first, others, rows = spread(w_1, share_1, rows)
    t, unit, rows = rest(own(True, w_1), first, others, w_1, rows)
    rows = add_round(rows, *rounds[-1])
    w_wide, w_2, share_2, v_2, scal = call(
        functools.partial(second_sums_kernel, entries),
        "sums",
        (wide, narrow, share_shape, narrow, scalars),
        (*gather_parts(t), rows, psi, w_1, unit),
    )
    first, others, _ = spread(w_2, share_2)
    (t,) = rest(own(False, w_2), first, others)
    r, z, rows = call(
        third_sums_kernel,
        "sums",
        (wide, wide, rows_shape),
        (*gather_parts(t), psi, w_1, v_2, w_wide, scal),
        limit=8,
    )
    return call(
        functools.partial(final_kernel, entries),
        "final",
        (
            jax.ShapeDtypeStruct((STEPS, 1, width // parts, width), jnp.bfloat16),
            jax.ShapeDtypeStruct((2, STEPS), jnp.float32),
        ),
        (exchange(rows), r, z, w_wide, v_2, scal),
    )


def solution(mesh):
    return jax.shard_map(
        shards,
        mesh=mesh,
        in_specs=(
            P(("groups", "blk", "rep"), None, None),
            P("mpo", ("groups", "blk", "rep"), None, None),
            P("mpo", ("groups", "blk", "rep"), None, None),
            P("mpo"),
        ),
        out_specs=(P(None, ("groups", "blk", "rep"), "mpo", None), P("groups", None)),
        check_vma=False,
    )
```

```python
import functools

import jax
import jax.numpy as jnp
from jax import lax
from jax.experimental import pallas as pl
from jax.experimental.pallas import tpu as pltpu
from jax.sharding import PartitionSpec as P

NS = 4
STEPS = 3
OFFSETS = (0, NS + 1, NS - 1, -(NS + 1), -(NS - 1))
EPSILON = 1e-06
WIDE = 8
SMALLEST = 1e-30
TILE = 16
MIB = 1024 * 1024
VMEM = pl.BlockSpec(memory_space=pltpu.VMEM)
SMEM = pl.BlockSpec(memory_space=pltpu.SMEM)


def reaches(kind, sector, blocks):
    source = sector - OFFSETS[kind]
    spin = sector % NS
    inside = (source >= 0) & (source < blocks)
    if kind in (1, 4):
        return inside & (spin >= 1)
    if kind in (2, 3):
        return inside & (spin <= NS - 2)
    return inside


def routes(blocks):
    degree, edges = [0] * blocks, []
    for kind in (1, 2):
        for k in range(blocks):
            if reaches(kind, k, blocks):
                edges.append((k - OFFSETS[kind], k))
                degree[k - OFFSETS[kind]] += 1
                degree[k] += 1
    edges.sort(key=lambda edge: degree[edge[0]] + degree[edge[1]])
    partner = [{} for _ in range(blocks)]

    def lowest(block):
        return next(c for c in range(len(edges)) if c not in partner[block])

    for a, b in edges:
        here_free, there_free = lowest(a), lowest(b)
        if here_free in partner[b]:
            path, block, colour = [b], b, here_free
            while colour in partner[block]:
                block = partner[block][colour]
                path.append(block)
                colour = there_free if colour == here_free else here_free
            for block in path:
                moved = {}
                for old, new in ((here_free, there_free), (there_free, here_free)):
                    if old in partner[block]:
                        moved[new] = partner[block].pop(old)
                partner[block].update(moved)
        partner[a][here_free], partner[b][here_free] = b, a
    colours = sorted({c for held in partner for c in held})
    permutes = [[(held[c], k) for k, held in enumerate(partner) if c in held] for c in colours]
    return sorted(permutes, key=len, reverse=True)


def slot_tables(permutes, blocks):
    origins = [{k: k for k in range(blocks)}] + [{k: s for s, k in pairs} for pairs in permutes]
    places = []
    for kind in range(5):
        place = {}
        for slot, origin in enumerate(origins):
            for k, source in origin.items():
                if source == k - OFFSETS[kind] and reaches(kind, k, blocks):
                    place[k] = slot
        places.append(place)
    return places, origins


def carried_rounds(permutes, blocks):
    if len(permutes) < 2 or blocks % 2:
        return None
    last = dict(permutes[1])
    for k in range(blocks):
        if k not in last:
            last[k] = blocks - 1 - k
    rounds = [dict(permutes[0]), {k: k ^ 1 for k in range(blocks)}, last]
    held = [{k} for k in range(blocks)]
    for pairs in rounds:
        if sorted(pairs.values()) != list(range(blocks)):
            return None
        if any(held[source] & held[k] for source, k in pairs.items()):
            return None
        grown = list(held)
        for source, k in pairs.items():
            grown[k] = held[k] | held[source]
        held = grown
    if any(len(rows) < blocks for rows in held):
        return None
    return [sorted(pairs.items()) for pairs in rounds[1:]]


def look_up(table, sector, default):
    out = jnp.int32(default)
    for k, value in table.items():
        if value != default:
            out = jnp.where(sector == k, jnp.int32(value), out)
    return out


def here():
    return lax.axis_index("blk") * lax.axis_size("rep") + lax.axis_index("rep")


def lane_of(rows, lane):
    return rows[:, lane : lane + 1]


def pack(values, shape):
    lanes = lax.broadcasted_iota(jnp.int32, shape, 1)
    out = jnp.zeros(shape, jnp.float32)
    for place, value in enumerate(values):
        out = jnp.where(lanes == place, value, out)
    return out


def total(x):
    return jnp.sum(jnp.sum(x, axis=0, keepdims=True), axis=1, keepdims=True)


def column_sum(x):
    return jnp.sum(x, axis=0, keepdims=True)


def peak(x):
    return jnp.max(jnp.max(jnp.abs(x), axis=0, keepdims=True), axis=1, keepdims=True)


def wide_float(ref):
    return ref[...].astype(jnp.float32)


def sum_parts(parts):
    w = wide_float(parts[0])
    for part in parts[1:]:
        w += wide_float(part)
    return w


def first_row(ref):
    return ref[0:1, :]


def list_channels(which, places, kinds_ref, order, slot_of, idle):
    sector = here()
    slots = [jnp.int32(-1 if which == "rest" else 0)]
    slots += [look_up(places[c], sector, -1) if which != "own" else jnp.int32(-1) for c in range(1, 5)]
    count = jnp.int32(0)
    for b in range(kinds_ref.shape[0]):
        kind = kinds_ref[b]
        slot = slots[0]
        for c in range(1, 5):
            slot = jnp.where(kind == c, slots[c], slot)
        order[count] = jnp.int32(b)
        slot_of[count] = slot
        count += jnp.where(slot >= 0, 1, 0)
    for extra in range(WIDE):
        order[count + extra] = jnp.int32(0)
        slot_of[count + extra] = jnp.int32(idle)
    return count


def multiply_listed(count, left_ref, right_ref, source, acc, order, slot_of):
    def multiply(start, wide):
        held = [order[start + inner] for inner in range(wide)]
        pieces = [
            jnp.dot(
                left_ref[b], source[slot_of[start + inner]], preferred_element_type=jnp.float32
            ).astype(jnp.bfloat16)
            for inner, b in enumerate(held)
        ]
        acc[...] += lax.dot_general(
            jnp.concatenate(pieces, axis=1),
            jnp.concatenate([right_ref[b] for b in held], axis=1),
            (((1,), (1,)), ((), ())),
            preferred_element_type=jnp.float32,
        )

    def full(group, carry):
        multiply(group * WIDE, WIDE)
        return carry

    groups = (count + WIDE // 2 - 1) // WIDE
    lax.fori_loop(0, groups, full, 0)
    rest = count - groups * WIDE
    for low, wide in ((0, 2), (2, 4)):

        @pl.when((rest > low) & (rest <= wide))
        def _():
            multiply(groups * WIDE, wide)


def own_kernel(scaled, places, kinds_ref, left_ref, right_ref, block_ref, acc, source, order, slot_of):
    count = list_channels("own", places, kinds_ref, order, slot_of, 1)
    if scaled:
        block = wide_float(block_ref)
        inverse = 1.0 / jnp.maximum(peak(block), SMALLEST)
        source[0] = (block * inverse).astype(jnp.bfloat16)
    else:
        source[0] = block_ref[...]
    source[1] = jnp.zeros(source.shape[1:], jnp.bfloat16)
    acc[...] = jnp.zeros_like(acc)
    multiply_listed(count, left_ref, right_ref, source, acc, order, slot_of)


def rest_kernel(scaled, passes, shares, slots, places, *refs):
    kinds_ref, left_ref, right_ref, own_ref = refs[:4]
    refs = refs[4:]
    if scaled:
        block_ref, refs = refs[0], refs[1:]
    first, refs = refs[:shares], refs[shares:]
    others, refs = refs[: slots - 2], refs[slots - 2 :]
    if passes:
        rows_ref, refs = refs[0], refs[1:]
    t_ref, refs = refs[0], refs[1:]
    if scaled:
        unit_ref, refs = refs[0], refs[1:]
    if passes:
        refs[0][...] = rows_ref[...]
        refs = refs[1:]
    acc, source, order, slot_of = refs
    count = list_channels("rest", places, kinds_ref, order, slot_of, slots)
    if scaled:
        mine = jnp.maximum(peak(wide_float(block_ref)), SMALLEST)
        unit = mine
        for block in (*first, *others):
            unit = jnp.maximum(unit, peak(wide_float(block)))
        unit_ref[...] = jnp.broadcast_to(unit, unit_ref.shape)
        inverse = 1.0 / unit

    def scale(block):
        return (wide_float(block) * inverse).astype(jnp.bfloat16) if scaled else block[...]

    share = source.shape[1] // shares
    for step, block in enumerate(first):
        at = 0 if shares == 1 else jnp.abs(step - lax.axis_index("mpo"))
        source[1, pl.ds(pl.multiple_of(at * share, share), share), :] = scale(block)
    for slot, block in enumerate(others, 2):
        source[slot] = scale(block)
    source[slots] = jnp.zeros(source.shape[1:], jnp.bfloat16)
    acc[...] = own_ref[...] * (mine * inverse) if scaled else own_ref[...]
    multiply_listed(count, left_ref, right_ref, source, acc, order, slot_of)
    t_ref[...] = acc[...].astype(jnp.bfloat16)


def pass_kernel(block_ref, rows_ref, out_ref):
    out_ref[...] = block_ref[...]


def unpack_kernel(origin, block_ref, rows_ref, out_ref, sums_ref):
    share = out_ref.shape[0]
    out_ref[...] = block_ref[0:share, :]
    terms = block_ref[share : share + 2 * TILE, :].astype(jnp.float32)
    sums = terms[0:TILE, 0:128] + terms[0:TILE, 128:256] + terms[TILE : 2 * TILE, 0:128]
    row = lax.broadcasted_iota(jnp.int32, rows_ref.shape, 0)
    source = look_up(origin, here(), 0)
    sums_ref[...] = jnp.where(row == source, first_row(sums), rows_ref[...])


def my_rows(share):
    return pl.ds(pl.multiple_of(lax.axis_index("mpo") * share, share), share)


def first_sums_kernel(share, *refs):
    parts, (psi_ref, unit_ref, w_ref, share_ref, rows_ref) = refs[:-5], refs[-5:]
    w = sum_parts(parts)
    unit = lane_of(first_row(unit_ref), 0)
    w_ref[...] = (w * unit).astype(jnp.bfloat16)
    share_ref[0:share, :] = w_ref[my_rows(share), :]
    v = wide_float(psi_ref) * (1.0 / unit)
    a = total(v * w)
    d = total(v * v)
    local = a / jnp.maximum(d, SMALLEST)
    r = w - local * v
    values = [a, d, local, total(r * v), total(r * r), unit]
    if share_ref.shape[0] > share:
        sums = pack(values, (TILE, 128))
        high = sums.astype(jnp.bfloat16)
        rest = sums - high.astype(jnp.float32)
        middle = rest.astype(jnp.bfloat16)
        low = (rest - middle.astype(jnp.float32)).astype(jnp.bfloat16)
        blank = jnp.zeros((2 * TILE, share_ref.shape[1]), jnp.bfloat16)
        share_ref[share : share + 2 * TILE, :] = blank
        share_ref[share : share + TILE, 0:128] = high
        share_ref[share : share + TILE, 128:256] = middle
        share_ref[share + TILE : share + 2 * TILE, 0:128] = low
        sums = high.astype(jnp.float32) + middle.astype(jnp.float32) + low.astype(jnp.float32)
        sums = jnp.broadcast_to(first_row(sums), rows_ref.shape)
    else:
        sums = pack(values, rows_ref.shape)
    row = lax.broadcasted_iota(jnp.int32, rows_ref.shape, 0)
    rows_ref[...] = jnp.where(row == here(), sums, 0.0)


def shrink(scal):
    return 1.0 / (jnp.abs(lane_of(scal, 0)) + lane_of(scal, 1))


def second_sums_kernel(entries, *refs):
    parts, refs = refs[:-9], refs[-9:]
    rows_ref, psi_ref, first_ref, unit_ref, wide_ref, w_ref, share_ref, v_ref, scal_ref = refs
    rows = rows_ref[...]
    a, d, local, p, q, unit = (lane_of(rows, lane) for lane in range(6))
    beta_0 = jnp.sqrt(column_sum(unit * unit * d) / entries + EPSILON)
    start_inverse = 1.0 / beta_0
    gain = unit * start_inverse
    alpha = column_sum(gain * (gain * a)) / entries
    off = local - alpha
    square = column_sum(gain * (gain * (q + off * (2.0 * p + off * d))))
    beta = jnp.sqrt(jnp.maximum(square, 0.0) / entries + EPSILON)
    inverse = 1.0 / beta
    scal = pack([alpha, beta, start_inverse], scal_ref.shape)
    scal_ref[...] = scal
    image = wide_float(first_ref) * start_inverse
    v_ref[...] = ((image - (alpha * start_inverse) * wide_float(psi_ref)) * inverse).astype(jnp.bfloat16)
    lift = lane_of(first_row(unit_ref), 0) * start_inverse
    w = (sum_parts(parts) * lift - alpha * image) * (inverse * shrink(first_row(scal)))
    wide_ref[...] = w
    w_ref[...] = w.astype(jnp.bfloat16)
    share_ref[...] = w_ref[my_rows(share_ref.shape[0]), :]


def third_sums_kernel(*refs):
    parts, refs = refs[:-8], refs[-8:]
    psi_ref, first_ref, v_ref, w_ref, scal_ref, r_ref, z_ref, rows_ref = refs
    scal = first_row(scal_ref)
    scale = shrink(scal)
    push = scale * lane_of(scal, 1) * lane_of(scal, 2)
    v, w = wide_float(v_ref), w_ref[...]
    vv, vw = total(v * v), total(v * w)
    local = vw / jnp.maximum(vv, SMALLEST)
    r = w - local * v - push * wide_float(psi_ref)
    z = sum_parts(parts) - (local / scale) * w - push * wide_float(first_ref)
    r_ref[...] = r
    z_ref[...] = z
    sums = [total(r * r), total(r * v), total(r * z), total(r * w)]
    sums += [total(z * v), total(z * w), total(z * z), total(w * w)]
    rows_ref[...] = pack([vv, vw, local] + sums, rows_ref.shape)


def final_kernel(entries, rows_ref, r_ref, z_ref, w_ref, v_ref, scal_ref, basis_ref, coef_ref):
    share = basis_ref.shape[2]
    mine = my_rows(share)
    vv, vw, local, rr, rv, rz, rw, zv, zw, zz, ww = (lane_of(rows_ref[...], i) for i in range(11))
    scal = first_row(scal_ref)
    scale = shrink(scal)
    inverse_scale = 1.0 / scale
    alpha_scaled = column_sum(vw) / entries
    off = local - alpha_scaled
    lift = off * inverse_scale
    square = column_sum(rr + off * (2.0 * rv + off * vv)) / entries
    beta_scaled = jnp.sqrt(jnp.maximum(square, 0.0) + scale * scale * EPSILON)
    inverse = 1.0 / beta_scaled
    mixed = column_sum(rz + lift * rw + off * (zv + lift * vw)) / entries
    alpha_3 = mixed * inverse * inverse
    r_v = column_sum(rv + off * vv) / entries
    z_v = column_sum(zv + lift * vw) / entries
    z_z = column_sum(zz + lift * (2.0 * zw + lift * ww)) / entries
    v_v = column_sum(vv) / entries
    beta_2 = beta_scaled * inverse_scale
    third = (z_z - 2.0 * alpha_3 * mixed + alpha_3 * alpha_3 * square) * inverse * inverse
    third += beta_2 * (beta_2 * v_v - 2.0 * inverse * (z_v - alpha_3 * r_v))
    beta_3 = jnp.sqrt(jnp.maximum(third, 0.0) + EPSILON)

    sector = here()
    row_of = lax.broadcasted_iota(jnp.int32, off.shape, 0)
    off_here = column_sum(jnp.where(row_of == sector, off, 0.0))
    v = v_ref[mine, :]
    v_wide = v.astype(jnp.float32)
    v_3 = (r_ref[mine, :] + off_here * v_wide) * inverse
    image = (z_ref[mine, :] + (off_here * inverse_scale) * w_ref[mine, :]) * inverse
    basis_ref[0, 0] = v
    basis_ref[1, 0] = v_3.astype(jnp.bfloat16)
    residual = image - alpha_3 * v_3 - beta_2 * v_wide
    basis_ref[2, 0] = (residual * (1.0 / beta_3)).astype(jnp.bfloat16)

    row = lax.broadcasted_iota(jnp.int32, coef_ref.shape, 0)
    column = lax.broadcasted_iota(jnp.int32, coef_ref.shape, 1)
    out = jnp.zeros(coef_ref.shape, jnp.float32)
    pairs = [(lane_of(scal, 0), lane_of(scal, 1)), (alpha_scaled * inverse_scale, beta_2), (alpha_3, beta_3)]
    for step, (a, b) in enumerate(pairs):
        out = jnp.where(column == step, jnp.where(row == 0, a, b), out)
    coef_ref[...] = out


def shards(wavefunction, env_left, env_right, channel_class):
    width = wavefunction.shape[1]
    ring = ("blk", "rep")
    parts = lax.axis_size("mpo")
    blocks = lax.axis_size("blk") * lax.axis_size("rep")
    entries = blocks * width * width
    permutes = routes(blocks)
    places, origins = slot_tables(permutes, blocks)
    slots = 1 + len(permutes)
    channels = channel_class.shape[0]
    psi, left, right = wavefunction[0], env_left[:, 0], env_right[:, 0]
    rows_shape = jax.ShapeDtypeStruct((blocks, 128), jnp.float32)
    scalars = jax.ShapeDtypeStruct((8, 128), jnp.float32)
    wide = jax.ShapeDtypeStruct((width, width), jnp.float32)
    narrow = jax.ShapeDtypeStruct((width, width), jnp.bfloat16)
    share_shape = jax.ShapeDtypeStruct((width // parts, width), jnp.bfloat16)
    lists = [pltpu.SMEM((channels + WIDE,), jnp.int32)] * 2

    def call(kernel, name, outs, args, scratch=(), share=0, limit=4):
        flops = int(4 * channels * share * width**3)
        cost = pl.CostEstimate(flops=flops, bytes_accessed=4 * width * width, transcendentals=0)
        listed = outs if isinstance(outs, tuple) else (outs,)
        first = SMEM if share else VMEM
        return pl.pallas_call(
            kernel,
            out_shape=outs,
            in_specs=[first] + [VMEM] * (len(args) - 1),
            out_specs=tuple(VMEM for _ in listed) if isinstance(outs, tuple) else VMEM,
            scratch_shapes=list(scratch),
            compiler_params=pltpu.CompilerParams(vmem_limit_bytes=limit * MIB),
            cost_estimate=cost,
            name=name,
        )(*args)

    def sources(count):
        return pltpu.VMEM((count + 1, width, width), jnp.bfloat16)

    def own(scaled, block):
        return call(
            functools.partial(own_kernel, scaled, places),
            "own",
            wide,
            (channel_class, left, right, block),
            [sources(1)] + lists,
            0.2,
            16,
        )

    def rest(mine, first, others, block=None, rows=None):
        scaled, passes = block is not None, rows is not None
        outs = (narrow,) + (scalars,) * scaled + (rows_shape,) * passes
        args = [channel_class, left, right, mine] + [block] * scaled + first + others + [rows] * passes
        return call(
            functools.partial(rest_kernel, scaled, passes, len(first), slots, places),
            "rest",
            outs,
            args,
            [pltpu.VMEM((width, width), jnp.float32), sources(slots)] + lists,
            0.4,
            16,
        )

    def shift(block, pairs):
        return lax.ppermute(block, ring, pairs)

    carried = carried_rounds(permutes, blocks)
    rounds = [(ring, pairs) for pairs in carried or []]
    for axis in () if carried else ("rep", "blk"):
        size = lax.axis_size(axis)
        bits = [1 << i for i in range(size.bit_length() - 1)]
        if sum(bits) == size - 1:
            rounds += [(axis, [(i, i ^ bit) for i in range(size)]) for bit in bits]
        else:
            rounds += [(axis, None)]

    def add_round(rows, axis, pairs):
        if pairs is None:
            return lax.psum(rows, axis)
        return rows + lax.ppermute(rows, axis, pairs)

    def spread(block, share, rows=None):
        piece = shift(share, permutes[0])
        if rows is not None and carried:
            piece, rows = call(
                functools.partial(unpack_kernel, origins[1]),
                "unpack",
                (share_shape, rows_shape),
                (piece, rows),
            )
            rows = add_round(rows, *rounds[0])
        elif rows is not None:
            for step in rounds[:-1]:
                rows = add_round(rows, *step)
            piece = call(pass_kernel, "hold", share_shape, (piece, rows))
        if parts == 2:
            first = [piece, lax.ppermute(piece, "mpo", [(0, 1), (1, 0)])]
        else:
            first = [lax.all_gather(piece, "mpo", axis=0, tiled=True)]
        return first, [shift(block, pairs) for pairs in permutes[1:]], rows

    def gather_parts(t):
        if parts == 2:
            return [t, lax.ppermute(t, "mpo", [(0, 1), (1, 0)])]
        held = lax.all_gather(t, "mpo")
        return [held[i] for i in range(parts)]

    def exchange(rows):
        return lax.all_to_all(rows, ring, 0, 0, tiled=True)

    held = [shift(psi, pairs) for pairs in permutes]
    t, unit = rest(own(True, psi), held[:1], held[1:], psi)
    rows_in_share = width // parts + (2 * TILE if carried else 0)
    w_1, share_1, rows = call(
        functools.partial(first_sums_kernel, width // parts),
        "sums",
        (narrow, jax.ShapeDtypeStruct((rows_in_share, width), jnp.bfloat16), rows_shape),
        (*gather_parts(t), psi, unit),
    )
    first, others, rows = spread(w_1, share_1, rows)
    t, unit, rows = rest(own(True, w_1), first, others, w_1, rows)
    rows = add_round(rows, *rounds[-1])
    w_wide, w_2, share_2, v_2, scal = call(
        functools.partial(second_sums_kernel, entries),
        "sums",
        (wide, narrow, share_shape, narrow, scalars),
        (*gather_parts(t), rows, psi, w_1, unit),
    )
    first, others, _ = spread(w_2, share_2)
    (t,) = rest(own(False, w_2), first, others)
    r, z, rows = call(
        third_sums_kernel,
        "sums",
        (wide, wide, rows_shape),
        (*gather_parts(t), psi, w_1, v_2, w_wide, scal),
        limit=8,
    )
    return call(
        functools.partial(final_kernel, entries),
        "final",
        (
            jax.ShapeDtypeStruct((STEPS, 1, width // parts, width), jnp.bfloat16),
            jax.ShapeDtypeStruct((2, STEPS), jnp.float32),
        ),
        (exchange(rows), r, z, w_wide, v_2, scal),
    )


def solution(mesh):
    return jax.shard_map(
        shards,
        mesh=mesh,
        in_specs=(
            P(("groups", "blk", "rep"), None, None),
            P("mpo", ("groups", "blk", "rep"), None, None),
            P("mpo", ("groups", "blk", "rep"), None, None),
            P("mpo"),
        ),
        out_specs=(P(None, ("groups", "blk", "rep"), "mpo", None), P("groups", None)),
        check_vma=False,
    )
```

```python
import functools

import jax
import jax.numpy as jnp
from jax import lax
from jax.experimental import pallas as pl
from jax.experimental.pallas import tpu as pltpu
from jax.sharding import PartitionSpec as P

NS = 4
STEPS = 3
OFFSETS = (0, NS + 1, NS - 1, -(NS + 1), -(NS - 1))
EPSILON = 1e-06
PAD = 12
SMALLEST = 1e-30
TILE = 16
MIB = 1024 * 1024
VMEM = pl.BlockSpec(memory_space=pltpu.VMEM)
SMEM = pl.BlockSpec(memory_space=pltpu.SMEM)


def reaches(kind, sector, blocks):
    source = sector - OFFSETS[kind]
    spin = sector % NS
    inside = (source >= 0) & (source < blocks)
    if kind in (1, 4):
        return inside & (spin >= 1)
    if kind in (2, 3):
        return inside & (spin <= NS - 2)
    return inside


def routes(blocks):
    degree, edges = [0] * blocks, []
    for kind in (1, 2):
        for k in range(blocks):
            if reaches(kind, k, blocks):
                edges.append((k - OFFSETS[kind], k))
                degree[k - OFFSETS[kind]] += 1
                degree[k] += 1
    edges.sort(key=lambda edge: degree[edge[0]] + degree[edge[1]])
    partner = [{} for _ in range(blocks)]

    def lowest(block):
        return next(c for c in range(len(edges)) if c not in partner[block])

    for a, b in edges:
        here_free, there_free = lowest(a), lowest(b)
        if here_free in partner[b]:
            path, block, colour = [b], b, here_free
            while colour in partner[block]:
                block = partner[block][colour]
                path.append(block)
                colour = there_free if colour == here_free else here_free
            for block in path:
                moved = {}
                for old, new in ((here_free, there_free), (there_free, here_free)):
                    if old in partner[block]:
                        moved[new] = partner[block].pop(old)
                partner[block].update(moved)
        partner[a][here_free], partner[b][here_free] = b, a
    colours = sorted({c for held in partner for c in held})
    permutes = [[(held[c], k) for k, held in enumerate(partner) if c in held] for c in colours]
    return sorted(permutes, key=len, reverse=True)


def slot_tables(permutes, blocks):
    origins = [{k: k for k in range(blocks)}] + [{k: s for s, k in pairs} for pairs in permutes]
    places = []
    for kind in range(5):
        place = {}
        for slot, origin in enumerate(origins):
            for k, source in origin.items():
                if source == k - OFFSETS[kind] and reaches(kind, k, blocks):
                    place[k] = slot
        places.append(place)
    return places, origins


def carried_rounds(permutes, blocks):
    if len(permutes) < 2 or blocks % 2:
        return None
    last = dict(permutes[1])
    for k in range(blocks):
        if k not in last:
            last[k] = blocks - 1 - k
    rounds = [dict(permutes[0]), {k: k ^ 1 for k in range(blocks)}, last]
    held = [{k} for k in range(blocks)]
    for pairs in rounds:
        if sorted(pairs.values()) != list(range(blocks)):
            return None
        if any(held[source] & held[k] for source, k in pairs.items()):
            return None
        grown = list(held)
        for source, k in pairs.items():
            grown[k] = held[k] | held[source]
        held = grown
    if any(len(rows) < blocks for rows in held):
        return None
    return [sorted(pairs.items()) for pairs in rounds[1:]]


def look_up(table, sector, default):
    out = jnp.int32(default)
    for k, value in table.items():
        if value != default:
            out = jnp.where(sector == k, jnp.int32(value), out)
    return out


def here():
    return lax.axis_index("blk") * lax.axis_size("rep") + lax.axis_index("rep")


def lane_of(rows, lane):
    return rows[:, lane : lane + 1]


def pack(values, shape):
    lanes = lax.broadcasted_iota(jnp.int32, shape, 1)
    out = jnp.zeros(shape, jnp.float32)
    for place, value in enumerate(values):
        out = jnp.where(lanes == place, value, out)
    return out


def total(x):
    return jnp.sum(jnp.sum(x, axis=0, keepdims=True), axis=1, keepdims=True)


def column_sum(x):
    return jnp.sum(x, axis=0, keepdims=True)


def peak(x):
    return jnp.max(jnp.max(jnp.abs(x), axis=0, keepdims=True), axis=1, keepdims=True)


def wide_float(ref):
    return ref[...].astype(jnp.float32)


def sum_parts(parts):
    w = wide_float(parts[0])
    for part in parts[1:]:
        w += wide_float(part)
    return w


def first_row(ref):
    return ref[0:1, :]


def list_kernel(places, idle, kinds_ref, lists_ref):
    channels = kinds_ref.shape[0]
    sector = here()
    slots = [jnp.int32(0)] + [look_up(places[c], sector, -1) for c in range(1, 5)]
    counts = [jnp.int32(0), jnp.int32(0)]
    for b in range(channels):
        kind = kinds_ref[b]
        slot = slots[0]
        for c in range(1, 5):
            slot = jnp.where(kind == c, slots[c], slot)
        for which in range(2):
            lists_ref[2 * which, counts[which]] = jnp.int32(b)
            lists_ref[2 * which + 1, counts[which]] = slot
        counts[0] += jnp.where(kind == 0, 1, 0)
        counts[1] += jnp.where((kind != 0) & (slot >= 0), 1, 0)
    for which, spare in enumerate((1, idle)):
        for extra in range(PAD):
            lists_ref[2 * which, counts[which] + extra] = jnp.int32(0)
            lists_ref[2 * which + 1, counts[which] + extra] = jnp.int32(spare)
        lists_ref[2 * which, channels + PAD] = counts[which]


def multiply_listed(which, wide, lists_ref, left_ref, right_ref, source, acc):
    count = lists_ref[2 * which, lists_ref.shape[1] - 1]

    def multiply(start, size):
        held = [lists_ref[2 * which, start + inner] for inner in range(size)]
        slots = [lists_ref[2 * which + 1, start + inner] for inner in range(size)]
        pieces = [
            jnp.dot(left_ref[b], source[slot], preferred_element_type=jnp.float32).astype(jnp.bfloat16)
            for b, slot in zip(held, slots)
        ]
        acc[...] += lax.dot_general(
            jnp.concatenate(pieces, axis=1),
            jnp.concatenate([right_ref[b] for b in held], axis=1),
            (((1,), (1,)), ((), ())),
            preferred_element_type=jnp.float32,
        )

    def full(group, carry):
        multiply(group * wide, wide)
        return carry

    smaller = [4, 8] if wide > 8 else [2, 4]
    groups = (count + wide - 1 - smaller[-1]) // wide
    lax.fori_loop(0, groups, full, 0)
    rest = count - groups * wide
    for low, size in zip([0] + smaller, smaller):

        @pl.when((rest > low) & (rest <= size))
        def _():
            multiply(groups * wide, size)


def own_kernel(scaled, lists_ref, left_ref, right_ref, block_ref, acc, source):
    if scaled:
        block = wide_float(block_ref)
        inverse = 1.0 / jnp.maximum(peak(block), SMALLEST)
        source[0] = (block * inverse).astype(jnp.bfloat16)
    else:
        source[0] = block_ref[...]
    source[1] = jnp.zeros(source.shape[1:], jnp.bfloat16)
    acc[...] = jnp.zeros_like(acc)
    multiply_listed(0, 8, lists_ref, left_ref, right_ref, source, acc)


def rest_kernel(scaled, passes, shares, slots, *refs):
    lists_ref, left_ref, right_ref, own_ref = refs[:4]
    refs = refs[4:]
    if scaled:
        block_ref, refs = refs[0], refs[1:]
    first, refs = refs[:shares], refs[shares:]
    others, refs = refs[: slots - 2], refs[slots - 2 :]
    if passes:
        rows_ref, refs = refs[0], refs[1:]
    t_ref, refs = refs[0], refs[1:]
    if scaled:
        unit_ref, refs = refs[0], refs[1:]
    if passes:
        refs[0][...] = rows_ref[...]
        refs = refs[1:]
    acc, source = refs
    if scaled:
        mine = jnp.maximum(peak(wide_float(block_ref)), SMALLEST)
        unit = mine
        for block in (*first, *others):
            unit = jnp.maximum(unit, peak(wide_float(block)))
        unit_ref[...] = jnp.broadcast_to(unit, unit_ref.shape)
        inverse = 1.0 / unit

    def scale(block):
        return (wide_float(block) * inverse).astype(jnp.bfloat16) if scaled else block[...]

    share = source.shape[1] // shares
    for step, block in enumerate(first):
        at = 0 if shares == 1 else jnp.abs(step - lax.axis_index("mpo"))
        source[1, pl.ds(pl.multiple_of(at * share, share), share), :] = scale(block)
    for slot, block in enumerate(others, 2):
        source[slot] = scale(block)
    source[slots] = jnp.zeros(source.shape[1:], jnp.bfloat16)
    acc[...] = own_ref[...] * (mine * inverse) if scaled else own_ref[...]
    multiply_listed(1, PAD, lists_ref, left_ref, right_ref, source, acc)
    t_ref[...] = acc[...].astype(jnp.bfloat16)


def pass_kernel(block_ref, rows_ref, out_ref):
    out_ref[...] = block_ref[...]


def unpack_kernel(origin, block_ref, rows_ref, out_ref, sums_ref):
    share = out_ref.shape[0]
    out_ref[...] = block_ref[0:share, :]
    terms = block_ref[share : share + 2 * TILE, :].astype(jnp.float32)
    sums = terms[0:TILE, 0:128] + terms[0:TILE, 128:256] + terms[TILE : 2 * TILE, 0:128]
    row = lax.broadcasted_iota(jnp.int32, rows_ref.shape, 0)
    source = look_up(origin, here(), 0)
    sums_ref[...] = jnp.where(row == source, first_row(sums), rows_ref[...])


def my_rows(share):
    return pl.ds(pl.multiple_of(lax.axis_index("mpo") * share, share), share)


def first_sums_kernel(share, *refs):
    parts, (psi_ref, unit_ref, w_ref, share_ref, rows_ref) = refs[:-5], refs[-5:]
    w = sum_parts(parts)
    unit = lane_of(first_row(unit_ref), 0)
    w_ref[...] = (w * unit).astype(jnp.bfloat16)
    share_ref[0:share, :] = w_ref[my_rows(share), :]
    v = wide_float(psi_ref) * (1.0 / unit)
    a = total(v * w)
    d = total(v * v)
    local = a / jnp.maximum(d, SMALLEST)
    r = w - local * v
    values = [a, d, local, total(r * v), total(r * r), unit]
    if share_ref.shape[0] > share:
        sums = pack(values, (TILE, 128))
        high = sums.astype(jnp.bfloat16)
        rest = sums - high.astype(jnp.float32)
        middle = rest.astype(jnp.bfloat16)
        low = (rest - middle.astype(jnp.float32)).astype(jnp.bfloat16)
        blank = jnp.zeros((2 * TILE, share_ref.shape[1]), jnp.bfloat16)
        share_ref[share : share + 2 * TILE, :] = blank
        share_ref[share : share + TILE, 0:128] = high
        share_ref[share : share + TILE, 128:256] = middle
        share_ref[share + TILE : share + 2 * TILE, 0:128] = low
        sums = high.astype(jnp.float32) + middle.astype(jnp.float32) + low.astype(jnp.float32)
        sums = jnp.broadcast_to(first_row(sums), rows_ref.shape)
    else:
        sums = pack(values, rows_ref.shape)
    row = lax.broadcasted_iota(jnp.int32, rows_ref.shape, 0)
    rows_ref[...] = jnp.where(row == here(), sums, 0.0)


def shrink(scal):
    return 1.0 / (jnp.abs(lane_of(scal, 0)) + lane_of(scal, 1))


def second_sums_kernel(entries, *refs):
    parts, refs = refs[:-9], refs[-9:]
    rows_ref, psi_ref, first_ref, unit_ref, wide_ref, w_ref, share_ref, v_ref, scal_ref = refs
    rows = rows_ref[...]
    a, d, local, p, q, unit = (lane_of(rows, lane) for lane in range(6))
    beta_0 = jnp.sqrt(column_sum(unit * unit * d) / entries + EPSILON)
    start_inverse = 1.0 / beta_0
    gain = unit * start_inverse
    alpha = column_sum(gain * (gain * a)) / entries
    off = local - alpha
    square = column_sum(gain * (gain * (q + off * (2.0 * p + off * d))))
    beta = jnp.sqrt(jnp.maximum(square, 0.0) / entries + EPSILON)
    inverse = 1.0 / beta
    scal = pack([alpha, beta, start_inverse], scal_ref.shape)
    scal_ref[...] = scal
    image = wide_float(first_ref) * start_inverse
    v_ref[...] = ((image - (alpha * start_inverse) * wide_float(psi_ref)) * inverse).astype(jnp.bfloat16)
    lift = lane_of(first_row(unit_ref), 0) * start_inverse
    w = (sum_parts(parts) * lift - alpha * image) * (inverse * shrink(first_row(scal)))
    wide_ref[...] = w
    w_ref[...] = w.astype(jnp.bfloat16)
    share_ref[...] = w_ref[my_rows(share_ref.shape[0]), :]


def third_sums_kernel(*refs):
    parts, refs = refs[:-8], refs[-8:]
    psi_ref, first_ref, v_ref, w_ref, scal_ref, r_ref, z_ref, rows_ref = refs
    scal = first_row(scal_ref)
    scale = shrink(scal)
    push = scale * lane_of(scal, 1) * lane_of(scal, 2)
    v, w = wide_float(v_ref), w_ref[...]
    vv, vw = total(v * v), total(v * w)
    local = vw / jnp.maximum(vv, SMALLEST)
    r = w - local * v - push * wide_float(psi_ref)
    z = sum_parts(parts) - (local / scale) * w - push * wide_float(first_ref)
    r_ref[...] = r
    z_ref[...] = z
    sums = [total(r * r), total(r * v), total(r * z), total(r * w)]
    sums += [total(z * v), total(z * w), total(z * z), total(w * w)]
    rows_ref[...] = pack([vv, vw, local] + sums, rows_ref.shape)


def final_kernel(entries, rows_ref, r_ref, z_ref, w_ref, v_ref, scal_ref, basis_ref, coef_ref):
    share = basis_ref.shape[2]
    mine = my_rows(share)
    vv, vw, local, rr, rv, rz, rw, zv, zw, zz, ww = (lane_of(rows_ref[...], i) for i in range(11))
    scal = first_row(scal_ref)
    scale = shrink(scal)
    inverse_scale = 1.0 / scale
    alpha_scaled = column_sum(vw) / entries
    off = local - alpha_scaled
    lift = off * inverse_scale
    square = column_sum(rr + off * (2.0 * rv + off * vv)) / entries
    beta_scaled = jnp.sqrt(jnp.maximum(square, 0.0) + scale * scale * EPSILON)
    inverse = 1.0 / beta_scaled
    mixed = column_sum(rz + lift * rw + off * (zv + lift * vw)) / entries
    alpha_3 = mixed * inverse * inverse
    r_v = column_sum(rv + off * vv) / entries
    z_v = column_sum(zv + lift * vw) / entries
    z_z = column_sum(zz + lift * (2.0 * zw + lift * ww)) / entries
    v_v = column_sum(vv) / entries
    beta_2 = beta_scaled * inverse_scale
    third = (z_z - 2.0 * alpha_3 * mixed + alpha_3 * alpha_3 * square) * inverse * inverse
    third += beta_2 * (beta_2 * v_v - 2.0 * inverse * (z_v - alpha_3 * r_v))
    beta_3 = jnp.sqrt(jnp.maximum(third, 0.0) + EPSILON)

    sector = here()
    row_of = lax.broadcasted_iota(jnp.int32, off.shape, 0)
    off_here = column_sum(jnp.where(row_of == sector, off, 0.0))
    v = v_ref[mine, :]
    v_wide = v.astype(jnp.float32)
    v_3 = (r_ref[mine, :] + off_here * v_wide) * inverse
    image = (z_ref[mine, :] + (off_here * inverse_scale) * w_ref[mine, :]) * inverse
    basis_ref[0, 0] = v
    basis_ref[1, 0] = v_3.astype(jnp.bfloat16)
    residual = image - alpha_3 * v_3 - beta_2 * v_wide
    basis_ref[2, 0] = (residual * (1.0 / beta_3)).astype(jnp.bfloat16)

    row = lax.broadcasted_iota(jnp.int32, coef_ref.shape, 0)
    column = lax.broadcasted_iota(jnp.int32, coef_ref.shape, 1)
    out = jnp.zeros(coef_ref.shape, jnp.float32)
    pairs = [(lane_of(scal, 0), lane_of(scal, 1)), (alpha_scaled * inverse_scale, beta_2), (alpha_3, beta_3)]
    for step, (a, b) in enumerate(pairs):
        out = jnp.where(column == step, jnp.where(row == 0, a, b), out)
    coef_ref[...] = out


def shards(wavefunction, env_left, env_right, channel_class):
    width = wavefunction.shape[1]
    ring = ("blk", "rep")
    parts = lax.axis_size("mpo")
    blocks = lax.axis_size("blk") * lax.axis_size("rep")
    entries = blocks * width * width
    permutes = routes(blocks)
    places, origins = slot_tables(permutes, blocks)
    slots = 1 + len(permutes)
    channels = channel_class.shape[0]
    psi, left, right = wavefunction[0], env_left[:, 0], env_right[:, 0]
    rows_shape = jax.ShapeDtypeStruct((blocks, 128), jnp.float32)
    scalars = jax.ShapeDtypeStruct((8, 128), jnp.float32)
    wide = jax.ShapeDtypeStruct((width, width), jnp.float32)
    narrow = jax.ShapeDtypeStruct((width, width), jnp.bfloat16)
    share_shape = jax.ShapeDtypeStruct((width // parts, width), jnp.bfloat16)
    lists = pl.pallas_call(
        functools.partial(list_kernel, places, slots),
        out_shape=jax.ShapeDtypeStruct((4, channels + PAD + 1), jnp.int32),
        in_specs=[SMEM],
        out_specs=SMEM,
        compiler_params=pltpu.CompilerParams(vmem_limit_bytes=4 * MIB),
        name="list",
    )(channel_class)

    def call(kernel, name, outs, args, scratch=(), share=0, limit=4):
        flops = int(4 * channels * share * width**3)
        cost = pl.CostEstimate(flops=flops, bytes_accessed=4 * width * width, transcendentals=0)
        listed = outs if isinstance(outs, tuple) else (outs,)
        first = SMEM if share else VMEM
        return pl.pallas_call(
            kernel,
            out_shape=outs,
            in_specs=[first] + [VMEM] * (len(args) - 1),
            out_specs=tuple(VMEM for _ in listed) if isinstance(outs, tuple) else VMEM,
            scratch_shapes=list(scratch),
            compiler_params=pltpu.CompilerParams(vmem_limit_bytes=limit * MIB),
            cost_estimate=cost,
            name=name,
        )(*args)

    def sources(count):
        return pltpu.VMEM((count + 1, width, width), jnp.bfloat16)

    def own(scaled, block):
        return call(
            functools.partial(own_kernel, scaled),
            "own",
            wide,
            (lists, left, right, block),
            [sources(1)],
            0.2,
            16,
        )

    def rest(mine, first, others, block=None, rows=None):
        scaled, passes = block is not None, rows is not None
        outs = (narrow,) + (scalars,) * scaled + (rows_shape,) * passes
        args = [lists, left, right, mine] + [block] * scaled + first + others + [rows] * passes
        return call(
            functools.partial(rest_kernel, scaled, passes, len(first), slots),
            "rest",
            outs,
            args,
            [pltpu.VMEM((width, width), jnp.float32), sources(slots)],
            0.4,
            16,
        )

    def shift(block, pairs):
        return lax.ppermute(block, ring, pairs)

    carried = carried_rounds(permutes, blocks)
    rounds = [(ring, pairs) for pairs in carried or []]
    for axis in () if carried else ("rep", "blk"):
        size = lax.axis_size(axis)
        bits = [1 << i for i in range(size.bit_length() - 1)]
        if sum(bits) == size - 1:
            rounds += [(axis, [(i, i ^ bit) for i in range(size)]) for bit in bits]
        else:
            rounds += [(axis, None)]

    def add_round(rows, axis, pairs):
        if pairs is None:
            return lax.psum(rows, axis)
        return rows + lax.ppermute(rows, axis, pairs)

    def spread(block, share, rows=None):
        piece = shift(share, permutes[0])
        if rows is not None and carried:
            piece, rows = call(
                functools.partial(unpack_kernel, origins[1]),
                "unpack",
                (share_shape, rows_shape),
                (piece, rows),
            )
            rows = add_round(rows, *rounds[0])
        elif rows is not None:
            for step in rounds[:-1]:
                rows = add_round(rows, *step)
            piece = call(pass_kernel, "hold", share_shape, (piece, rows))
        if parts == 2:
            first = [piece, lax.ppermute(piece, "mpo", [(0, 1), (1, 0)])]
        else:
            first = [lax.all_gather(piece, "mpo", axis=0, tiled=True)]
        return first, [shift(block, pairs) for pairs in permutes[1:]], rows

    def gather_parts(t):
        if parts == 2:
            return [t, lax.ppermute(t, "mpo", [(0, 1), (1, 0)])]
        held = lax.all_gather(t, "mpo")
        return [held[i] for i in range(parts)]

    def exchange(rows):
        return lax.all_to_all(rows, ring, 0, 0, tiled=True)

    held = [shift(psi, pairs) for pairs in permutes]
    t, unit = rest(own(True, psi), held[:1], held[1:], psi)
    rows_in_share = width // parts + (2 * TILE if carried else 0)
    w_1, share_1, rows = call(
        functools.partial(first_sums_kernel, width // parts),
        "sums",
        (narrow, jax.ShapeDtypeStruct((rows_in_share, width), jnp.bfloat16), rows_shape),
        (*gather_parts(t), psi, unit),
    )
    first, others, rows = spread(w_1, share_1, rows)
    t, unit, rows = rest(own(True, w_1), first, others, w_1, rows)
    rows = add_round(rows, *rounds[-1])
    w_wide, w_2, share_2, v_2, scal = call(
        functools.partial(second_sums_kernel, entries),
        "sums",
        (wide, narrow, share_shape, narrow, scalars),
        (*gather_parts(t), rows, psi, w_1, unit),
    )
    first, others, _ = spread(w_2, share_2)
    (t,) = rest(own(False, w_2), first, others)
    r, z, rows = call(
        third_sums_kernel,
        "sums",
        (wide, wide, rows_shape),
        (*gather_parts(t), psi, w_1, v_2, w_wide, scal),
        limit=8,
    )
    return call(
        functools.partial(final_kernel, entries),
        "final",
        (
            jax.ShapeDtypeStruct((STEPS, 1, width // parts, width), jnp.bfloat16),
            jax.ShapeDtypeStruct((2, STEPS), jnp.float32),
        ),
        (exchange(rows), r, z, w_wide, v_2, scal),
    )


def solution(mesh):
    return jax.shard_map(
        shards,
        mesh=mesh,
        in_specs=(
            P(("groups", "blk", "rep"), None, None),
            P("mpo", ("groups", "blk", "rep"), None, None),
            P("mpo", ("groups", "blk", "rep"), None, None),
            P("mpo"),
        ),
        out_specs=(P(None, ("groups", "blk", "rep"), "mpo", None), P("groups", None)),
        check_vma=False,
    )
```

```python
import functools

import jax
import jax.numpy as jnp
from jax import lax
from jax.experimental import pallas as pl
from jax.experimental.pallas import tpu as pltpu
from jax.sharding import PartitionSpec as P

NS = 4
STEPS = 3
OFFSETS = (0, NS + 1, NS - 1, -(NS + 1), -(NS - 1))
EPSILON = 1e-06
WIDE = 8
SMALLEST = 1e-30
TILE = 16
MIB = 1024 * 1024
VMEM = pl.BlockSpec(memory_space=pltpu.VMEM)
SMEM = pl.BlockSpec(memory_space=pltpu.SMEM)


def reaches(kind, sector, blocks):
    source = sector - OFFSETS[kind]
    spin = sector % NS
    inside = (source >= 0) & (source < blocks)
    if kind in (1, 4):
        return inside & (spin >= 1)
    if kind in (2, 3):
        return inside & (spin <= NS - 2)
    return inside


def routes(blocks):
    degree, edges = [0] * blocks, []
    for kind in (1, 2):
        for k in range(blocks):
            if reaches(kind, k, blocks):
                edges.append((k - OFFSETS[kind], k))
                degree[k - OFFSETS[kind]] += 1
                degree[k] += 1
    edges.sort(key=lambda edge: degree[edge[0]] + degree[edge[1]])
    partner = [{} for _ in range(blocks)]

    def lowest(block):
        return next(c for c in range(len(edges)) if c not in partner[block])

    for a, b in edges:
        here_free, there_free = lowest(a), lowest(b)
        if here_free in partner[b]:
            path, block, colour = [b], b, here_free
            while colour in partner[block]:
                block = partner[block][colour]
                path.append(block)
                colour = there_free if colour == here_free else here_free
            for block in path:
                moved = {}
                for old, new in ((here_free, there_free), (there_free, here_free)):
                    if old in partner[block]:
                        moved[new] = partner[block].pop(old)
                partner[block].update(moved)
        partner[a][here_free], partner[b][here_free] = b, a
    colours = sorted({c for held in partner for c in held})
    permutes = [[(held[c], k) for k, held in enumerate(partner) if c in held] for c in colours]
    return sorted(permutes, key=len, reverse=True)


def slot_tables(permutes, blocks):
    origins = [{k: k for k in range(blocks)}] + [{k: s for s, k in pairs} for pairs in permutes]
    places = []
    for kind in range(5):
        place = {}
        for slot, origin in enumerate(origins):
            for k, source in origin.items():
                if source == k - OFFSETS[kind] and reaches(kind, k, blocks):
                    place[k] = slot
        places.append(place)
    return places, origins


def carried_rounds(permutes, blocks):
    if not permutes or blocks % 4:
        return None
    rounds = [dict(permutes[0])] + [{k: k ^ bit for k in range(blocks)} for bit in (1, 2)]
    held = [{k} for k in range(blocks)]
    for pairs in rounds:
        if sorted(pairs.values()) != list(range(blocks)):
            return None
        if any(held[source] & held[k] for source, k in pairs.items()):
            return None
        grown = list(held)
        for source, k in pairs.items():
            grown[k] = held[k] | held[source]
        held = grown
    if any(len(rows) < blocks for rows in held):
        return None
    return [sorted(pairs.items()) for pairs in rounds[1:]]


def look_up(table, sector, default):
    out = jnp.int32(default)
    for k, value in table.items():
        if value != default:
            out = jnp.where(sector == k, jnp.int32(value), out)
    return out


def here():
    return lax.axis_index("blk") * lax.axis_size("rep") + lax.axis_index("rep")


def lane_of(rows, lane):
    return rows[:, lane : lane + 1]


def pack(values, shape):
    lanes = lax.broadcasted_iota(jnp.int32, shape, 1)
    out = jnp.zeros(shape, jnp.float32)
    for place, value in enumerate(values):
        out = jnp.where(lanes == place, value, out)
    return out


def total(x):
    return jnp.sum(jnp.sum(x, axis=0, keepdims=True), axis=1, keepdims=True)


def column_sum(x):
    return jnp.sum(x, axis=0, keepdims=True)


def peak(x):
    return jnp.max(jnp.max(jnp.abs(x), axis=0, keepdims=True), axis=1, keepdims=True)


def wide_float(ref):
    return ref[...].astype(jnp.float32)


def sum_parts(parts):
    w = wide_float(parts[0])
    for part in parts[1:]:
        w += wide_float(part)
    return w


def first_row(ref):
    return ref[0:1, :]


def list_channels(which, places, kinds_ref, order, slot_of, idle):
    sector = here()
    slots = [jnp.int32(-1 if which == "rest" else 0)]
    slots += [look_up(places[c], sector, -1) if which != "own" else jnp.int32(-1) for c in range(1, 5)]
    count = jnp.int32(0)
    for b in range(kinds_ref.shape[0]):
        kind = kinds_ref[b]
        slot = slots[0]
        for c in range(1, 5):
            slot = jnp.where(kind == c, slots[c], slot)
        order[count] = jnp.int32(b)
        slot_of[count] = slot
        count += jnp.where(slot >= 0, 1, 0)
    for extra in range(WIDE):
        order[count + extra] = jnp.int32(0)
        slot_of[count + extra] = jnp.int32(idle)
    return count


def multiply_listed(count, left_ref, right_ref, source, acc, order, slot_of):
    def multiply(start, wide):
        held = [order[start + inner] for inner in range(wide)]
        pieces = [
            jnp.dot(
                left_ref[b], source[slot_of[start + inner]], preferred_element_type=jnp.float32
            ).astype(jnp.bfloat16)
            for inner, b in enumerate(held)
        ]
        acc[...] += lax.dot_general(
            jnp.concatenate(pieces, axis=1),
            jnp.concatenate([right_ref[b] for b in held], axis=1),
            (((1,), (1,)), ((), ())),
            preferred_element_type=jnp.float32,
        )

    def full(group, carry):
        multiply(group * WIDE, WIDE)
        return carry

    groups = (count + WIDE // 2 - 1) // WIDE
    lax.fori_loop(0, groups, full, 0)
    rest = count - groups * WIDE
    for low, wide in ((0, 2), (2, 4)):

        @pl.when((rest > low) & (rest <= wide))
        def _():
            multiply(groups * WIDE, wide)


def own_kernel(scaled, places, kinds_ref, left_ref, right_ref, block_ref, acc, source, order, slot_of):
    count = list_channels("own", places, kinds_ref, order, slot_of, 1)
    if scaled:
        block = wide_float(block_ref)
        inverse = 1.0 / jnp.maximum(peak(block), SMALLEST)
        source[0] = (block * inverse).astype(jnp.bfloat16)
    else:
        source[0] = block_ref[...]
    source[1] = jnp.zeros(source.shape[1:], jnp.bfloat16)
    acc[...] = jnp.zeros_like(acc)
    multiply_listed(count, left_ref, right_ref, source, acc, order, slot_of)


def rest_kernel(scaled, passes, shares, slots, places, *refs):
    kinds_ref, left_ref, right_ref, own_ref = refs[:4]
    refs = refs[4:]
    if scaled:
        block_ref, refs = refs[0], refs[1:]
    first, refs = refs[:shares], refs[shares:]
    others, refs = refs[: slots - 2], refs[slots - 2 :]
    if passes:
        rows_ref, refs = refs[0], refs[1:]
    t_ref, refs = refs[0], refs[1:]
    if scaled:
        unit_ref, refs = refs[0], refs[1:]
    if passes:
        refs[0][...] = rows_ref[...]
        refs = refs[1:]
    acc, source, order, slot_of = refs
    count = list_channels("rest", places, kinds_ref, order, slot_of, slots)
    if scaled:
        mine = jnp.maximum(peak(wide_float(block_ref)), SMALLEST)
        unit = mine
        for block in (*first, *others):
            unit = jnp.maximum(unit, peak(wide_float(block)))
        unit_ref[...] = jnp.broadcast_to(unit, unit_ref.shape)
        inverse = 1.0 / unit

    def scale(block):
        return (wide_float(block) * inverse).astype(jnp.bfloat16) if scaled else block[...]

    share = source.shape[1] // shares
    for step, block in enumerate(first):
        at = 0 if shares == 1 else jnp.abs(step - lax.axis_index("mpo"))
        source[1, pl.ds(pl.multiple_of(at * share, share), share), :] = scale(block)
    for slot, block in enumerate(others, 2):
        source[slot] = scale(block)
    source[slots] = jnp.zeros(source.shape[1:], jnp.bfloat16)
    acc[...] = own_ref[...] * (mine * inverse) if scaled else own_ref[...]
    multiply_listed(count, left_ref, right_ref, source, acc, order, slot_of)
    t_ref[...] = acc[...].astype(jnp.bfloat16)


def pass_kernel(block_ref, rows_ref, out_ref):
    out_ref[...] = block_ref[...]


def unpack_kernel(origin, block_ref, rows_ref, out_ref, sums_ref):
    share = out_ref.shape[0]
    out_ref[...] = block_ref[0:share, :]
    terms = block_ref[share : share + 2 * TILE, :].astype(jnp.float32)
    sums = terms[0:TILE, 0:128] + terms[0:TILE, 128:256] + terms[TILE : 2 * TILE, 0:128]
    row = lax.broadcasted_iota(jnp.int32, rows_ref.shape, 0)
    source = look_up(origin, here(), 0)
    sums_ref[...] = jnp.where(row == source, first_row(sums), rows_ref[...])


def my_rows(share):
    return pl.ds(pl.multiple_of(lax.axis_index("mpo") * share, share), share)


def first_sums_kernel(share, *refs):
    parts, (psi_ref, unit_ref, w_ref, share_ref, rows_ref) = refs[:-5], refs[-5:]
    w = sum_parts(parts)
    unit = lane_of(first_row(unit_ref), 0)
    w_ref[...] = (w * unit).astype(jnp.bfloat16)
    share_ref[0:share, :] = w_ref[my_rows(share), :]
    v = wide_float(psi_ref) * (1.0 / unit)
    a = total(v * w)
    d = total(v * v)
    local = a / jnp.maximum(d, SMALLEST)
    r = w - local * v
    values = [a, d, local, total(r * v), total(r * r), unit]
    if share_ref.shape[0] > share:
        sums = pack(values, (TILE, 128))
        high = sums.astype(jnp.bfloat16)
        rest = sums - high.astype(jnp.float32)
        middle = rest.astype(jnp.bfloat16)
        low = (rest - middle.astype(jnp.float32)).astype(jnp.bfloat16)
        blank = jnp.zeros((2 * TILE, share_ref.shape[1]), jnp.bfloat16)
        share_ref[share : share + 2 * TILE, :] = blank
        share_ref[share : share + TILE, 0:128] = high
        share_ref[share : share + TILE, 128:256] = middle
        share_ref[share + TILE : share + 2 * TILE, 0:128] = low
        sums = high.astype(jnp.float32) + middle.astype(jnp.float32) + low.astype(jnp.float32)
        sums = jnp.broadcast_to(first_row(sums), rows_ref.shape)
    else:
        sums = pack(values, rows_ref.shape)
    row = lax.broadcasted_iota(jnp.int32, rows_ref.shape, 0)
    rows_ref[...] = jnp.where(row == here(), sums, 0.0)


def shrink(scal):
    return 1.0 / (jnp.abs(lane_of(scal, 0)) + lane_of(scal, 1))


def second_sums_kernel(entries, *refs):
    parts, refs = refs[:-9], refs[-9:]
    rows_ref, psi_ref, first_ref, unit_ref, wide_ref, w_ref, share_ref, v_ref, scal_ref = refs
    rows = rows_ref[...]
    a, d, local, p, q, unit = (lane_of(rows, lane) for lane in range(6))
    beta_0 = jnp.sqrt(column_sum(unit * unit * d) / entries + EPSILON)
    start_inverse = 1.0 / beta_0
    gain = unit * start_inverse
    alpha = column_sum(gain * (gain * a)) / entries
    off = local - alpha
    square = column_sum(gain * (gain * (q + off * (2.0 * p + off * d))))
    beta = jnp.sqrt(jnp.maximum(square, 0.0) / entries + EPSILON)
    inverse = 1.0 / beta
    scal = pack([alpha, beta, start_inverse], scal_ref.shape)
    scal_ref[...] = scal
    image = wide_float(first_ref) * start_inverse
    v_ref[...] = ((image - (alpha * start_inverse) * wide_float(psi_ref)) * inverse).astype(jnp.bfloat16)
    lift = lane_of(first_row(unit_ref), 0) * start_inverse
    w = (sum_parts(parts) * lift - alpha * image) * (inverse * shrink(first_row(scal)))
    wide_ref[...] = w
    w_ref[...] = w.astype(jnp.bfloat16)
    share_ref[...] = w_ref[my_rows(share_ref.shape[0]), :]


def third_sums_kernel(*refs):
    parts, refs = refs[:-8], refs[-8:]
    psi_ref, first_ref, v_ref, w_ref, scal_ref, r_ref, z_ref, rows_ref = refs
    scal = first_row(scal_ref)
    scale = shrink(scal)
    push = scale * lane_of(scal, 1) * lane_of(scal, 2)
    v, w = wide_float(v_ref), w_ref[...]
    vv, vw = total(v * v), total(v * w)
    local = vw / jnp.maximum(vv, SMALLEST)
    r = w - local * v - push * wide_float(psi_ref)
    z = sum_parts(parts) - (local / scale) * w - push * wide_float(first_ref)
    r_ref[...] = r
    z_ref[...] = z
    sums = [total(r * r), total(r * v), total(r * z), total(r * w)]
    sums += [total(z * v), total(z * w), total(z * z), total(w * w)]
    rows_ref[...] = pack([vv, vw, local] + sums, rows_ref.shape)


def final_kernel(entries, rows_ref, r_ref, z_ref, w_ref, v_ref, scal_ref, basis_ref, coef_ref):
    share = basis_ref.shape[2]
    mine = my_rows(share)
    vv, vw, local, rr, rv, rz, rw, zv, zw, zz, ww = (lane_of(rows_ref[...], i) for i in range(11))
    scal = first_row(scal_ref)
    scale = shrink(scal)
    inverse_scale = 1.0 / scale
    alpha_scaled = column_sum(vw) / entries
    off = local - alpha_scaled
    lift = off * inverse_scale
    square = column_sum(rr + off * (2.0 * rv + off * vv)) / entries
    beta_scaled = jnp.sqrt(jnp.maximum(square, 0.0) + scale * scale * EPSILON)
    inverse = 1.0 / beta_scaled
    mixed = column_sum(rz + lift * rw + off * (zv + lift * vw)) / entries
    alpha_3 = mixed * inverse * inverse
    r_v = column_sum(rv + off * vv) / entries
    z_v = column_sum(zv + lift * vw) / entries
    z_z = column_sum(zz + lift * (2.0 * zw + lift * ww)) / entries
    v_v = column_sum(vv) / entries
    beta_2 = beta_scaled * inverse_scale
    third = (z_z - 2.0 * alpha_3 * mixed + alpha_3 * alpha_3 * square) * inverse * inverse
    third += beta_2 * (beta_2 * v_v - 2.0 * inverse * (z_v - alpha_3 * r_v))
    beta_3 = jnp.sqrt(jnp.maximum(third, 0.0) + EPSILON)

    sector = here()
    row_of = lax.broadcasted_iota(jnp.int32, off.shape, 0)
    off_here = column_sum(jnp.where(row_of == sector, off, 0.0))
    v = v_ref[mine, :]
    v_wide = v.astype(jnp.float32)
    v_3 = (r_ref[mine, :] + off_here * v_wide) * inverse
    image = (z_ref[mine, :] + (off_here * inverse_scale) * w_ref[mine, :]) * inverse
    basis_ref[0, 0] = v
    basis_ref[1, 0] = v_3.astype(jnp.bfloat16)
    residual = image - alpha_3 * v_3 - beta_2 * v_wide
    basis_ref[2, 0] = (residual * (1.0 / beta_3)).astype(jnp.bfloat16)

    row = lax.broadcasted_iota(jnp.int32, coef_ref.shape, 0)
    column = lax.broadcasted_iota(jnp.int32, coef_ref.shape, 1)
    out = jnp.zeros(coef_ref.shape, jnp.float32)
    pairs = [(lane_of(scal, 0), lane_of(scal, 1)), (alpha_scaled * inverse_scale, beta_2), (alpha_3, beta_3)]
    for step, (a, b) in enumerate(pairs):
        out = jnp.where(column == step, jnp.where(row == 0, a, b), out)
    coef_ref[...] = out


def shards(wavefunction, env_left, env_right, channel_class):
    width = wavefunction.shape[1]
    ring = ("blk", "rep")
    parts = lax.axis_size("mpo")
    blocks = lax.axis_size("blk") * lax.axis_size("rep")
    entries = blocks * width * width
    permutes = routes(blocks)
    places, origins = slot_tables(permutes, blocks)
    slots = 1 + len(permutes)
    channels = channel_class.shape[0]
    psi, left, right = wavefunction[0], env_left[:, 0], env_right[:, 0]
    rows_shape = jax.ShapeDtypeStruct((blocks, 128), jnp.float32)
    scalars = jax.ShapeDtypeStruct((8, 128), jnp.float32)
    wide = jax.ShapeDtypeStruct((width, width), jnp.float32)
    narrow = jax.ShapeDtypeStruct((width, width), jnp.bfloat16)
    share_shape = jax.ShapeDtypeStruct((width // parts, width), jnp.bfloat16)
    lists = [pltpu.SMEM((channels + WIDE,), jnp.int32)] * 2

    def call(kernel, name, outs, args, scratch=(), share=0, limit=4):
        flops = int(4 * channels * share * width**3)
        cost = pl.CostEstimate(flops=flops, bytes_accessed=4 * width * width, transcendentals=0)
        listed = outs if isinstance(outs, tuple) else (outs,)
        first = SMEM if share else VMEM
        return pl.pallas_call(
            kernel,
            out_shape=outs,
            in_specs=[first] + [VMEM] * (len(args) - 1),
            out_specs=tuple(VMEM for _ in listed) if isinstance(outs, tuple) else VMEM,
            scratch_shapes=list(scratch),
            compiler_params=pltpu.CompilerParams(vmem_limit_bytes=limit * MIB),
            cost_estimate=cost,
            name=name,
        )(*args)

    def sources(count):
        return pltpu.VMEM((count + 1, width, width), jnp.bfloat16)

    def own(scaled, block):
        return call(
            functools.partial(own_kernel, scaled, places),
            "own",
            wide,
            (channel_class, left, right, block),
            [sources(1)] + lists,
            0.2,
            16,
        )

    def rest(mine, first, others, block=None, rows=None):
        scaled, passes = block is not None, rows is not None
        outs = (narrow,) + (scalars,) * scaled + (rows_shape,) * passes
        args = [channel_class, left, right, mine] + [block] * scaled + first + others + [rows] * passes
        return call(
            functools.partial(rest_kernel, scaled, passes, len(first), slots, places),
            "rest",
            outs,
            args,
            [pltpu.VMEM((width, width), jnp.float32), sources(slots)] + lists,
            0.4,
            16,
        )

    def shift(block, pairs):
        return lax.ppermute(block, ring, pairs)

    carried = carried_rounds(permutes, blocks)
    rounds = [(ring, pairs) for pairs in carried or []]
    for axis in () if carried else ("rep", "blk"):
        size = lax.axis_size(axis)
        bits = [1 << i for i in range(size.bit_length() - 1)]
        if sum(bits) == size - 1:
            rounds += [(axis, [(i, i ^ bit) for i in range(size)]) for bit in bits]
        else:
            rounds += [(axis, None)]

    def add_round(rows, axis, pairs):
        if pairs is None:
            return lax.psum(rows, axis)
        return rows + lax.ppermute(rows, axis, pairs)

    def spread(block, share, rows=None):
        piece = shift(share, permutes[0])
        if rows is not None and carried:
            piece, rows = call(
                functools.partial(unpack_kernel, origins[1]),
                "unpack",
                (share_shape, rows_shape),
                (piece, rows),
            )
            rows = add_round(rows, *rounds[0])
        elif rows is not None:
            for step in rounds[:-1]:
                rows = add_round(rows, *step)
            piece = call(pass_kernel, "hold", share_shape, (piece, rows))
        if parts == 2:
            first = [piece, lax.ppermute(piece, "mpo", [(0, 1), (1, 0)])]
        else:
            first = [lax.all_gather(piece, "mpo", axis=0, tiled=True)]
        return first, [shift(block, pairs) for pairs in permutes[1:]], rows

    def gather_parts(t):
        if parts == 2:
            return [t, lax.ppermute(t, "mpo", [(0, 1), (1, 0)])]
        held = lax.all_gather(t, "mpo")
        return [held[i] for i in range(parts)]

    def exchange(rows):
        return lax.all_to_all(rows, ring, 0, 0, tiled=True)

    held = [shift(psi, pairs) for pairs in permutes]
    t, unit = rest(own(True, psi), held[:1], held[1:], psi)
    rows_in_share = width // parts + (2 * TILE if carried else 0)
    w_1, share_1, rows = call(
        functools.partial(first_sums_kernel, width // parts),
        "sums",
        (narrow, jax.ShapeDtypeStruct((rows_in_share, width), jnp.bfloat16), rows_shape),
        (*gather_parts(t), psi, unit),
    )
    first, others, rows = spread(w_1, share_1, rows)
    t, unit, rows = rest(own(True, w_1), first, others, w_1, rows)
    rows = add_round(rows, *rounds[-1])
    w_wide, w_2, share_2, v_2, scal = call(
        functools.partial(second_sums_kernel, entries),
        "sums",
        (wide, narrow, share_shape, narrow, scalars),
        (*gather_parts(t), rows, psi, w_1, unit),
    )
    first, others, _ = spread(w_2, share_2)
    (t,) = rest(own(False, w_2), first, others)
    r, z, rows = call(
        third_sums_kernel,
        "sums",
        (wide, wide, rows_shape),
        (*gather_parts(t), psi, w_1, v_2, w_wide, scal),
        limit=8,
    )
    return call(
        functools.partial(final_kernel, entries),
        "final",
        (
            jax.ShapeDtypeStruct((STEPS, 1, width // parts, width), jnp.bfloat16),
            jax.ShapeDtypeStruct((2, STEPS), jnp.float32),
        ),
        (exchange(rows), r, z, w_wide, v_2, scal),
    )


def solution(mesh):
    return jax.shard_map(
        shards,
        mesh=mesh,
        in_specs=(
            P(("groups", "blk", "rep"), None, None),
            P("mpo", ("groups", "blk", "rep"), None, None),
            P("mpo", ("groups", "blk", "rep"), None, None),
            P("mpo"),
        ),
        out_specs=(P(None, ("groups", "blk", "rep"), "mpo", None), P("groups", None)),
        check_vma=False,
    )
```

```python
import functools

import jax
import jax.numpy as jnp
from jax import lax
from jax.experimental import pallas as pl
from jax.experimental.pallas import tpu as pltpu
from jax.sharding import PartitionSpec as P

NS = 4
STEPS = 3
OFFSETS = (0, NS + 1, NS - 1, -(NS + 1), -(NS - 1))
EPSILON = 1e-06
WIDE = 8
SMALLEST = 1e-30
TILE = 16
LOADS = 4
MIB = 1024 * 1024
VMEM = pl.BlockSpec(memory_space=pltpu.VMEM)
SMEM = pl.BlockSpec(memory_space=pltpu.SMEM)


def reaches(kind, sector, blocks):
    source = sector - OFFSETS[kind]
    spin = sector % NS
    inside = (source >= 0) & (source < blocks)
    if kind in (1, 4):
        return inside & (spin >= 1)
    if kind in (2, 3):
        return inside & (spin <= NS - 2)
    return inside


def routes(blocks):
    degree, edges = [0] * blocks, []
    for kind in (1, 2):
        for k in range(blocks):
            if reaches(kind, k, blocks):
                edges.append((k - OFFSETS[kind], k))
                degree[k - OFFSETS[kind]] += 1
                degree[k] += 1
    edges.sort(key=lambda edge: degree[edge[0]] + degree[edge[1]])
    partner = [{} for _ in range(blocks)]

    def lowest(block):
        return next(c for c in range(len(edges)) if c not in partner[block])

    for a, b in edges:
        here_free, there_free = lowest(a), lowest(b)
        if here_free in partner[b]:
            path, block, colour = [b], b, here_free
            while colour in partner[block]:
                block = partner[block][colour]
                path.append(block)
                colour = there_free if colour == here_free else here_free
            for block in path:
                moved = {}
                for old, new in ((here_free, there_free), (there_free, here_free)):
                    if old in partner[block]:
                        moved[new] = partner[block].pop(old)
                partner[block].update(moved)
        partner[a][here_free], partner[b][here_free] = b, a
    colours = sorted({c for held in partner for c in held})
    permutes = [[(held[c], k) for k, held in enumerate(partner) if c in held] for c in colours]
    return sorted(permutes, key=len, reverse=True)


def slot_tables(permutes, blocks):
    origins = [{k: k for k in range(blocks)}] + [{k: s for s, k in pairs} for pairs in permutes]
    places = []
    for kind in range(5):
        place = {}
        for slot, origin in enumerate(origins):
            for k, source in origin.items():
                if source == k - OFFSETS[kind] and reaches(kind, k, blocks):
                    place[k] = slot
        places.append(place)
    return places, origins


def carried_rounds(permutes, blocks):
    if not permutes or blocks % 4:
        return None
    rounds = [dict(permutes[0])] + [{k: k ^ bit for k in range(blocks)} for bit in (1, 2)]
    held = [{k} for k in range(blocks)]
    for pairs in rounds:
        if sorted(pairs.values()) != list(range(blocks)):
            return None
        if any(held[source] & held[k] for source, k in pairs.items()):
            return None
        grown = list(held)
        for source, k in pairs.items():
            grown[k] = held[k] | held[source]
        held = grown
    if any(len(rows) < blocks for rows in held):
        return None
    return [sorted(pairs.items()) for pairs in rounds[1:]]


def look_up(table, sector, default):
    out = jnp.int32(default)
    for k, value in table.items():
        if value != default:
            out = jnp.where(sector == k, jnp.int32(value), out)
    return out


def here():
    return lax.axis_index("blk") * lax.axis_size("rep") + lax.axis_index("rep")


def lane_of(rows, lane):
    return rows[:, lane : lane + 1]


def pack(values, shape):
    lanes = lax.broadcasted_iota(jnp.int32, shape, 1)
    out = jnp.zeros(shape, jnp.float32)
    for place, value in enumerate(values):
        out = jnp.where(lanes == place, value, out)
    return out


def total(x):
    return jnp.sum(jnp.sum(x, axis=0, keepdims=True), axis=1, keepdims=True)


def column_sum(x):
    return jnp.sum(x, axis=0, keepdims=True)


def peak(x):
    return jnp.max(jnp.max(jnp.abs(x), axis=0, keepdims=True), axis=1, keepdims=True)


def wide_float(ref):
    return ref[...].astype(jnp.float32)


def sum_parts(parts):
    w = wide_float(parts[0])
    for part in parts[1:]:
        w += wide_float(part)
    return w


def first_row(ref):
    return ref[0:1, :]


def list_channels(which, places, kinds_ref, order, slot_of, idle):
    sector = here()
    slots = [jnp.int32(-1 if which == "rest" else 0)]
    slots += [look_up(places[c], sector, -1) if which != "own" else jnp.int32(-1) for c in range(1, 5)]
    count = jnp.int32(0)
    for b in range(kinds_ref.shape[0]):
        kind = kinds_ref[b]
        slot = slots[0]
        for c in range(1, 5):
            slot = jnp.where(kind == c, slots[c], slot)
        order[count] = jnp.int32(b)
        slot_of[count] = slot
        count += jnp.where(slot >= 0, 1, 0)
    for extra in range(WIDE):
        order[count + extra] = jnp.int32(0)
        slot_of[count + extra] = jnp.int32(idle)
    return count


def multiply_listed(count, left_ref, right_ref, source, acc, order, slot_of):
    def multiply(start, wide):
        held = [order[start + inner] for inner in range(wide)]
        pieces = [
            jnp.dot(
                left_ref[b], source[slot_of[start + inner]], preferred_element_type=jnp.float32
            ).astype(jnp.bfloat16)
            for inner, b in enumerate(held)
        ]
        acc[...] += lax.dot_general(
            jnp.concatenate(pieces, axis=1),
            jnp.concatenate([right_ref[b] for b in held], axis=1),
            (((1,), (1,)), ((), ())),
            preferred_element_type=jnp.float32,
        )

    def full(group, carry):
        multiply(group * WIDE, WIDE)
        return carry

    groups = (count + WIDE // 2 - 1) // WIDE
    lax.fori_loop(0, groups, full, 0)
    rest = count - groups * WIDE
    for low, wide in ((0, 2), (2, 4)):

        @pl.when((rest > low) & (rest <= wide))
        def _():
            multiply(groups * WIDE, wide)


def load_kernel(left_hbm, right_hbm, left_ref, right_ref, sems):
    channels = left_ref.shape[0]
    step = max(1, channels // LOADS)
    copies = []
    for side, (source, target) in enumerate(((left_hbm, left_ref), (right_hbm, right_ref))):
        for at, low in enumerate(range(0, channels, step)):
            part = pl.ds(low, min(step, channels - low))
            copies.append(pltpu.make_async_copy(source.at[part], target.at[part], sems.at[side, at]))
    for copy in copies:
        copy.start()
    for copy in copies:
        copy.wait()


def own_kernel(scaled, places, kinds_ref, left_ref, right_ref, block_ref, acc, source, order, slot_of):
    count = list_channels("own", places, kinds_ref, order, slot_of, 1)
    if scaled:
        block = wide_float(block_ref)
        inverse = 1.0 / jnp.maximum(peak(block), SMALLEST)
        source[0] = (block * inverse).astype(jnp.bfloat16)
    else:
        source[0] = block_ref[...]
    source[1] = jnp.zeros(source.shape[1:], jnp.bfloat16)
    acc[...] = jnp.zeros_like(acc)
    multiply_listed(count, left_ref, right_ref, source, acc, order, slot_of)


def rest_kernel(scaled, passes, shares, slots, places, *refs):
    kinds_ref, left_ref, right_ref, own_ref = refs[:4]
    refs = refs[4:]
    if scaled:
        block_ref, refs = refs[0], refs[1:]
    first, refs = refs[:shares], refs[shares:]
    others, refs = refs[: slots - 2], refs[slots - 2 :]
    if passes:
        rows_ref, refs = refs[0], refs[1:]
    t_ref, refs = refs[0], refs[1:]
    if scaled:
        unit_ref, refs = refs[0], refs[1:]
    if passes:
        refs[0][...] = rows_ref[...]
        refs = refs[1:]
    acc, source, order, slot_of = refs
    count = list_channels("rest", places, kinds_ref, order, slot_of, slots)
    if scaled:
        mine = jnp.maximum(peak(wide_float(block_ref)), SMALLEST)
        unit = mine
        for block in (*first, *others):
            unit = jnp.maximum(unit, peak(wide_float(block)))
        unit_ref[...] = jnp.broadcast_to(unit, unit_ref.shape)
        inverse = 1.0 / unit

    def scale(block):
        return (wide_float(block) * inverse).astype(jnp.bfloat16) if scaled else block[...]

    share = source.shape[1] // shares
    for step, block in enumerate(first):
        at = 0 if shares == 1 else jnp.abs(step - lax.axis_index("mpo"))
        source[1, pl.ds(pl.multiple_of(at * share, share), share), :] = scale(block)
    for slot, block in enumerate(others, 2):
        source[slot] = scale(block)
    source[slots] = jnp.zeros(source.shape[1:], jnp.bfloat16)
    acc[...] = own_ref[...] * (mine * inverse) if scaled else own_ref[...]
    multiply_listed(count, left_ref, right_ref, source, acc, order, slot_of)
    t_ref[...] = acc[...].astype(jnp.bfloat16)


def pass_kernel(block_ref, rows_ref, out_ref):
    out_ref[...] = block_ref[...]


def unpack_kernel(origin, block_ref, rows_ref, out_ref, sums_ref):
    share = out_ref.shape[0]
    out_ref[...] = block_ref[0:share, :]
    terms = block_ref[share : share + 2 * TILE, :].astype(jnp.float32)
    sums = terms[0:TILE, 0:128] + terms[0:TILE, 128:256] + terms[TILE : 2 * TILE, 0:128]
    row = lax.broadcasted_iota(jnp.int32, rows_ref.shape, 0)
    source = look_up(origin, here(), 0)
    sums_ref[...] = jnp.where(row == source, first_row(sums), rows_ref[...])


def take_kernel(block_ref, share_ref):
    share_ref[...] = block_ref[my_rows(share_ref.shape[0]), :]


def my_rows(share):
    return pl.ds(pl.multiple_of(lax.axis_index("mpo") * share, share), share)


def first_sums_kernel(share, *refs):
    parts, (psi_ref, unit_ref, w_ref, share_ref, rows_ref) = refs[:-5], refs[-5:]
    w = sum_parts(parts)
    unit = lane_of(first_row(unit_ref), 0)
    w_ref[...] = (w * unit).astype(jnp.bfloat16)
    share_ref[0:share, :] = w_ref[my_rows(share), :]
    v = wide_float(psi_ref) * (1.0 / unit)
    a = total(v * w)
    d = total(v * v)
    local = a / jnp.maximum(d, SMALLEST)
    r = w - local * v
    values = [a, d, local, total(r * v), total(r * r), unit]
    if share_ref.shape[0] > share:
        sums = pack(values, (TILE, 128))
        high = sums.astype(jnp.bfloat16)
        rest = sums - high.astype(jnp.float32)
        middle = rest.astype(jnp.bfloat16)
        low = (rest - middle.astype(jnp.float32)).astype(jnp.bfloat16)
        blank = jnp.zeros((2 * TILE, share_ref.shape[1]), jnp.bfloat16)
        share_ref[share : share + 2 * TILE, :] = blank
        share_ref[share : share + TILE, 0:128] = high
        share_ref[share : share + TILE, 128:256] = middle
        share_ref[share + TILE : share + 2 * TILE, 0:128] = low
        sums = high.astype(jnp.float32) + middle.astype(jnp.float32) + low.astype(jnp.float32)
        sums = jnp.broadcast_to(first_row(sums), rows_ref.shape)
    else:
        sums = pack(values, rows_ref.shape)
    row = lax.broadcasted_iota(jnp.int32, rows_ref.shape, 0)
    rows_ref[...] = jnp.where(row == here(), sums, 0.0)


def shrink(scal):
    return 1.0 / (jnp.abs(lane_of(scal, 0)) + lane_of(scal, 1))


def second_sums_kernel(entries, *refs):
    parts, refs = refs[:-9], refs[-9:]
    rows_ref, psi_ref, first_ref, unit_ref, wide_ref, w_ref, share_ref, v_ref, scal_ref = refs
    rows = rows_ref[...]
    a, d, local, p, q, unit = (lane_of(rows, lane) for lane in range(6))
    beta_0 = jnp.sqrt(column_sum(unit * unit * d) / entries + EPSILON)
    start_inverse = 1.0 / beta_0
    gain = unit * start_inverse
    alpha = column_sum(gain * (gain * a)) / entries
    off = local - alpha
    square = column_sum(gain * (gain * (q + off * (2.0 * p + off * d))))
    beta = jnp.sqrt(jnp.maximum(square, 0.0) / entries + EPSILON)
    inverse = 1.0 / beta
    scal = pack([alpha, beta, start_inverse], scal_ref.shape)
    scal_ref[...] = scal
    image = wide_float(first_ref) * start_inverse
    v_ref[...] = ((image - (alpha * start_inverse) * wide_float(psi_ref)) * inverse).astype(jnp.bfloat16)
    lift = lane_of(first_row(unit_ref), 0) * start_inverse
    w = (sum_parts(parts) * lift - alpha * image) * (inverse * shrink(first_row(scal)))
    wide_ref[...] = w
    w_ref[...] = w.astype(jnp.bfloat16)
    share_ref[...] = w_ref[my_rows(share_ref.shape[0]), :]


def third_sums_kernel(*refs):
    parts, refs = refs[:-8], refs[-8:]
    psi_ref, first_ref, v_ref, w_ref, scal_ref, r_ref, z_ref, rows_ref = refs
    scal = first_row(scal_ref)
    scale = shrink(scal)
    push = scale * lane_of(scal, 1) * lane_of(scal, 2)
    v, w = wide_float(v_ref), w_ref[...]
    vv, vw = total(v * v), total(v * w)
    local = vw / jnp.maximum(vv, SMALLEST)
    r = w - local * v - push * wide_float(psi_ref)
    z = sum_parts(parts) - (local / scale) * w - push * wide_float(first_ref)
    r_ref[...] = r
    z_ref[...] = z
    sums = [total(r * r), total(r * v), total(r * z), total(r * w)]
    sums += [total(z * v), total(z * w), total(z * z), total(w * w)]
    rows_ref[...] = pack([vv, vw, local] + sums, rows_ref.shape)


def final_kernel(entries, rows_ref, r_ref, z_ref, w_ref, v_ref, scal_ref, basis_ref, coef_ref):
    share = basis_ref.shape[2]
    mine = my_rows(share)
    vv, vw, local, rr, rv, rz, rw, zv, zw, zz, ww = (lane_of(rows_ref[...], i) for i in range(11))
    scal = first_row(scal_ref)
    scale = shrink(scal)
    inverse_scale = 1.0 / scale
    alpha_scaled = column_sum(vw) / entries
    off = local - alpha_scaled
    lift = off * inverse_scale
    square = column_sum(rr + off * (2.0 * rv + off * vv)) / entries
    beta_scaled = jnp.sqrt(jnp.maximum(square, 0.0) + scale * scale * EPSILON)
    inverse = 1.0 / beta_scaled
    mixed = column_sum(rz + lift * rw + off * (zv + lift * vw)) / entries
    alpha_3 = mixed * inverse * inverse
    r_v = column_sum(rv + off * vv) / entries
    z_v = column_sum(zv + lift * vw) / entries
    z_z = column_sum(zz + lift * (2.0 * zw + lift * ww)) / entries
    v_v = column_sum(vv) / entries
    beta_2 = beta_scaled * inverse_scale
    third = (z_z - 2.0 * alpha_3 * mixed + alpha_3 * alpha_3 * square) * inverse * inverse
    third += beta_2 * (beta_2 * v_v - 2.0 * inverse * (z_v - alpha_3 * r_v))
    beta_3 = jnp.sqrt(jnp.maximum(third, 0.0) + EPSILON)

    sector = here()
    row_of = lax.broadcasted_iota(jnp.int32, off.shape, 0)
    off_here = column_sum(jnp.where(row_of == sector, off, 0.0))
    v = v_ref[mine, :]
    v_wide = v.astype(jnp.float32)
    v_3 = (r_ref[mine, :] + off_here * v_wide) * inverse
    image = (z_ref[mine, :] + (off_here * inverse_scale) * w_ref[mine, :]) * inverse
    basis_ref[0, 0] = v
    basis_ref[1, 0] = v_3.astype(jnp.bfloat16)
    residual = image - alpha_3 * v_3 - beta_2 * v_wide
    basis_ref[2, 0] = (residual * (1.0 / beta_3)).astype(jnp.bfloat16)

    row = lax.broadcasted_iota(jnp.int32, coef_ref.shape, 0)
    column = lax.broadcasted_iota(jnp.int32, coef_ref.shape, 1)
    out = jnp.zeros(coef_ref.shape, jnp.float32)
    pairs = [(lane_of(scal, 0), lane_of(scal, 1)), (alpha_scaled * inverse_scale, beta_2), (alpha_3, beta_3)]
    for step, (a, b) in enumerate(pairs):
        out = jnp.where(column == step, jnp.where(row == 0, a, b), out)
    coef_ref[...] = out


def shards(wavefunction, env_left, env_right, channel_class):
    width = wavefunction.shape[1]
    ring = ("blk", "rep")
    parts = lax.axis_size("mpo")
    blocks = lax.axis_size("blk") * lax.axis_size("rep")
    entries = blocks * width * width
    permutes = routes(blocks)
    places, origins = slot_tables(permutes, blocks)
    slots = 1 + len(permutes)
    channels = channel_class.shape[0]
    psi, left, right = wavefunction[0], env_left[:, 0], env_right[:, 0]
    left, right = pl.pallas_call(
        load_kernel,
        out_shape=(jax.ShapeDtypeStruct(left.shape, left.dtype),) * 2,
        in_specs=[pl.BlockSpec(memory_space=pl.ANY)] * 2,
        out_specs=(VMEM, VMEM),
        scratch_shapes=[pltpu.SemaphoreType.DMA((2, channels))],
        compiler_params=pltpu.CompilerParams(vmem_limit_bytes=46 * MIB),
        name="load",
    )(left, right)
    rows_shape = jax.ShapeDtypeStruct((blocks, 128), jnp.float32)
    scalars = jax.ShapeDtypeStruct((8, 128), jnp.float32)
    wide = jax.ShapeDtypeStruct((width, width), jnp.float32)
    narrow = jax.ShapeDtypeStruct((width, width), jnp.bfloat16)
    share_shape = jax.ShapeDtypeStruct((width // parts, width), jnp.bfloat16)
    lists = [pltpu.SMEM((channels + WIDE,), jnp.int32)] * 2

    def call(kernel, name, outs, args, scratch=(), share=0, limit=4):
        flops = int(4 * channels * share * width**3)
        cost = pl.CostEstimate(flops=flops, bytes_accessed=4 * width * width, transcendentals=0)
        listed = outs if isinstance(outs, tuple) else (outs,)
        first = SMEM if share else VMEM
        return pl.pallas_call(
            kernel,
            out_shape=outs,
            in_specs=[first] + [VMEM] * (len(args) - 1),
            out_specs=tuple(VMEM for _ in listed) if isinstance(outs, tuple) else VMEM,
            scratch_shapes=list(scratch),
            compiler_params=pltpu.CompilerParams(vmem_limit_bytes=limit * MIB),
            cost_estimate=cost,
            name=name,
        )(*args)

    def sources(count):
        return pltpu.VMEM((count + 1, width, width), jnp.bfloat16)

    def own(scaled, block):
        return call(
            functools.partial(own_kernel, scaled, places),
            "own",
            wide,
            (channel_class, left, right, block),
            [sources(1)] + lists,
            0.2,
            16,
        )

    def rest(mine, first, others, block=None, rows=None):
        scaled, passes = block is not None, rows is not None
        outs = (narrow,) + (scalars,) * scaled + (rows_shape,) * passes
        args = [channel_class, left, right, mine] + [block] * scaled + first + others + [rows] * passes
        return call(
            functools.partial(rest_kernel, scaled, passes, len(first), slots, places),
            "rest",
            outs,
            args,
            [pltpu.VMEM((width, width), jnp.float32), sources(slots)] + lists,
            0.4,
            16,
        )

    def shift(block, pairs):
        return lax.ppermute(block, ring, pairs)

    carried = carried_rounds(permutes, blocks)
    rounds = [(ring, pairs) for pairs in carried or []]
    for axis in () if carried else ("rep", "blk"):
        size = lax.axis_size(axis)
        bits = [1 << i for i in range(size.bit_length() - 1)]
        if sum(bits) == size - 1:
            rounds += [(axis, [(i, i ^ bit) for i in range(size)]) for bit in bits]
        else:
            rounds += [(axis, None)]

    def add_round(rows, axis, pairs):
        if pairs is None:
            return lax.psum(rows, axis)
        return rows + lax.ppermute(rows, axis, pairs)

    def spread(block, share, rows=None, after=None):
        piece = shift(share, permutes[0])
        if rows is not None and carried:
            piece, rows = call(
                functools.partial(unpack_kernel, origins[1]),
                "unpack",
                (share_shape, rows_shape),
                (piece, rows),
            )
            rows = add_round(rows, *rounds[0])
        elif rows is not None:
            for step in rounds[:-1]:
                rows = add_round(rows, *step)
            piece = call(pass_kernel, "hold", share_shape, (piece, rows))
        elif after is not None:
            piece = call(pass_kernel, "hold", share_shape, (piece, after))
        if parts == 2:
            first = [piece, lax.ppermute(piece, "mpo", [(0, 1), (1, 0)])]
        else:
            first = [lax.all_gather(piece, "mpo", axis=0, tiled=True)]
        return first, [shift(block, pairs) for pairs in permutes[1:]], rows

    def gather_parts(t):
        if parts == 2:
            return [t, lax.ppermute(t, "mpo", [(0, 1), (1, 0)])]
        held = lax.all_gather(t, "mpo")
        return [held[i] for i in range(parts)]

    def exchange(rows):
        return lax.all_to_all(rows, ring, 0, 0, tiled=True)

    first, others, _ = spread(psi, call(take_kernel, "take", share_shape, (psi,)), after=left)
    t, unit = rest(own(True, psi), first, others, psi)
    rows_in_share = width // parts + (2 * TILE if carried else 0)
    w_1, share_1, rows = call(
        functools.partial(first_sums_kernel, width // parts),
        "sums",
        (narrow, jax.ShapeDtypeStruct((rows_in_share, width), jnp.bfloat16), rows_shape),
        (*gather_parts(t), psi, unit),
    )
    first, others, rows = spread(w_1, share_1, rows)
    t, unit, rows = rest(own(True, w_1), first, others, w_1, rows)
    rows = add_round(rows, *rounds[-1])
    w_wide, w_2, share_2, v_2, scal = call(
        functools.partial(second_sums_kernel, entries),
        "sums",
        (wide, narrow, share_shape, narrow, scalars),
        (*gather_parts(t), rows, psi, w_1, unit),
    )
    first, others, _ = spread(w_2, share_2)
    (t,) = rest(own(False, w_2), first, others)
    r, z, rows = call(
        third_sums_kernel,
        "sums",
        (wide, wide, rows_shape),
        (*gather_parts(t), psi, w_1, v_2, w_wide, scal),
        limit=8,
    )
    return call(
        functools.partial(final_kernel, entries),
        "final",
        (
            jax.ShapeDtypeStruct((STEPS, 1, width // parts, width), jnp.bfloat16),
            jax.ShapeDtypeStruct((2, STEPS), jnp.float32),
        ),
        (exchange(rows), r, z, w_wide, v_2, scal),
    )


def solution(mesh):
    return jax.shard_map(
        shards,
        mesh=mesh,
        in_specs=(
            P(("groups", "blk", "rep"), None, None),
            P("mpo", ("groups", "blk", "rep"), None, None),
            P("mpo", ("groups", "blk", "rep"), None, None),
            P("mpo"),
        ),
        out_specs=(P(None, ("groups", "blk", "rep"), "mpo", None), P("groups", None)),
        check_vma=False,
    )
```

```python
import functools

import jax
import jax.numpy as jnp
from jax import lax
from jax.experimental import pallas as pl
from jax.experimental.pallas import tpu as pltpu
from jax.sharding import PartitionSpec as P

NS = 4
STEPS = 3
OFFSETS = (0, NS + 1, NS - 1, -(NS + 1), -(NS - 1))
EPSILON = 1e-06
WIDE = 8
SMALLEST = 1e-30
TILE = 16
LOADS = 4
MIB = 1024 * 1024
VMEM = pl.BlockSpec(memory_space=pltpu.VMEM)
SMEM = pl.BlockSpec(memory_space=pltpu.SMEM)


def reaches(kind, sector, blocks):
    source = sector - OFFSETS[kind]
    spin = sector % NS
    inside = (source >= 0) & (source < blocks)
    if kind in (1, 4):
        return inside & (spin >= 1)
    if kind in (2, 3):
        return inside & (spin <= NS - 2)
    return inside


def routes(blocks):
    degree, edges = [0] * blocks, []
    for kind in (1, 2):
        for k in range(blocks):
            if reaches(kind, k, blocks):
                edges.append((k - OFFSETS[kind], k))
                degree[k - OFFSETS[kind]] += 1
                degree[k] += 1
    edges.sort(key=lambda edge: degree[edge[0]] + degree[edge[1]])
    partner = [{} for _ in range(blocks)]

    def lowest(block):
        return next(c for c in range(len(edges)) if c not in partner[block])

    for a, b in edges:
        here_free, there_free = lowest(a), lowest(b)
        if here_free in partner[b]:
            path, block, colour = [b], b, here_free
            while colour in partner[block]:
                block = partner[block][colour]
                path.append(block)
                colour = there_free if colour == here_free else here_free
            for block in path:
                moved = {}
                for old, new in ((here_free, there_free), (there_free, here_free)):
                    if old in partner[block]:
                        moved[new] = partner[block].pop(old)
                partner[block].update(moved)
        partner[a][here_free], partner[b][here_free] = b, a
    colours = sorted({c for held in partner for c in held})
    permutes = [[(held[c], k) for k, held in enumerate(partner) if c in held] for c in colours]
    return sorted(permutes, key=len, reverse=True)


def slot_tables(permutes, blocks):
    origins = [{k: k for k in range(blocks)}] + [{k: s for s, k in pairs} for pairs in permutes]
    places = []
    for kind in range(5):
        place = {}
        for slot, origin in enumerate(origins):
            for k, source in origin.items():
                if source == k - OFFSETS[kind] and reaches(kind, k, blocks):
                    place[k] = slot
        places.append(place)
    return places, origins


def carried_rounds(permutes, blocks):
    if not permutes or blocks % 4:
        return None
    rounds = [dict(permutes[0])] + [{k: k ^ bit for k in range(blocks)} for bit in (1, 2)]
    held = [{k} for k in range(blocks)]
    for pairs in rounds:
        if sorted(pairs.values()) != list(range(blocks)):
            return None
        if any(held[source] & held[k] for source, k in pairs.items()):
            return None
        grown = list(held)
        for source, k in pairs.items():
            grown[k] = held[k] | held[source]
        held = grown
    if any(len(rows) < blocks for rows in held):
        return None
    return [sorted(pairs.items()) for pairs in rounds[1:]]


def look_up(table, sector, default):
    out = jnp.int32(default)
    for k, value in table.items():
        if value != default:
            out = jnp.where(sector == k, jnp.int32(value), out)
    return out


def here():
    return lax.axis_index("blk") * lax.axis_size("rep") + lax.axis_index("rep")


def lane_of(rows, lane):
    return rows[:, lane : lane + 1]


def pack(values, shape):
    lanes = lax.broadcasted_iota(jnp.int32, shape, 1)
    out = jnp.zeros(shape, jnp.float32)
    for place, value in enumerate(values):
        out = jnp.where(lanes == place, value, out)
    return out


def total(x):
    return jnp.sum(jnp.sum(x, axis=0, keepdims=True), axis=1, keepdims=True)


def column_sum(x):
    return jnp.sum(x, axis=0, keepdims=True)


def peak(x):
    return jnp.max(jnp.max(jnp.abs(x), axis=0, keepdims=True), axis=1, keepdims=True)


def wide_float(ref):
    return ref[...].astype(jnp.float32)


def sum_parts(parts):
    w = wide_float(parts[0])
    for part in parts[1:]:
        w += wide_float(part)
    return w


def first_row(ref):
    return ref[0:1, :]


def list_channels(which, places, kinds_ref, order, slot_of, idle):
    sector = here()
    slots = [jnp.int32(-1 if which == "rest" else 0)]
    slots += [look_up(places[c], sector, -1) if which != "own" else jnp.int32(-1) for c in range(1, 5)]
    count = jnp.int32(0)
    for b in range(kinds_ref.shape[0]):
        kind = kinds_ref[b]
        slot = slots[0]
        for c in range(1, 5):
            slot = jnp.where(kind == c, slots[c], slot)
        order[count] = jnp.int32(b)
        slot_of[count] = slot
        count += jnp.where(slot >= 0, 1, 0)
    for extra in range(WIDE):
        order[count + extra] = jnp.int32(0)
        slot_of[count + extra] = jnp.int32(idle)
    return count


def multiply_listed(count, left_ref, right_ref, source, acc, order, slot_of):
    def multiply(start, wide):
        held = [order[start + inner] for inner in range(wide)]
        pieces = [
            jnp.dot(
                left_ref[b], source[slot_of[start + inner]], preferred_element_type=jnp.float32
            ).astype(jnp.bfloat16)
            for inner, b in enumerate(held)
        ]
        acc[...] += lax.dot_general(
            jnp.concatenate(pieces, axis=1),
            jnp.concatenate([right_ref[b] for b in held], axis=1),
            (((1,), (1,)), ((), ())),
            preferred_element_type=jnp.float32,
        )

    def full(group, carry):
        multiply(group * WIDE, WIDE)
        return carry

    groups = (count + WIDE // 2 - 1) // WIDE
    lax.fori_loop(0, groups, full, 0)
    rest = count - groups * WIDE
    for low, wide in ((0, 2), (2, 4)):

        @pl.when((rest > low) & (rest <= wide))
        def _():
            multiply(groups * WIDE, wide)


def load_kernel(left_hbm, right_hbm, left_ref, right_ref, sems):
    channels = left_ref.shape[0]
    step = max(1, channels // LOADS)
    copies = []
    for side, (source, target) in enumerate(((left_hbm, left_ref), (right_hbm, right_ref))):
        for at, low in enumerate(range(0, channels, step)):
            part = pl.ds(low, min(step, channels - low))
            copies.append(pltpu.make_async_copy(source.at[part], target.at[part], sems.at[side, at]))
    for copy in copies:
        copy.start()
    for copy in copies:
        copy.wait()


def own_kernel(scaled, places, kinds_ref, left_ref, right_ref, block_ref, acc, source, order, slot_of):
    count = list_channels("own", places, kinds_ref, order, slot_of, 1)
    if scaled:
        block = wide_float(block_ref)
        inverse = 1.0 / jnp.maximum(peak(block), SMALLEST)
        source[0] = (block * inverse).astype(jnp.bfloat16)
    else:
        source[0] = block_ref[...]
    source[1] = jnp.zeros(source.shape[1:], jnp.bfloat16)
    acc[...] = jnp.zeros_like(acc)
    multiply_listed(count, left_ref, right_ref, source, acc, order, slot_of)


def rest_kernel(scaled, passes, shares, slots, places, *refs):
    kinds_ref, left_ref, right_ref, own_ref = refs[:4]
    refs = refs[4:]
    if scaled:
        block_ref, refs = refs[0], refs[1:]
    first, refs = refs[:shares], refs[shares:]
    others, refs = refs[: slots - 2], refs[slots - 2 :]
    if passes:
        rows_ref, refs = refs[0], refs[1:]
    t_ref, refs = refs[0], refs[1:]
    if scaled:
        unit_ref, refs = refs[0], refs[1:]
    if passes:
        refs[0][...] = rows_ref[...]
        refs = refs[1:]
    acc, source, order, slot_of = refs
    count = list_channels("rest", places, kinds_ref, order, slot_of, slots)
    if scaled:
        mine = jnp.maximum(peak(wide_float(block_ref)), SMALLEST)
        unit = mine
        for block in (*first, *others):
            unit = jnp.maximum(unit, peak(wide_float(block)))
        unit_ref[...] = jnp.broadcast_to(unit, unit_ref.shape)
        inverse = 1.0 / unit

    def scale(block):
        return (wide_float(block) * inverse).astype(jnp.bfloat16) if scaled else block[...]

    share = source.shape[1] // shares
    for step, block in enumerate(first):
        at = 0 if shares == 1 else jnp.abs(step - lax.axis_index("mpo"))
        source[1, pl.ds(pl.multiple_of(at * share, share), share), :] = scale(block)
    for slot, block in enumerate(others, 2):
        source[slot] = scale(block)
    source[slots] = jnp.zeros(source.shape[1:], jnp.bfloat16)
    acc[...] = own_ref[...] * (mine * inverse) if scaled else own_ref[...]
    multiply_listed(count, left_ref, right_ref, source, acc, order, slot_of)
    t_ref[...] = acc[...].astype(jnp.bfloat16)


def pass_kernel(block_ref, rows_ref, out_ref):
    out_ref[...] = block_ref[...]


def unpack_kernel(origin, block_ref, rows_ref, out_ref, sums_ref):
    share = out_ref.shape[0]
    out_ref[...] = block_ref[0:share, :]
    terms = block_ref[share : share + 2 * TILE, :].astype(jnp.float32)
    sums = terms[0:TILE, 0:128] + terms[0:TILE, 128:256] + terms[TILE : 2 * TILE, 0:128]
    row = lax.broadcasted_iota(jnp.int32, rows_ref.shape, 0)
    source = look_up(origin, here(), 0)
    sums_ref[...] = jnp.where(row == source, first_row(sums), rows_ref[...])


def take_kernel(block_ref, copy_ref, share_ref):
    copy_ref[...] = block_ref[...]
    share_ref[...] = block_ref[my_rows(share_ref.shape[0]), :]


def my_rows(share):
    return pl.ds(pl.multiple_of(lax.axis_index("mpo") * share, share), share)


def first_sums_kernel(share, *refs):
    parts, (psi_ref, unit_ref, w_ref, share_ref, rows_ref) = refs[:-5], refs[-5:]
    w = sum_parts(parts)
    unit = lane_of(first_row(unit_ref), 0)
    w_ref[...] = (w * unit).astype(jnp.bfloat16)
    share_ref[0:share, :] = w_ref[my_rows(share), :]
    v = wide_float(psi_ref) * (1.0 / unit)
    a = total(v * w)
    d = total(v * v)
    local = a / jnp.maximum(d, SMALLEST)
    r = w - local * v
    values = [a, d, local, total(r * v), total(r * r), unit]
    if share_ref.shape[0] > share:
        sums = pack(values, (TILE, 128))
        high = sums.astype(jnp.bfloat16)
        rest = sums - high.astype(jnp.float32)
        middle = rest.astype(jnp.bfloat16)
        low = (rest - middle.astype(jnp.float32)).astype(jnp.bfloat16)
        blank = jnp.zeros((2 * TILE, share_ref.shape[1]), jnp.bfloat16)
        share_ref[share : share + 2 * TILE, :] = blank
        share_ref[share : share + TILE, 0:128] = high
        share_ref[share : share + TILE, 128:256] = middle
        share_ref[share + TILE : share + 2 * TILE, 0:128] = low
        sums = high.astype(jnp.float32) + middle.astype(jnp.float32) + low.astype(jnp.float32)
        sums = jnp.broadcast_to(first_row(sums), rows_ref.shape)
    else:
        sums = pack(values, rows_ref.shape)
    row = lax.broadcasted_iota(jnp.int32, rows_ref.shape, 0)
    rows_ref[...] = jnp.where(row == here(), sums, 0.0)


def shrink(scal):
    return 1.0 / (jnp.abs(lane_of(scal, 0)) + lane_of(scal, 1))


def second_sums_kernel(entries, *refs):
    parts, refs = refs[:-9], refs[-9:]
    rows_ref, psi_ref, first_ref, unit_ref, wide_ref, w_ref, share_ref, v_ref, scal_ref = refs
    rows = rows_ref[...]
    a, d, local, p, q, unit = (lane_of(rows, lane) for lane in range(6))
    beta_0 = jnp.sqrt(column_sum(unit * unit * d) / entries + EPSILON)
    start_inverse = 1.0 / beta_0
    gain = unit * start_inverse
    alpha = column_sum(gain * (gain * a)) / entries
    off = local - alpha
    square = column_sum(gain * (gain * (q + off * (2.0 * p + off * d))))
    beta = jnp.sqrt(jnp.maximum(square, 0.0) / entries + EPSILON)
    inverse = 1.0 / beta
    scal = pack([alpha, beta, start_inverse], scal_ref.shape)
    scal_ref[...] = scal
    image = wide_float(first_ref) * start_inverse
    v_ref[...] = ((image - (alpha * start_inverse) * wide_float(psi_ref)) * inverse).astype(jnp.bfloat16)
    lift = lane_of(first_row(unit_ref), 0) * start_inverse
    w = (sum_parts(parts) * lift - alpha * image) * (inverse * shrink(first_row(scal)))
    wide_ref[...] = w
    w_ref[...] = w.astype(jnp.bfloat16)
    share_ref[...] = w_ref[my_rows(share_ref.shape[0]), :]


def third_sums_kernel(*refs):
    parts, refs = refs[:-8], refs[-8:]
    psi_ref, first_ref, v_ref, w_ref, scal_ref, r_ref, z_ref, rows_ref = refs
    scal = first_row(scal_ref)
    scale = shrink(scal)
    push = scale * lane_of(scal, 1) * lane_of(scal, 2)
    v, w = wide_float(v_ref), w_ref[...]
    vv, vw = total(v * v), total(v * w)
    local = vw / jnp.maximum(vv, SMALLEST)
    r = w - local * v - push * wide_float(psi_ref)
    z = sum_parts(parts) - (local / scale) * w - push * wide_float(first_ref)
    r_ref[...] = r
    z_ref[...] = z
    sums = [total(r * r), total(r * v), total(r * z), total(r * w)]
    sums += [total(z * v), total(z * w), total(z * z), total(w * w)]
    rows_ref[...] = pack([vv, vw, local] + sums, rows_ref.shape)


def final_kernel(entries, rows_ref, r_ref, z_ref, w_ref, v_ref, scal_ref, basis_ref, coef_ref):
    share = basis_ref.shape[2]
    mine = my_rows(share)
    vv, vw, local, rr, rv, rz, rw, zv, zw, zz, ww = (lane_of(rows_ref[...], i) for i in range(11))
    scal = first_row(scal_ref)
    scale = shrink(scal)
    inverse_scale = 1.0 / scale
    alpha_scaled = column_sum(vw) / entries
    off = local - alpha_scaled
    lift = off * inverse_scale
    square = column_sum(rr + off * (2.0 * rv + off * vv)) / entries
    beta_scaled = jnp.sqrt(jnp.maximum(square, 0.0) + scale * scale * EPSILON)
    inverse = 1.0 / beta_scaled
    mixed = column_sum(rz + lift * rw + off * (zv + lift * vw)) / entries
    alpha_3 = mixed * inverse * inverse
    r_v = column_sum(rv + off * vv) / entries
    z_v = column_sum(zv + lift * vw) / entries
    z_z = column_sum(zz + lift * (2.0 * zw + lift * ww)) / entries
    v_v = column_sum(vv) / entries
    beta_2 = beta_scaled * inverse_scale
    third = (z_z - 2.0 * alpha_3 * mixed + alpha_3 * alpha_3 * square) * inverse * inverse
    third += beta_2 * (beta_2 * v_v - 2.0 * inverse * (z_v - alpha_3 * r_v))
    beta_3 = jnp.sqrt(jnp.maximum(third, 0.0) + EPSILON)

    sector = here()
    row_of = lax.broadcasted_iota(jnp.int32, off.shape, 0)
    off_here = column_sum(jnp.where(row_of == sector, off, 0.0))
    v = v_ref[mine, :]
    v_wide = v.astype(jnp.float32)
    v_3 = (r_ref[mine, :] + off_here * v_wide) * inverse
    image = (z_ref[mine, :] + (off_here * inverse_scale) * w_ref[mine, :]) * inverse
    basis_ref[0, 0] = v
    basis_ref[1, 0] = v_3.astype(jnp.bfloat16)
    residual = image - alpha_3 * v_3 - beta_2 * v_wide
    basis_ref[2, 0] = (residual * (1.0 / beta_3)).astype(jnp.bfloat16)

    row = lax.broadcasted_iota(jnp.int32, coef_ref.shape, 0)
    column = lax.broadcasted_iota(jnp.int32, coef_ref.shape, 1)
    out = jnp.zeros(coef_ref.shape, jnp.float32)
    pairs = [(lane_of(scal, 0), lane_of(scal, 1)), (alpha_scaled * inverse_scale, beta_2), (alpha_3, beta_3)]
    for step, (a, b) in enumerate(pairs):
        out = jnp.where(column == step, jnp.where(row == 0, a, b), out)
    coef_ref[...] = out


def shards(wavefunction, env_left, env_right, channel_class):
    width = wavefunction.shape[1]
    ring = ("blk", "rep")
    parts = lax.axis_size("mpo")
    blocks = lax.axis_size("blk") * lax.axis_size("rep")
    entries = blocks * width * width
    permutes = routes(blocks)
    places, origins = slot_tables(permutes, blocks)
    slots = 1 + len(permutes)
    channels = channel_class.shape[0]
    psi, left, right = wavefunction[0], env_left[:, 0], env_right[:, 0]
    left, right = pl.pallas_call(
        load_kernel,
        out_shape=(jax.ShapeDtypeStruct(left.shape, left.dtype),) * 2,
        in_specs=[pl.BlockSpec(memory_space=pl.ANY)] * 2,
        out_specs=(VMEM, VMEM),
        scratch_shapes=[pltpu.SemaphoreType.DMA((2, channels))],
        compiler_params=pltpu.CompilerParams(vmem_limit_bytes=46 * MIB),
        name="load",
    )(left, right)
    rows_shape = jax.ShapeDtypeStruct((blocks, 128), jnp.float32)
    scalars = jax.ShapeDtypeStruct((8, 128), jnp.float32)
    wide = jax.ShapeDtypeStruct((width, width), jnp.float32)
    narrow = jax.ShapeDtypeStruct((width, width), jnp.bfloat16)
    share_shape = jax.ShapeDtypeStruct((width // parts, width), jnp.bfloat16)
    lists = [pltpu.SMEM((channels + WIDE,), jnp.int32)] * 2

    def call(kernel, name, outs, args, scratch=(), share=0, limit=4):
        flops = int(4 * channels * share * width**3)
        cost = pl.CostEstimate(flops=flops, bytes_accessed=4 * width * width, transcendentals=0)
        listed = outs if isinstance(outs, tuple) else (outs,)
        first = SMEM if share else VMEM
        return pl.pallas_call(
            kernel,
            out_shape=outs,
            in_specs=[first] + [VMEM] * (len(args) - 1),
            out_specs=tuple(VMEM for _ in listed) if isinstance(outs, tuple) else VMEM,
            scratch_shapes=list(scratch),
            compiler_params=pltpu.CompilerParams(vmem_limit_bytes=limit * MIB),
            cost_estimate=cost,
            name=name,
        )(*args)

    def sources(count):
        return pltpu.VMEM((count + 1, width, width), jnp.bfloat16)

    def own(scaled, block):
        return call(
            functools.partial(own_kernel, scaled, places),
            "own",
            wide,
            (channel_class, left, right, block),
            [sources(1)] + lists,
            0.2,
            16,
        )

    def rest(mine, first, others, block=None, rows=None):
        scaled, passes = block is not None, rows is not None
        outs = (narrow,) + (scalars,) * scaled + (rows_shape,) * passes
        args = [channel_class, left, right, mine] + [block] * scaled + first + others + [rows] * passes
        return call(
            functools.partial(rest_kernel, scaled, passes, len(first), slots, places),
            "rest",
            outs,
            args,
            [pltpu.VMEM((width, width), jnp.float32), sources(slots)] + lists,
            0.4,
            16,
        )

    def shift(block, pairs):
        return lax.ppermute(block, ring, pairs)

    carried = carried_rounds(permutes, blocks)
    rounds = [(ring, pairs) for pairs in carried or []]
    for axis in () if carried else ("rep", "blk"):
        size = lax.axis_size(axis)
        bits = [1 << i for i in range(size.bit_length() - 1)]
        if sum(bits) == size - 1:
            rounds += [(axis, [(i, i ^ bit) for i in range(size)]) for bit in bits]
        else:
            rounds += [(axis, None)]

    def add_round(rows, axis, pairs):
        if pairs is None:
            return lax.psum(rows, axis)
        return rows + lax.ppermute(rows, axis, pairs)

    def spread(block, share, rows=None, after=None):
        piece = shift(share, permutes[0])
        if rows is not None and carried:
            piece, rows = call(
                functools.partial(unpack_kernel, origins[1]),
                "unpack",
                (share_shape, rows_shape),
                (piece, rows),
            )
            rows = add_round(rows, *rounds[0])
        elif rows is not None:
            for step in rounds[:-1]:
                rows = add_round(rows, *step)
            piece = call(pass_kernel, "hold", share_shape, (piece, rows))
        elif after is not None:
            piece = call(pass_kernel, "hold", share_shape, (piece, after))
        if parts == 2:
            first = [piece, lax.ppermute(piece, "mpo", [(0, 1), (1, 0)])]
        else:
            first = [lax.all_gather(piece, "mpo", axis=0, tiled=True)]
        return first, [shift(block, pairs) for pairs in permutes[1:]], rows

    def gather_parts(t):
        if parts == 2:
            return [t, lax.ppermute(t, "mpo", [(0, 1), (1, 0)])]
        held = lax.all_gather(t, "mpo")
        return [held[i] for i in range(parts)]

    def exchange(rows):
        return lax.all_to_all(rows, ring, 0, 0, tiled=True)

    psi, share_0 = call(take_kernel, "take", (narrow, share_shape), (psi,))
    first, others, _ = spread(psi, share_0, after=left)
    t, unit = rest(own(True, psi), first, others, psi)
    rows_in_share = width // parts + (2 * TILE if carried else 0)
    w_1, share_1, rows = call(
        functools.partial(first_sums_kernel, width // parts),
        "sums",
        (narrow, jax.ShapeDtypeStruct((rows_in_share, width), jnp.bfloat16), rows_shape),
        (*gather_parts(t), psi, unit),
    )
    first, others, rows = spread(w_1, share_1, rows)
    t, unit, rows = rest(own(True, w_1), first, others, w_1, rows)
    rows = add_round(rows, *rounds[-1])
    w_wide, w_2, share_2, v_2, scal = call(
        functools.partial(second_sums_kernel, entries),
        "sums",
        (wide, narrow, share_shape, narrow, scalars),
        (*gather_parts(t), rows, psi, w_1, unit),
    )
    first, others, _ = spread(w_2, share_2)
    (t,) = rest(own(False, w_2), first, others)
    r, z, rows = call(
        third_sums_kernel,
        "sums",
        (wide, wide, rows_shape),
        (*gather_parts(t), psi, w_1, v_2, w_wide, scal),
        limit=8,
    )
    return call(
        functools.partial(final_kernel, entries),
        "final",
        (
            jax.ShapeDtypeStruct((STEPS, 1, width // parts, width), jnp.bfloat16),
            jax.ShapeDtypeStruct((2, STEPS), jnp.float32),
        ),
        (exchange(rows), r, z, w_wide, v_2, scal),
    )


def solution(mesh):
    return jax.shard_map(
        shards,
        mesh=mesh,
        in_specs=(
            P(("groups", "blk", "rep"), None, None),
            P("mpo", ("groups", "blk", "rep"), None, None),
            P("mpo", ("groups", "blk", "rep"), None, None),
            P("mpo"),
        ),
        out_specs=(P(None, ("groups", "blk", "rep"), "mpo", None), P("groups", None)),
        check_vma=False,
    )
```

```python
import functools

import jax
import jax.numpy as jnp
from jax import lax
from jax.experimental import pallas as pl
from jax.experimental.pallas import tpu as pltpu
from jax.sharding import PartitionSpec as P

NS = 4
STEPS = 3
OFFSETS = (0, NS + 1, NS - 1, -(NS + 1), -(NS - 1))
EPSILON = 1e-06
WIDE = 8
SMALLEST = 1e-30
TILE = 16
LOADS = 4
MIB = 1024 * 1024
VMEM = pl.BlockSpec(memory_space=pltpu.VMEM)
SMEM = pl.BlockSpec(memory_space=pltpu.SMEM)


def reaches(kind, sector, blocks):
    source = sector - OFFSETS[kind]
    spin = sector % NS
    inside = (source >= 0) & (source < blocks)
    if kind in (1, 4):
        return inside & (spin >= 1)
    if kind in (2, 3):
        return inside & (spin <= NS - 2)
    return inside


def routes(blocks):
    degree, edges = [0] * blocks, []
    for kind in (1, 2):
        for k in range(blocks):
            if reaches(kind, k, blocks):
                edges.append((k - OFFSETS[kind], k))
                degree[k - OFFSETS[kind]] += 1
                degree[k] += 1
    edges.sort(key=lambda edge: degree[edge[0]] + degree[edge[1]])
    partner = [{} for _ in range(blocks)]

    def lowest(block):
        return next(c for c in range(len(edges)) if c not in partner[block])

    for a, b in edges:
        here_free, there_free = lowest(a), lowest(b)
        if here_free in partner[b]:
            path, block, colour = [b], b, here_free
            while colour in partner[block]:
                block = partner[block][colour]
                path.append(block)
                colour = there_free if colour == here_free else here_free
            for block in path:
                moved = {}
                for old, new in ((here_free, there_free), (there_free, here_free)):
                    if old in partner[block]:
                        moved[new] = partner[block].pop(old)
                partner[block].update(moved)
        partner[a][here_free], partner[b][here_free] = b, a
    colours = sorted({c for held in partner for c in held})
    permutes = [[(held[c], k) for k, held in enumerate(partner) if c in held] for c in colours]
    return sorted(permutes, key=len, reverse=True)


def slot_tables(permutes, blocks):
    origins = [{k: k for k in range(blocks)}] + [{k: s for s, k in pairs} for pairs in permutes]
    places = []
    for kind in range(5):
        place = {}
        for slot, origin in enumerate(origins):
            for k, source in origin.items():
                if source == k - OFFSETS[kind] and reaches(kind, k, blocks):
                    place[k] = slot
        places.append(place)
    return places, origins


def carried_rounds(permutes, blocks):
    if not permutes or blocks % 4:
        return None
    rounds = [dict(permutes[0])] + [{k: k ^ bit for k in range(blocks)} for bit in (1, 2)]
    held = [{k} for k in range(blocks)]
    for pairs in rounds:
        if sorted(pairs.values()) != list(range(blocks)):
            return None
        if any(held[source] & held[k] for source, k in pairs.items()):
            return None
        grown = list(held)
        for source, k in pairs.items():
            grown[k] = held[k] | held[source]
        held = grown
    if any(len(rows) < blocks for rows in held):
        return None
    return [sorted(pairs.items()) for pairs in rounds[1:]]


def look_up(table, sector, default):
    out = jnp.int32(default)
    for k, value in table.items():
        if value != default:
            out = jnp.where(sector == k, jnp.int32(value), out)
    return out


def here():
    return lax.axis_index("blk") * lax.axis_size("rep") + lax.axis_index("rep")


def lane_of(rows, lane):
    return rows[:, lane : lane + 1]


def pack(values, shape):
    lanes = lax.broadcasted_iota(jnp.int32, shape, 1)
    out = jnp.zeros(shape, jnp.float32)
    for place, value in enumerate(values):
        out = jnp.where(lanes == place, value, out)
    return out


def total(x):
    return jnp.sum(jnp.sum(x, axis=0, keepdims=True), axis=1, keepdims=True)


def column_sum(x):
    return jnp.sum(x, axis=0, keepdims=True)


def peak(x):
    return jnp.max(jnp.max(jnp.abs(x), axis=0, keepdims=True), axis=1, keepdims=True)


def wide_float(ref):
    return ref[...].astype(jnp.float32)


def sum_parts(parts):
    w = wide_float(parts[0])
    for part in parts[1:]:
        w += wide_float(part)
    return w


def first_row(ref):
    return ref[0:1, :]


def list_channels(which, places, kinds_ref, order, slot_of, idle):
    sector = here()
    low, high = {"own": (0, 0), "rest": (1, idle), "first": (1, 1), "others": (2, idle)}[which]
    slots = []
    for place in places:
        kept = {k: slot for k, slot in place.items() if low <= slot <= high}
        slots.append(look_up(kept, sector, -1))
    count = jnp.int32(0)
    for b in range(kinds_ref.shape[0]):
        kind = kinds_ref[b]
        slot = slots[0]
        for c in range(1, 5):
            slot = jnp.where(kind == c, slots[c], slot)
        order[count] = jnp.int32(b)
        slot_of[count] = slot
        count += jnp.where(slot >= 0, 1, 0)
    for extra in range(WIDE):
        order[count + extra] = jnp.int32(0)
        slot_of[count + extra] = jnp.int32(idle)
    return count


def multiply_listed(count, left_ref, right_ref, source, acc, order, slot_of):
    def multiply(start, wide):
        held = [order[start + inner] for inner in range(wide)]
        pieces = [
            jnp.dot(
                left_ref[b], source[slot_of[start + inner]], preferred_element_type=jnp.float32
            ).astype(jnp.bfloat16)
            for inner, b in enumerate(held)
        ]
        acc[...] += lax.dot_general(
            jnp.concatenate(pieces, axis=1),
            jnp.concatenate([right_ref[b] for b in held], axis=1),
            (((1,), (1,)), ((), ())),
            preferred_element_type=jnp.float32,
        )

    def full(group, carry):
        multiply(group * WIDE, WIDE)
        return carry

    groups = (count + WIDE // 2 - 1) // WIDE
    lax.fori_loop(0, groups, full, 0)
    rest = count - groups * WIDE
    for low, wide in ((0, 2), (2, 4)):

        @pl.when((rest > low) & (rest <= wide))
        def _():
            multiply(groups * WIDE, wide)


def load_kernel(left_hbm, right_hbm, left_ref, right_ref, sems):
    channels = left_ref.shape[0]
    step = max(1, channels // LOADS)
    copies = []
    for side, (source, target) in enumerate(((left_hbm, left_ref), (right_hbm, right_ref))):
        for at, low in enumerate(range(0, channels, step)):
            part = pl.ds(low, min(step, channels - low))
            copies.append(pltpu.make_async_copy(source.at[part], target.at[part], sems.at[side, at]))
    for copy in copies:
        copy.start()
    for copy in copies:
        copy.wait()


def own_kernel(scaled, places, *refs):
    kinds_ref, left_ref, right_ref, block_ref, acc = refs[:5]
    source, order, slot_of = refs[-3:]
    count = list_channels("own", places, kinds_ref, order, slot_of, 1)
    if scaled:
        block = wide_float(block_ref)
        unit = jnp.maximum(peak(block), SMALLEST)
        refs[5][...] = jnp.broadcast_to(unit, refs[5].shape)
        source[0] = (block * (1.0 / unit)).astype(jnp.bfloat16)
    else:
        source[0] = block_ref[...]
    source[1] = jnp.zeros(source.shape[1:], jnp.bfloat16)
    acc[...] = jnp.zeros_like(acc)
    multiply_listed(count, left_ref, right_ref, source, acc, order, slot_of)


def rest_kernel(which, scaled, passes, shares, slots, places, *refs):
    kinds_ref, left_ref, right_ref, own_ref = refs[:4]
    refs = refs[4:]
    if scaled:
        met_ref, refs = refs[0], refs[1:]
    first, refs = refs[:shares], refs[shares:]
    count_others = 0 if which == "first" else slots - 2
    others, refs = refs[:count_others], refs[count_others:]
    if passes:
        rows_ref, refs = refs[0], refs[1:]
    t_ref, refs = refs[0], refs[1:]
    if scaled:
        unit_ref, refs = refs[0], refs[1:]
    if passes:
        refs[0][...] = rows_ref[...]
        refs = refs[1:]
    acc, source, order, slot_of = refs
    count = list_channels(which, places, kinds_ref, order, slot_of, slots)
    if scaled:
        met = lane_of(first_row(met_ref), 0)
        unit = met
        for block in (*first, *others):
            unit = jnp.maximum(unit, peak(wide_float(block)))
        unit_ref[...] = jnp.broadcast_to(unit, unit_ref.shape)
        inverse = 1.0 / unit

    def scale(block):
        return (wide_float(block) * inverse).astype(jnp.bfloat16) if scaled else block[...]

    for step, block in enumerate(first):
        share = source.shape[1] // shares
        at = 0 if shares == 1 else jnp.abs(step - lax.axis_index("mpo"))
        source[1, pl.ds(pl.multiple_of(at * share, share), share), :] = scale(block)
    for slot, block in enumerate(others, 2):
        source[slot] = scale(block)
    source[slots] = jnp.zeros(source.shape[1:], jnp.bfloat16)
    acc[...] = own_ref[...] * (met * inverse) if scaled else own_ref[...]
    multiply_listed(count, left_ref, right_ref, source, acc, order, slot_of)
    t_ref[...] = acc[...].astype(t_ref.dtype)


def pass_kernel(block_ref, rows_ref, out_ref):
    out_ref[...] = block_ref[...]


def unpack_kernel(origin, block_ref, rows_ref, out_ref, sums_ref):
    share = out_ref.shape[0]
    out_ref[...] = block_ref[0:share, :]
    terms = block_ref[share : share + 2 * TILE, :].astype(jnp.float32)
    sums = terms[0:TILE, 0:128] + terms[0:TILE, 128:256] + terms[TILE : 2 * TILE, 0:128]
    row = lax.broadcasted_iota(jnp.int32, rows_ref.shape, 0)
    source = look_up(origin, here(), 0)
    sums_ref[...] = jnp.where(row == source, first_row(sums), rows_ref[...])


def take_kernel(block_ref, copy_ref, share_ref):
    copy_ref[...] = block_ref[...]
    share_ref[...] = block_ref[my_rows(share_ref.shape[0]), :]


def my_rows(share):
    return pl.ds(pl.multiple_of(lax.axis_index("mpo") * share, share), share)


def first_sums_kernel(share, *refs):
    parts, (psi_ref, unit_ref, w_ref, share_ref, rows_ref) = refs[:-5], refs[-5:]
    w = sum_parts(parts)
    unit = lane_of(first_row(unit_ref), 0)
    w_ref[...] = (w * unit).astype(jnp.bfloat16)
    share_ref[0:share, :] = w_ref[my_rows(share), :]
    v = wide_float(psi_ref) * (1.0 / unit)
    a = total(v * w)
    d = total(v * v)
    local = a / jnp.maximum(d, SMALLEST)
    r = w - local * v
    values = [a, d, local, total(r * v), total(r * r), unit]
    if share_ref.shape[0] > share:
        sums = pack(values, (TILE, 128))
        high = sums.astype(jnp.bfloat16)
        rest = sums - high.astype(jnp.float32)
        middle = rest.astype(jnp.bfloat16)
        low = (rest - middle.astype(jnp.float32)).astype(jnp.bfloat16)
        blank = jnp.zeros((2 * TILE, share_ref.shape[1]), jnp.bfloat16)
        share_ref[share : share + 2 * TILE, :] = blank
        share_ref[share : share + TILE, 0:128] = high
        share_ref[share : share + TILE, 128:256] = middle
        share_ref[share + TILE : share + 2 * TILE, 0:128] = low
        sums = high.astype(jnp.float32) + middle.astype(jnp.float32) + low.astype(jnp.float32)
        sums = jnp.broadcast_to(first_row(sums), rows_ref.shape)
    else:
        sums = pack(values, rows_ref.shape)
    row = lax.broadcasted_iota(jnp.int32, rows_ref.shape, 0)
    rows_ref[...] = jnp.where(row == here(), sums, 0.0)


def shrink(scal):
    return 1.0 / (jnp.abs(lane_of(scal, 0)) + lane_of(scal, 1))


def second_sums_kernel(entries, *refs):
    parts, refs = refs[:-9], refs[-9:]
    rows_ref, psi_ref, first_ref, unit_ref, wide_ref, w_ref, share_ref, v_ref, scal_ref = refs
    rows = rows_ref[...]
    a, d, local, p, q, unit = (lane_of(rows, lane) for lane in range(6))
    beta_0 = jnp.sqrt(column_sum(unit * unit * d) / entries + EPSILON)
    start_inverse = 1.0 / beta_0
    gain = unit * start_inverse
    alpha = column_sum(gain * (gain * a)) / entries
    off = local - alpha
    square = column_sum(gain * (gain * (q + off * (2.0 * p + off * d))))
    beta = jnp.sqrt(jnp.maximum(square, 0.0) / entries + EPSILON)
    inverse = 1.0 / beta
    scal = pack([alpha, beta, start_inverse], scal_ref.shape)
    scal_ref[...] = scal
    image = wide_float(first_ref) * start_inverse
    v_ref[...] = ((image - (alpha * start_inverse) * wide_float(psi_ref)) * inverse).astype(jnp.bfloat16)
    lift = lane_of(first_row(unit_ref), 0) * start_inverse
    w = (sum_parts(parts) * lift - alpha * image) * (inverse * shrink(first_row(scal)))
    wide_ref[...] = w
    w_ref[...] = w.astype(jnp.bfloat16)
    share_ref[...] = w_ref[my_rows(share_ref.shape[0]), :]


def third_sums_kernel(*refs):
    parts, refs = refs[:-8], refs[-8:]
    psi_ref, first_ref, v_ref, w_ref, scal_ref, r_ref, z_ref, rows_ref = refs
    scal = first_row(scal_ref)
    scale = shrink(scal)
    push = scale * lane_of(scal, 1) * lane_of(scal, 2)
    v, w = wide_float(v_ref), w_ref[...]
    vv, vw = total(v * v), total(v * w)
    local = vw / jnp.maximum(vv, SMALLEST)
    r = w - local * v - push * wide_float(psi_ref)
    z = sum_parts(parts) - (local / scale) * w - push * wide_float(first_ref)
    r_ref[...] = r
    z_ref[...] = z
    sums = [total(r * r), total(r * v), total(r * z), total(r * w)]
    sums += [total(z * v), total(z * w), total(z * z), total(w * w)]
    rows_ref[...] = pack([vv, vw, local] + sums, rows_ref.shape)


def final_kernel(entries, rows_ref, r_ref, z_ref, w_ref, v_ref, scal_ref, basis_ref, coef_ref):
    share = basis_ref.shape[2]
    mine = my_rows(share)
    vv, vw, local, rr, rv, rz, rw, zv, zw, zz, ww = (lane_of(rows_ref[...], i) for i in range(11))
    scal = first_row(scal_ref)
    scale = shrink(scal)
    inverse_scale = 1.0 / scale
    alpha_scaled = column_sum(vw) / entries
    off = local - alpha_scaled
    lift = off * inverse_scale
    square = column_sum(rr + off * (2.0 * rv + off * vv)) / entries
    beta_scaled = jnp.sqrt(jnp.maximum(square, 0.0) + scale * scale * EPSILON)
    inverse = 1.0 / beta_scaled
    mixed = column_sum(rz + lift * rw + off * (zv + lift * vw)) / entries
    alpha_3 = mixed * inverse * inverse
    r_v = column_sum(rv + off * vv) / entries
    z_v = column_sum(zv + lift * vw) / entries
    z_z = column_sum(zz + lift * (2.0 * zw + lift * ww)) / entries
    v_v = column_sum(vv) / entries
    beta_2 = beta_scaled * inverse_scale
    third = (z_z - 2.0 * alpha_3 * mixed + alpha_3 * alpha_3 * square) * inverse * inverse
    third += beta_2 * (beta_2 * v_v - 2.0 * inverse * (z_v - alpha_3 * r_v))
    beta_3 = jnp.sqrt(jnp.maximum(third, 0.0) + EPSILON)

    sector = here()
    row_of = lax.broadcasted_iota(jnp.int32, off.shape, 0)
    off_here = column_sum(jnp.where(row_of == sector, off, 0.0))
    v = v_ref[mine, :]
    v_wide = v.astype(jnp.float32)
    v_3 = (r_ref[mine, :] + off_here * v_wide) * inverse
    image = (z_ref[mine, :] + (off_here * inverse_scale) * w_ref[mine, :]) * inverse
    basis_ref[0, 0] = v
    basis_ref[1, 0] = v_3.astype(jnp.bfloat16)
    residual = image - alpha_3 * v_3 - beta_2 * v_wide
    basis_ref[2, 0] = (residual * (1.0 / beta_3)).astype(jnp.bfloat16)

    row = lax.broadcasted_iota(jnp.int32, coef_ref.shape, 0)
    column = lax.broadcasted_iota(jnp.int32, coef_ref.shape, 1)
    out = jnp.zeros(coef_ref.shape, jnp.float32)
    pairs = [(lane_of(scal, 0), lane_of(scal, 1)), (alpha_scaled * inverse_scale, beta_2), (alpha_3, beta_3)]
    for step, (a, b) in enumerate(pairs):
        out = jnp.where(column == step, jnp.where(row == 0, a, b), out)
    coef_ref[...] = out


def shards(wavefunction, env_left, env_right, channel_class):
    width = wavefunction.shape[1]
    ring = ("blk", "rep")
    parts = lax.axis_size("mpo")
    blocks = lax.axis_size("blk") * lax.axis_size("rep")
    entries = blocks * width * width
    permutes = routes(blocks)
    places, origins = slot_tables(permutes, blocks)
    slots = 1 + len(permutes)
    channels = channel_class.shape[0]
    psi, left, right = wavefunction[0], env_left[:, 0], env_right[:, 0]
    left, right = pl.pallas_call(
        load_kernel,
        out_shape=(jax.ShapeDtypeStruct(left.shape, left.dtype),) * 2,
        in_specs=[pl.BlockSpec(memory_space=pl.ANY)] * 2,
        out_specs=(VMEM, VMEM),
        scratch_shapes=[pltpu.SemaphoreType.DMA((2, channels))],
        compiler_params=pltpu.CompilerParams(vmem_limit_bytes=46 * MIB),
        name="load",
    )(left, right)
    rows_shape = jax.ShapeDtypeStruct((blocks, 128), jnp.float32)
    scalars = jax.ShapeDtypeStruct((8, 128), jnp.float32)
    wide = jax.ShapeDtypeStruct((width, width), jnp.float32)
    narrow = jax.ShapeDtypeStruct((width, width), jnp.bfloat16)
    share_shape = jax.ShapeDtypeStruct((width // parts, width), jnp.bfloat16)
    lists = [pltpu.SMEM((channels + WIDE,), jnp.int32)] * 2

    def call(kernel, name, outs, args, scratch=(), share=0, limit=4, weight=0):
        flops = int(4 * channels * max(share, weight) * width**3)
        cost = pl.CostEstimate(flops=flops, bytes_accessed=4 * width * width, transcendentals=0)
        listed = outs if isinstance(outs, tuple) else (outs,)
        first = SMEM if share else VMEM
        return pl.pallas_call(
            kernel,
            out_shape=outs,
            in_specs=[first] + [VMEM] * (len(args) - 1),
            out_specs=tuple(VMEM for _ in listed) if isinstance(outs, tuple) else VMEM,
            scratch_shapes=list(scratch),
            compiler_params=pltpu.CompilerParams(vmem_limit_bytes=limit * MIB),
            cost_estimate=cost,
            name=name,
        )(*args)

    def sources(count):
        return pltpu.VMEM((count + 1, width, width), jnp.bfloat16)

    def own(scaled, block):
        return call(
            functools.partial(own_kernel, scaled, places),
            "own",
            (wide,) + (scalars,) * scaled,
            (channel_class, left, right, block),
            [sources(1)] + lists,
            0.2,
            16,
        )

    def rest(which, summed, first, others, rows=None):
        scaled, passes = len(summed) > 1, rows is not None
        outs = (wide if which == "others" else narrow,) + (scalars,) * scaled + (rows_shape,) * passes
        args = [channel_class, left, right, *summed] + first + others + [rows] * passes
        return call(
            functools.partial(rest_kernel, which, scaled, passes, len(first), slots, places),
            "rest",
            outs,
            args,
            [pltpu.VMEM((width, width), jnp.float32), sources(slots)] + lists,
            0.4 if which == "rest" else 0.2,
            16,
        )

    def shift(block, pairs):
        return lax.ppermute(block, ring, pairs)

    carried = carried_rounds(permutes, blocks)
    rounds = [(ring, pairs) for pairs in carried or []]
    for axis in () if carried else ("rep", "blk"):
        size = lax.axis_size(axis)
        bits = [1 << i for i in range(size.bit_length() - 1)]
        if sum(bits) == size - 1:
            rounds += [(axis, [(i, i ^ bit) for i in range(size)]) for bit in bits]
        else:
            rounds += [(axis, None)]

    def add_round(rows, axis, pairs):
        if pairs is None:
            return lax.psum(rows, axis)
        return rows + lax.ppermute(rows, axis, pairs)

    def spread(block, share, rows=None, after=None):
        piece = shift(share, permutes[0])
        if rows is not None and carried:
            piece, rows = call(
                functools.partial(unpack_kernel, origins[1]),
                "unpack",
                (share_shape, rows_shape),
                (piece, rows),
            )
            rows = add_round(rows, *rounds[0])
        elif rows is not None:
            for step in rounds[:-1]:
                rows = add_round(rows, *step)
            piece = call(pass_kernel, "hold", share_shape, (piece, rows))
        elif after is not None:
            piece = call(pass_kernel, "hold", share_shape, (piece, after), weight=0.5)
        if parts == 2:
            first = [piece, lax.ppermute(piece, "mpo", [(0, 1), (1, 0)])]
        else:
            first = [lax.all_gather(piece, "mpo", axis=0, tiled=True)]
        return first, [shift(block, pairs) for pairs in permutes[1:]], rows

    def gather_parts(t):
        if parts == 2:
            return [t, lax.ppermute(t, "mpo", [(0, 1), (1, 0)])]
        held = lax.all_gather(t, "mpo")
        return [held[i] for i in range(parts)]

    def exchange(rows):
        return lax.all_to_all(rows, ring, 0, 0, tiled=True)

    psi, share_0 = call(take_kernel, "take", (narrow, share_shape), (psi,))
    first, others, _ = spread(psi, share_0, after=left)
    summed = rest("others", own(True, psi), [], others)
    t, unit = rest("first", summed, first, [])
    rows_in_share = width // parts + (2 * TILE if carried else 0)
    w_1, share_1, rows = call(
        functools.partial(first_sums_kernel, width // parts),
        "sums",
        (narrow, jax.ShapeDtypeStruct((rows_in_share, width), jnp.bfloat16), rows_shape),
        (*gather_parts(t), psi, unit),
    )
    first, others, rows = spread(w_1, share_1, rows)
    t, unit, rows = rest("rest", own(True, w_1), first, others, rows)
    rows = add_round(rows, *rounds[-1])
    w_wide, w_2, share_2, v_2, scal = call(
        functools.partial(second_sums_kernel, entries),
        "sums",
        (wide, narrow, share_shape, narrow, scalars),
        (*gather_parts(t), rows, psi, w_1, unit),
    )
    first, others, _ = spread(w_2, share_2, after=w_2)
    summed = rest("others", own(False, w_2), [], others)
    (t,) = rest("first", summed, first, [])
    r, z, rows = call(
        third_sums_kernel,
        "sums",
        (wide, wide, rows_shape),
        (*gather_parts(t), psi, w_1, v_2, w_wide, scal),
        limit=8,
    )
    return call(
        functools.partial(final_kernel, entries),
        "final",
        (
            jax.ShapeDtypeStruct((STEPS, 1, width // parts, width), jnp.bfloat16),
            jax.ShapeDtypeStruct((2, STEPS), jnp.float32),
        ),
        (exchange(rows), r, z, w_wide, v_2, scal),
    )


def solution(mesh):
    return jax.shard_map(
        shards,
        mesh=mesh,
        in_specs=(
            P(("groups", "blk", "rep"), None, None),
            P("mpo", ("groups", "blk", "rep"), None, None),
            P("mpo", ("groups", "blk", "rep"), None, None),
            P("mpo"),
        ),
        out_specs=(P(None, ("groups", "blk", "rep"), "mpo", None), P("groups", None)),
        check_vma=False,
    )
```

```python
import functools

import jax
import jax.numpy as jnp
from jax import lax
from jax.experimental import pallas as pl
from jax.experimental.pallas import tpu as pltpu
from jax.sharding import PartitionSpec as P

NS = 4
STEPS = 3
OFFSETS = (0, NS + 1, NS - 1, -(NS + 1), -(NS - 1))
EPSILON = 1e-06
WIDE = 8
SMALLEST = 1e-30
TILE = 16
MIB = 1024 * 1024
VMEM = pl.BlockSpec(memory_space=pltpu.VMEM)
SMEM = pl.BlockSpec(memory_space=pltpu.SMEM)


def reaches(kind, sector, blocks):
    source = sector - OFFSETS[kind]
    spin = sector % NS
    inside = (source >= 0) & (source < blocks)
    if kind in (1, 4):
        return inside & (spin >= 1)
    if kind in (2, 3):
        return inside & (spin <= NS - 2)
    return inside


def routes(blocks):
    degree, edges = [0] * blocks, []
    for kind in (1, 2):
        for k in range(blocks):
            if reaches(kind, k, blocks):
                edges.append((k - OFFSETS[kind], k))
                degree[k - OFFSETS[kind]] += 1
                degree[k] += 1
    edges.sort(key=lambda edge: degree[edge[0]] + degree[edge[1]])
    partner = [{} for _ in range(blocks)]

    def lowest(block):
        return next(c for c in range(len(edges)) if c not in partner[block])

    for a, b in edges:
        here_free, there_free = lowest(a), lowest(b)
        if here_free in partner[b]:
            path, block, colour = [b], b, here_free
            while colour in partner[block]:
                block = partner[block][colour]
                path.append(block)
                colour = there_free if colour == here_free else here_free
            for block in path:
                moved = {}
                for old, new in ((here_free, there_free), (there_free, here_free)):
                    if old in partner[block]:
                        moved[new] = partner[block].pop(old)
                partner[block].update(moved)
        partner[a][here_free], partner[b][here_free] = b, a
    colours = sorted({c for held in partner for c in held})
    permutes = [[(held[c], k) for k, held in enumerate(partner) if c in held] for c in colours]
    return sorted(permutes, key=len, reverse=True)


def slot_tables(permutes, blocks):
    origins = [{k: k for k in range(blocks)}] + [{k: s for s, k in pairs} for pairs in permutes]
    places = []
    for kind in range(5):
        place = {}
        for slot, origin in enumerate(origins):
            for k, source in origin.items():
                if source == k - OFFSETS[kind] and reaches(kind, k, blocks):
                    place[k] = slot
        places.append(place)
    return places, origins


def carried_rounds(permutes, blocks):
    if not permutes or blocks % 4:
        return None
    rounds = [dict(permutes[0])] + [{k: k ^ bit for k in range(blocks)} for bit in (1, 2)]
    held = [{k} for k in range(blocks)]
    for pairs in rounds:
        if sorted(pairs.values()) != list(range(blocks)):
            return None
        if any(held[source] & held[k] for source, k in pairs.items()):
            return None
        grown = list(held)
        for source, k in pairs.items():
            grown[k] = held[k] | held[source]
        held = grown
    if any(len(rows) < blocks for rows in held):
        return None
    return [sorted(pairs.items()) for pairs in rounds[1:]]


def look_up(table, sector, default):
    out = jnp.int32(default)
    for k, value in table.items():
        if value != default:
            out = jnp.where(sector == k, jnp.int32(value), out)
    return out


def here():
    return lax.axis_index("blk") * lax.axis_size("rep") + lax.axis_index("rep")


def lane_of(rows, lane):
    return rows[:, lane : lane + 1]


def pack(values, shape):
    lanes = lax.broadcasted_iota(jnp.int32, shape, 1)
    out = jnp.zeros(shape, jnp.float32)
    for place, value in enumerate(values):
        out = jnp.where(lanes == place, value, out)
    return out


def total(x):
    return jnp.sum(jnp.sum(x, axis=0, keepdims=True), axis=1, keepdims=True)


def column_sum(x):
    return jnp.sum(x, axis=0, keepdims=True)


def peak(x):
    return jnp.max(jnp.max(jnp.abs(x), axis=0, keepdims=True), axis=1, keepdims=True)


def wide_float(ref):
    return ref[...].astype(jnp.float32)


def sum_parts(parts):
    w = wide_float(parts[0])
    for part in parts[1:]:
        w += wide_float(part)
    return w


def first_row(ref):
    return ref[0:1, :]


def list_channels(which, places, kinds_ref, order, slot_of, idle):
    sector = here()
    low, high = {"own": (0, 0), "rest": (1, idle), "first": (1, 1), "others": (2, idle)}[which]
    slots = []
    for place in places:
        kept = {k: slot for k, slot in place.items() if low <= slot <= high}
        slots.append(look_up(kept, sector, -1))
    count = jnp.int32(0)
    for b in range(kinds_ref.shape[0]):
        kind = kinds_ref[b]
        slot = slots[0]
        for c in range(1, 5):
            slot = jnp.where(kind == c, slots[c], slot)
        order[count] = jnp.int32(b)
        slot_of[count] = slot
        count += jnp.where(slot >= 0, 1, 0)
    for extra in range(WIDE):
        order[count + extra] = jnp.int32(0)
        slot_of[count + extra] = jnp.int32(idle)
    return count


def multiply_listed(count, left_ref, right_ref, source, acc, order, slot_of):
    def multiply(start, wide):
        held = [order[start + inner] for inner in range(wide)]
        pieces = [
            jnp.dot(
                left_ref[b], source[slot_of[start + inner]], preferred_element_type=jnp.float32
            ).astype(jnp.bfloat16)
            for inner, b in enumerate(held)
        ]
        acc[...] += lax.dot_general(
            jnp.concatenate(pieces, axis=1),
            jnp.concatenate([right_ref[b] for b in held], axis=1),
            (((1,), (1,)), ((), ())),
            preferred_element_type=jnp.float32,
        )

    def full(group, carry):
        multiply(group * WIDE, WIDE)
        return carry

    groups = (count + WIDE // 2 - 1) // WIDE
    lax.fori_loop(0, groups, full, 0)
    rest = count - groups * WIDE
    for low, wide in ((0, 2), (2, 4)):

        @pl.when((rest > low) & (rest <= wide))
        def _():
            multiply(groups * WIDE, wide)


def load_kernel(places, kinds_ref, left_hbm, right_hbm, left_ref, right_ref, sems):
    sector = here()
    slots = [look_up(place, sector, -1) for place in places]

    def each(act):
        for b in range(left_ref.shape[0]):
            kind = kinds_ref[b]
            slot = slots[0]
            for c in range(1, 5):
                slot = jnp.where(kind == c, slots[c], slot)

            @pl.when((slot >= 0) | (b == 0))
            def _():
                act(pltpu.make_async_copy(left_hbm.at[b], left_ref.at[b], sems.at[0, b]))
                act(pltpu.make_async_copy(right_hbm.at[b], right_ref.at[b], sems.at[1, b]))

    each(lambda copy: copy.start())
    each(lambda copy: copy.wait())


def own_kernel(scaled, places, *refs):
    kinds_ref, left_ref, right_ref, block_ref, acc = refs[:5]
    source, order, slot_of = refs[-3:]
    count = list_channels("own", places, kinds_ref, order, slot_of, 1)
    if scaled:
        block = wide_float(block_ref)
        unit = jnp.maximum(peak(block), SMALLEST)
        refs[5][...] = jnp.broadcast_to(unit, refs[5].shape)
        source[0] = (block * (1.0 / unit)).astype(jnp.bfloat16)
    else:
        source[0] = block_ref[...]
    source[1] = jnp.zeros(source.shape[1:], jnp.bfloat16)
    acc[...] = jnp.zeros_like(acc)
    multiply_listed(count, left_ref, right_ref, source, acc, order, slot_of)


def rest_kernel(which, scaled, passes, shares, slots, places, *refs):
    kinds_ref, left_ref, right_ref, own_ref = refs[:4]
    refs = refs[4:]
    if scaled:
        met_ref, refs = refs[0], refs[1:]
    first, refs = refs[:shares], refs[shares:]
    count_others = 0 if which == "first" else slots - 2
    others, refs = refs[:count_others], refs[count_others:]
    if passes:
        rows_ref, refs = refs[0], refs[1:]
    t_ref, refs = refs[0], refs[1:]
    if scaled:
        unit_ref, refs = refs[0], refs[1:]
    if passes:
        refs[0][...] = rows_ref[...]
        refs = refs[1:]
    acc, source, order, slot_of = refs
    count = list_channels(which, places, kinds_ref, order, slot_of, slots)
    if scaled:
        met = lane_of(first_row(met_ref), 0)
        unit = met
        for block in (*first, *others):
            unit = jnp.maximum(unit, peak(wide_float(block)))
        unit_ref[...] = jnp.broadcast_to(unit, unit_ref.shape)
        inverse = 1.0 / unit

    def scale(block):
        return (wide_float(block) * inverse).astype(jnp.bfloat16) if scaled else block[...]

    for step, block in enumerate(first):
        share = source.shape[1] // shares
        at = 0 if shares == 1 else jnp.abs(step - lax.axis_index("mpo"))
        source[1, pl.ds(pl.multiple_of(at * share, share), share), :] = scale(block)
    for slot, block in enumerate(others, 2):
        source[slot] = scale(block)
    source[slots] = jnp.zeros(source.shape[1:], jnp.bfloat16)
    acc[...] = own_ref[...] * (met * inverse) if scaled else own_ref[...]
    multiply_listed(count, left_ref, right_ref, source, acc, order, slot_of)
    t_ref[...] = acc[...].astype(t_ref.dtype)


def pass_kernel(block_ref, rows_ref, out_ref):
    out_ref[...] = block_ref[...]


def unpack_kernel(origin, block_ref, rows_ref, out_ref, sums_ref):
    share = out_ref.shape[0]
    out_ref[...] = block_ref[0:share, :]
    terms = block_ref[share : share + 2 * TILE, :].astype(jnp.float32)
    sums = terms[0:TILE, 0:128] + terms[0:TILE, 128:256] + terms[TILE : 2 * TILE, 0:128]
    row = lax.broadcasted_iota(jnp.int32, rows_ref.shape, 0)
    source = look_up(origin, here(), 0)
    sums_ref[...] = jnp.where(row == source, first_row(sums), rows_ref[...])


def take_kernel(block_ref, copy_ref, share_ref):
    copy_ref[...] = block_ref[...]
    share_ref[...] = block_ref[my_rows(share_ref.shape[0]), :]


def my_rows(share):
    return pl.ds(pl.multiple_of(lax.axis_index("mpo") * share, share), share)


def first_sums_kernel(share, *refs):
    parts, (psi_ref, unit_ref, w_ref, share_ref, rows_ref) = refs[:-5], refs[-5:]
    w = sum_parts(parts)
    unit = lane_of(first_row(unit_ref), 0)
    w_ref[...] = (w * unit).astype(jnp.bfloat16)
    share_ref[0:share, :] = w_ref[my_rows(share), :]
    v = wide_float(psi_ref) * (1.0 / unit)
    a = total(v * w)
    d = total(v * v)
    local = a / jnp.maximum(d, SMALLEST)
    r = w - local * v
    values = [a, d, local, total(r * v), total(r * r), unit]
    if share_ref.shape[0] > share:
        sums = pack(values, (TILE, 128))
        high = sums.astype(jnp.bfloat16)
        rest = sums - high.astype(jnp.float32)
        middle = rest.astype(jnp.bfloat16)
        low = (rest - middle.astype(jnp.float32)).astype(jnp.bfloat16)
        blank = jnp.zeros((2 * TILE, share_ref.shape[1]), jnp.bfloat16)
        share_ref[share : share + 2 * TILE, :] = blank
        share_ref[share : share + TILE, 0:128] = high
        share_ref[share : share + TILE, 128:256] = middle
        share_ref[share + TILE : share + 2 * TILE, 0:128] = low
        sums = high.astype(jnp.float32) + middle.astype(jnp.float32) + low.astype(jnp.float32)
        sums = jnp.broadcast_to(first_row(sums), rows_ref.shape)
    else:
        sums = pack(values, rows_ref.shape)
    row = lax.broadcasted_iota(jnp.int32, rows_ref.shape, 0)
    rows_ref[...] = jnp.where(row == here(), sums, 0.0)


def shrink(scal):
    return 1.0 / (jnp.abs(lane_of(scal, 0)) + lane_of(scal, 1))


def second_sums_kernel(entries, *refs):
    parts, refs = refs[:-9], refs[-9:]
    rows_ref, psi_ref, first_ref, unit_ref, wide_ref, w_ref, share_ref, v_ref, scal_ref = refs
    rows = rows_ref[...]
    a, d, local, p, q, unit = (lane_of(rows, lane) for lane in range(6))
    beta_0 = jnp.sqrt(column_sum(unit * unit * d) / entries + EPSILON)
    start_inverse = 1.0 / beta_0
    gain = unit * start_inverse
    alpha = column_sum(gain * (gain * a)) / entries
    off = local - alpha
    square = column_sum(gain * (gain * (q + off * (2.0 * p + off * d))))
    beta = jnp.sqrt(jnp.maximum(square, 0.0) / entries + EPSILON)
    inverse = 1.0 / beta
    scal = pack([alpha, beta, start_inverse], scal_ref.shape)
    scal_ref[...] = scal
    image = wide_float(first_ref) * start_inverse
    v_ref[...] = ((image - (alpha * start_inverse) * wide_float(psi_ref)) * inverse).astype(jnp.bfloat16)
    lift = lane_of(first_row(unit_ref), 0) * start_inverse
    w = (sum_parts(parts) * lift - alpha * image) * (inverse * shrink(first_row(scal)))
    wide_ref[...] = w
    w_ref[...] = w.astype(jnp.bfloat16)
    share_ref[...] = w_ref[my_rows(share_ref.shape[0]), :]


def third_sums_kernel(*refs):
    parts, refs = refs[:-8], refs[-8:]
    psi_ref, first_ref, v_ref, w_ref, scal_ref, r_ref, z_ref, rows_ref = refs
    scal = first_row(scal_ref)
    scale = shrink(scal)
    push = scale * lane_of(scal, 1) * lane_of(scal, 2)
    v, w = wide_float(v_ref), w_ref[...]
    vv, vw = total(v * v), total(v * w)
    local = vw / jnp.maximum(vv, SMALLEST)
    r = w - local * v - push * wide_float(psi_ref)
    z = sum_parts(parts) - (local / scale) * w - push * wide_float(first_ref)
    r_ref[...] = r
    z_ref[...] = z
    sums = [total(r * r), total(r * v), total(r * z), total(r * w)]
    sums += [total(z * v), total(z * w), total(z * z), total(w * w)]
    rows_ref[...] = pack([vv, vw, local] + sums, rows_ref.shape)


def final_kernel(entries, rows_ref, r_ref, z_ref, w_ref, v_ref, scal_ref, basis_ref, coef_ref):
    share = basis_ref.shape[2]
    mine = my_rows(share)
    vv, vw, local, rr, rv, rz, rw, zv, zw, zz, ww = (lane_of(rows_ref[...], i) for i in range(11))
    scal = first_row(scal_ref)
    scale = shrink(scal)
    inverse_scale = 1.0 / scale
    alpha_scaled = column_sum(vw) / entries
    off = local - alpha_scaled
    lift = off * inverse_scale
    square = column_sum(rr + off * (2.0 * rv + off * vv)) / entries
    beta_scaled = jnp.sqrt(jnp.maximum(square, 0.0) + scale * scale * EPSILON)
    inverse = 1.0 / beta_scaled
    mixed = column_sum(rz + lift * rw + off * (zv + lift * vw)) / entries
    alpha_3 = mixed * inverse * inverse
    r_v = column_sum(rv + off * vv) / entries
    z_v = column_sum(zv + lift * vw) / entries
    z_z = column_sum(zz + lift * (2.0 * zw + lift * ww)) / entries
    v_v = column_sum(vv) / entries
    beta_2 = beta_scaled * inverse_scale
    third = (z_z - 2.0 * alpha_3 * mixed + alpha_3 * alpha_3 * square) * inverse * inverse
    third += beta_2 * (beta_2 * v_v - 2.0 * inverse * (z_v - alpha_3 * r_v))
    beta_3 = jnp.sqrt(jnp.maximum(third, 0.0) + EPSILON)

    sector = here()
    row_of = lax.broadcasted_iota(jnp.int32, off.shape, 0)
    off_here = column_sum(jnp.where(row_of == sector, off, 0.0))
    v = v_ref[mine, :]
    v_wide = v.astype(jnp.float32)
    v_3 = (r_ref[mine, :] + off_here * v_wide) * inverse
    image = (z_ref[mine, :] + (off_here * inverse_scale) * w_ref[mine, :]) * inverse
    basis_ref[0, 0] = v
    basis_ref[1, 0] = v_3.astype(jnp.bfloat16)
    residual = image - alpha_3 * v_3 - beta_2 * v_wide
    basis_ref[2, 0] = (residual * (1.0 / beta_3)).astype(jnp.bfloat16)

    row = lax.broadcasted_iota(jnp.int32, coef_ref.shape, 0)
    column = lax.broadcasted_iota(jnp.int32, coef_ref.shape, 1)
    out = jnp.zeros(coef_ref.shape, jnp.float32)
    pairs = [(lane_of(scal, 0), lane_of(scal, 1)), (alpha_scaled * inverse_scale, beta_2), (alpha_3, beta_3)]
    for step, (a, b) in enumerate(pairs):
        out = jnp.where(column == step, jnp.where(row == 0, a, b), out)
    coef_ref[...] = out


def shards(wavefunction, env_left, env_right, channel_class):
    width = wavefunction.shape[1]
    ring = ("blk", "rep")
    parts = lax.axis_size("mpo")
    blocks = lax.axis_size("blk") * lax.axis_size("rep")
    entries = blocks * width * width
    permutes = routes(blocks)
    places, origins = slot_tables(permutes, blocks)
    slots = 1 + len(permutes)
    channels = channel_class.shape[0]
    psi, left, right = wavefunction[0], env_left[:, 0], env_right[:, 0]
    left, right = pl.pallas_call(
        functools.partial(load_kernel, places),
        out_shape=(jax.ShapeDtypeStruct(left.shape, left.dtype),) * 2,
        in_specs=[SMEM] + [pl.BlockSpec(memory_space=pl.ANY)] * 2,
        out_specs=(VMEM, VMEM),
        scratch_shapes=[pltpu.SemaphoreType.DMA((2, channels))],
        compiler_params=pltpu.CompilerParams(vmem_limit_bytes=46 * MIB),
        name="load",
    )(channel_class, left, right)
    rows_shape = jax.ShapeDtypeStruct((blocks, 128), jnp.float32)
    scalars = jax.ShapeDtypeStruct((8, 128), jnp.float32)
    wide = jax.ShapeDtypeStruct((width, width), jnp.float32)
    narrow = jax.ShapeDtypeStruct((width, width), jnp.bfloat16)
    share_shape = jax.ShapeDtypeStruct((width // parts, width), jnp.bfloat16)
    lists = [pltpu.SMEM((channels + WIDE,), jnp.int32)] * 2

    def call(kernel, name, outs, args, scratch=(), share=0, limit=4, weight=0):
        flops = int(4 * channels * max(share, weight) * width**3)
        cost = pl.CostEstimate(flops=flops, bytes_accessed=4 * width * width, transcendentals=0)
        listed = outs if isinstance(outs, tuple) else (outs,)
        first = SMEM if share else VMEM
        return pl.pallas_call(
            kernel,
            out_shape=outs,
            in_specs=[first] + [VMEM] * (len(args) - 1),
            out_specs=tuple(VMEM for _ in listed) if isinstance(outs, tuple) else VMEM,
            scratch_shapes=list(scratch),
            compiler_params=pltpu.CompilerParams(vmem_limit_bytes=limit * MIB),
            cost_estimate=cost,
            name=name,
        )(*args)

    def sources(count):
        return pltpu.VMEM((count + 1, width, width), jnp.bfloat16)

    def own(scaled, block):
        return call(
            functools.partial(own_kernel, scaled, places),
            "own",
            (wide,) + (scalars,) * scaled,
            (channel_class, left, right, block),
            [sources(1)] + lists,
            0.2,
            16,
        )

    def rest(which, summed, first, others, rows=None):
        scaled, passes = len(summed) > 1, rows is not None
        outs = (wide if which == "others" else narrow,) + (scalars,) * scaled + (rows_shape,) * passes
        args = [channel_class, left, right, *summed] + first + others + [rows] * passes
        return call(
            functools.partial(rest_kernel, which, scaled, passes, len(first), slots, places),
            "rest",
            outs,
            args,
            [pltpu.VMEM((width, width), jnp.float32), sources(slots)] + lists,
            0.4 if which == "rest" else 0.2,
            16,
        )

    def shift(block, pairs):
        return lax.ppermute(block, ring, pairs)

    carried = carried_rounds(permutes, blocks)
    rounds = [(ring, pairs) for pairs in carried or []]
    for axis in () if carried else ("rep", "blk"):
        size = lax.axis_size(axis)
        bits = [1 << i for i in range(size.bit_length() - 1)]
        if sum(bits) == size - 1:
            rounds += [(axis, [(i, i ^ bit) for i in range(size)]) for bit in bits]
        else:
            rounds += [(axis, None)]

    def add_round(rows, axis, pairs):
        if pairs is None:
            return lax.psum(rows, axis)
        return rows + lax.ppermute(rows, axis, pairs)

    def spread(block, share, rows=None, after=None):
        piece = shift(share, permutes[0])
        if rows is not None and carried:
            piece, rows = call(
                functools.partial(unpack_kernel, origins[1]),
                "unpack",
                (share_shape, rows_shape),
                (piece, rows),
            )
            rows = add_round(rows, *rounds[0])
        elif rows is not None:
            for step in rounds[:-1]:
                rows = add_round(rows, *step)
            piece = call(pass_kernel, "hold", share_shape, (piece, rows))
        elif after is not None:
            piece = call(pass_kernel, "hold", share_shape, (piece, after), weight=0.5)
        if parts == 2:
            first = [piece, lax.ppermute(piece, "mpo", [(0, 1), (1, 0)])]
        else:
            first = [lax.all_gather(piece, "mpo", axis=0, tiled=True)]
        return first, [shift(block, pairs) for pairs in permutes[1:]], rows

    def gather_parts(t):
        if parts == 2:
            return [t, lax.ppermute(t, "mpo", [(0, 1), (1, 0)])]
        held = lax.all_gather(t, "mpo")
        return [held[i] for i in range(parts)]

    def exchange(rows):
        return lax.all_to_all(rows, ring, 0, 0, tiled=True)

    psi, share_0 = call(take_kernel, "take", (narrow, share_shape), (psi,))
    first, others, _ = spread(psi, share_0, after=left)
    summed = rest("others", own(True, psi), [], others)
    t, unit = rest("first", summed, first, [])
    rows_in_share = width // parts + (2 * TILE if carried else 0)
    w_1, share_1, rows = call(
        functools.partial(first_sums_kernel, width // parts),
        "sums",
        (narrow, jax.ShapeDtypeStruct((rows_in_share, width), jnp.bfloat16), rows_shape),
        (*gather_parts(t), psi, unit),
    )
    first, others, rows = spread(w_1, share_1, rows)
    t, unit, rows = rest("rest", own(True, w_1), first, others, rows)
    rows = add_round(rows, *rounds[-1])
    w_wide, w_2, share_2, v_2, scal = call(
        functools.partial(second_sums_kernel, entries),
        "sums",
        (wide, narrow, share_shape, narrow, scalars),
        (*gather_parts(t), rows, psi, w_1, unit),
    )
    first, others, _ = spread(w_2, share_2, after=w_2)
    summed = rest("others", own(False, w_2), [], others)
    (t,) = rest("first", summed, first, [])
    r, z, rows = call(
        third_sums_kernel,
        "sums",
        (wide, wide, rows_shape),
        (*gather_parts(t), psi, w_1, v_2, w_wide, scal),
        limit=8,
    )
    return call(
        functools.partial(final_kernel, entries),
        "final",
        (
            jax.ShapeDtypeStruct((STEPS, 1, width // parts, width), jnp.bfloat16),
            jax.ShapeDtypeStruct((2, STEPS), jnp.float32),
        ),
        (exchange(rows), r, z, w_wide, v_2, scal),
    )


def solution(mesh):
    return jax.shard_map(
        shards,
        mesh=mesh,
        in_specs=(
            P(("groups", "blk", "rep"), None, None),
            P("mpo", ("groups", "blk", "rep"), None, None),
            P("mpo", ("groups", "blk", "rep"), None, None),
            P("mpo"),
        ),
        out_specs=(P(None, ("groups", "blk", "rep"), "mpo", None), P("groups", None)),
        check_vma=False,
    )
```

```python
import functools

import jax
import jax.numpy as jnp
from jax import lax
from jax.experimental import pallas as pl
from jax.experimental.pallas import tpu as pltpu
from jax.sharding import PartitionSpec as P

NS = 4
STEPS = 3
OFFSETS = (0, NS + 1, NS - 1, -(NS + 1), -(NS - 1))
EPSILON = 1e-06
WIDE = 8
SMALLEST = 1e-30
TILE = 16
MIB = 1024 * 1024
VMEM = pl.BlockSpec(memory_space=pltpu.VMEM)
SMEM = pl.BlockSpec(memory_space=pltpu.SMEM)


def reaches(kind, sector, blocks):
    source = sector - OFFSETS[kind]
    spin = sector % NS
    inside = (source >= 0) & (source < blocks)
    if kind in (1, 4):
        return inside & (spin >= 1)
    if kind in (2, 3):
        return inside & (spin <= NS - 2)
    return inside


def routes(blocks):
    degree, edges = [0] * blocks, []
    for kind in (1, 2):
        for k in range(blocks):
            if reaches(kind, k, blocks):
                edges.append((k - OFFSETS[kind], k))
                degree[k - OFFSETS[kind]] += 1
                degree[k] += 1
    edges.sort(key=lambda edge: degree[edge[0]] + degree[edge[1]])
    partner = [{} for _ in range(blocks)]

    def lowest(block):
        return next(c for c in range(len(edges)) if c not in partner[block])

    for a, b in edges:
        here_free, there_free = lowest(a), lowest(b)
        if here_free in partner[b]:
            path, block, colour = [b], b, here_free
            while colour in partner[block]:
                block = partner[block][colour]
                path.append(block)
                colour = there_free if colour == here_free else here_free
            for block in path:
                moved = {}
                for old, new in ((here_free, there_free), (there_free, here_free)):
                    if old in partner[block]:
                        moved[new] = partner[block].pop(old)
                partner[block].update(moved)
        partner[a][here_free], partner[b][here_free] = b, a
    colours = sorted({c for held in partner for c in held})
    permutes = [[(held[c], k) for k, held in enumerate(partner) if c in held] for c in colours]
    return sorted(permutes, key=len, reverse=True)


def slot_tables(permutes, blocks):
    origins = [{k: k for k in range(blocks)}] + [{k: s for s, k in pairs} for pairs in permutes]
    places = []
    for kind in range(5):
        place = {}
        for slot, origin in enumerate(origins):
            for k, source in origin.items():
                if source == k - OFFSETS[kind] and reaches(kind, k, blocks):
                    place[k] = slot
        places.append(place)
    return places, origins


def carried_rounds(permutes, blocks):
    if not permutes or blocks % 4:
        return None
    rounds = [dict(permutes[0])] + [{k: k ^ bit for k in range(blocks)} for bit in (1, 2)]
    held = [{k} for k in range(blocks)]
    for pairs in rounds:
        if sorted(pairs.values()) != list(range(blocks)):
            return None
        if any(held[source] & held[k] for source, k in pairs.items()):
            return None
        grown = list(held)
        for source, k in pairs.items():
            grown[k] = held[k] | held[source]
        held = grown
    if any(len(rows) < blocks for rows in held):
        return None
    return [sorted(pairs.items()) for pairs in rounds[1:]]


def look_up(table, sector, default):
    out = jnp.int32(default)
    for k, value in table.items():
        if value != default:
            out = jnp.where(sector == k, jnp.int32(value), out)
    return out


def here():
    return lax.axis_index("blk") * lax.axis_size("rep") + lax.axis_index("rep")


def lane_of(rows, lane):
    return rows[:, lane : lane + 1]


def pack(values, shape):
    lanes = lax.broadcasted_iota(jnp.int32, shape, 1)
    out = jnp.zeros(shape, jnp.float32)
    for place, value in enumerate(values):
        out = jnp.where(lanes == place, value, out)
    return out


def total(x):
    return jnp.sum(jnp.sum(x, axis=0, keepdims=True), axis=1, keepdims=True)


def column_sum(x):
    return jnp.sum(x, axis=0, keepdims=True)


def peak(x):
    return jnp.max(jnp.max(jnp.abs(x), axis=0, keepdims=True), axis=1, keepdims=True)


def wide_float(ref):
    return ref[...].astype(jnp.float32)


def sum_parts(parts):
    w = wide_float(parts[0])
    for part in parts[1:]:
        w += wide_float(part)
    return w


def first_row(ref):
    return ref[0:1, :]


def list_channels(which, places, kinds_ref, order, slot_of, idle):
    sector = here()
    low, high = {"own": (0, 0), "rest": (1, idle), "first": (1, 1), "others": (2, idle)}[which]
    slots = []
    for place in places:
        kept = {k: slot for k, slot in place.items() if low <= slot <= high}
        slots.append(look_up(kept, sector, -1))
    count = jnp.int32(0)
    for b in range(kinds_ref.shape[0]):
        kind = kinds_ref[b]
        slot = slots[0]
        for c in range(1, 5):
            slot = jnp.where(kind == c, slots[c], slot)
        order[count] = jnp.int32(b)
        slot_of[count] = slot
        count += jnp.where(slot >= 0, 1, 0)
    for extra in range(WIDE):
        order[count + extra] = jnp.int32(0)
        slot_of[count + extra] = jnp.int32(idle)
    return count


def multiply_listed(count, left_ref, right_ref, source, acc, order, slot_of):
    def multiply(start, wide):
        held = [order[start + inner] for inner in range(wide)]
        pieces = [
            jnp.dot(
                left_ref[b], source[slot_of[start + inner]], preferred_element_type=jnp.float32
            ).astype(jnp.bfloat16)
            for inner, b in enumerate(held)
        ]
        acc[...] += lax.dot_general(
            jnp.concatenate(pieces, axis=1),
            jnp.concatenate([right_ref[b] for b in held], axis=1),
            (((1,), (1,)), ((), ())),
            preferred_element_type=jnp.float32,
        )

    def full(group, carry):
        multiply(group * WIDE, WIDE)
        return carry

    groups = (count + WIDE // 2 - 1) // WIDE
    lax.fori_loop(0, groups, full, 0)
    rest = count - groups * WIDE
    for low, wide in ((0, 2), (2, 4)):

        @pl.when((rest > low) & (rest <= wide))
        def _():
            multiply(groups * WIDE, wide)


def own_kernel(scaled, places, *refs):
    kinds_ref, left_ref, right_ref, block_ref, acc = refs[:5]
    source, order, slot_of = refs[-3:]
    count = list_channels("own", places, kinds_ref, order, slot_of, 1)
    if scaled:
        block = wide_float(block_ref)
        unit = jnp.maximum(peak(block), SMALLEST)
        refs[5][...] = jnp.broadcast_to(unit, refs[5].shape)
        source[0] = (block * (1.0 / unit)).astype(jnp.bfloat16)
    else:
        source[0] = block_ref[...]
    source[1] = jnp.zeros(source.shape[1:], jnp.bfloat16)
    acc[...] = jnp.zeros_like(acc)
    multiply_listed(count, left_ref, right_ref, source, acc, order, slot_of)


def rest_kernel(which, scaled, passes, shares, slots, places, *refs):
    kinds_ref, left_ref, right_ref, own_ref = refs[:4]
    refs = refs[4:]
    if scaled:
        met_ref, refs = refs[0], refs[1:]
    first, refs = refs[:shares], refs[shares:]
    count_others = 0 if which == "first" else slots - 2
    others, refs = refs[:count_others], refs[count_others:]
    if passes:
        rows_ref, refs = refs[0], refs[1:]
    t_ref, refs = refs[0], refs[1:]
    if scaled:
        unit_ref, refs = refs[0], refs[1:]
    if passes:
        refs[0][...] = rows_ref[...]
        refs = refs[1:]
    acc, source, order, slot_of = refs
    count = list_channels(which, places, kinds_ref, order, slot_of, slots)
    if scaled:
        met = lane_of(first_row(met_ref), 0)
        unit = met
        for block in (*first, *others):
            unit = jnp.maximum(unit, peak(wide_float(block)))
        unit_ref[...] = jnp.broadcast_to(unit, unit_ref.shape)
        inverse = 1.0 / unit

    def scale(block):
        return (wide_float(block) * inverse).astype(jnp.bfloat16) if scaled else block[...]

    for step, block in enumerate(first):
        share = source.shape[1] // shares
        at = 0 if shares == 1 else jnp.abs(step - lax.axis_index("mpo"))
        source[1, pl.ds(pl.multiple_of(at * share, share), share), :] = scale(block)
    for slot, block in enumerate(others, 2):
        source[slot] = scale(block)
    source[slots] = jnp.zeros(source.shape[1:], jnp.bfloat16)
    acc[...] = own_ref[...] * (met * inverse) if scaled else own_ref[...]
    multiply_listed(count, left_ref, right_ref, source, acc, order, slot_of)
    t_ref[...] = acc[...].astype(t_ref.dtype)


def pass_kernel(block_ref, rows_ref, out_ref):
    out_ref[...] = block_ref[...]


def unpack_kernel(origin, block_ref, rows_ref, out_ref, sums_ref):
    share = out_ref.shape[0]
    out_ref[...] = block_ref[0:share, :]
    terms = block_ref[share : share + 2 * TILE, :].astype(jnp.float32)
    sums = terms[0:TILE, 0:128] + terms[0:TILE, 128:256] + terms[TILE : 2 * TILE, 0:128]
    row = lax.broadcasted_iota(jnp.int32, rows_ref.shape, 0)
    source = look_up(origin, here(), 0)
    sums_ref[...] = jnp.where(row == source, first_row(sums), rows_ref[...])


def take_kernel(block_ref, copy_ref, share_ref):
    copy_ref[...] = block_ref[...]
    share_ref[...] = block_ref[my_rows(share_ref.shape[0]), :]


def my_rows(share):
    return pl.ds(pl.multiple_of(lax.axis_index("mpo") * share, share), share)


def first_sums_kernel(share, *refs):
    parts, (psi_ref, unit_ref, w_ref, share_ref, rows_ref) = refs[:-5], refs[-5:]
    w = sum_parts(parts)
    unit = lane_of(first_row(unit_ref), 0)
    w_ref[...] = (w * unit).astype(jnp.bfloat16)
    share_ref[0:share, :] = w_ref[my_rows(share), :]
    v = wide_float(psi_ref) * (1.0 / unit)
    a = total(v * w)
    d = total(v * v)
    local = a / jnp.maximum(d, SMALLEST)
    r = w - local * v
    values = [a, d, local, total(r * v), total(r * r), unit]
    if share_ref.shape[0] > share:
        sums = pack(values, (TILE, 128))
        high = sums.astype(jnp.bfloat16)
        rest = sums - high.astype(jnp.float32)
        middle = rest.astype(jnp.bfloat16)
        low = (rest - middle.astype(jnp.float32)).astype(jnp.bfloat16)
        blank = jnp.zeros((2 * TILE, share_ref.shape[1]), jnp.bfloat16)
        share_ref[share : share + 2 * TILE, :] = blank
        share_ref[share : share + TILE, 0:128] = high
        share_ref[share : share + TILE, 128:256] = middle
        share_ref[share + TILE : share + 2 * TILE, 0:128] = low
        sums = high.astype(jnp.float32) + middle.astype(jnp.float32) + low.astype(jnp.float32)
        sums = jnp.broadcast_to(first_row(sums), rows_ref.shape)
    else:
        sums = pack(values, rows_ref.shape)
    row = lax.broadcasted_iota(jnp.int32, rows_ref.shape, 0)
    rows_ref[...] = jnp.where(row == here(), sums, 0.0)


def shrink(scal):
    return 1.0 / (jnp.abs(lane_of(scal, 0)) + lane_of(scal, 1))


def second_sums_kernel(entries, *refs):
    parts, refs = refs[:-9], refs[-9:]
    rows_ref, psi_ref, first_ref, unit_ref, wide_ref, w_ref, share_ref, v_ref, scal_ref = refs
    rows = rows_ref[...]
    a, d, local, p, q, unit = (lane_of(rows, lane) for lane in range(6))
    beta_0 = jnp.sqrt(column_sum(unit * unit * d) / entries + EPSILON)
    start_inverse = 1.0 / beta_0
    gain = unit * start_inverse
    alpha = column_sum(gain * (gain * a)) / entries
    off = local - alpha
    square = column_sum(gain * (gain * (q + off * (2.0 * p + off * d))))
    beta = jnp.sqrt(jnp.maximum(square, 0.0) / entries + EPSILON)
    inverse = 1.0 / beta
    scal = pack([alpha, beta, start_inverse], scal_ref.shape)
    scal_ref[...] = scal
    image = wide_float(first_ref) * start_inverse
    v_ref[...] = ((image - (alpha * start_inverse) * wide_float(psi_ref)) * inverse).astype(jnp.bfloat16)
    lift = lane_of(first_row(unit_ref), 0) * start_inverse
    w = (sum_parts(parts) * lift - alpha * image) * (inverse * shrink(first_row(scal)))
    wide_ref[...] = w
    w_ref[...] = w.astype(jnp.bfloat16)
    share_ref[...] = w_ref[my_rows(share_ref.shape[0]), :]


def third_sums_kernel(*refs):
    parts, refs = refs[:-8], refs[-8:]
    psi_ref, first_ref, v_ref, w_ref, scal_ref, r_ref, z_ref, rows_ref = refs
    scal = first_row(scal_ref)
    scale = shrink(scal)
    push = scale * lane_of(scal, 1) * lane_of(scal, 2)
    v, w = wide_float(v_ref), w_ref[...]
    vv, vw = total(v * v), total(v * w)
    local = vw / jnp.maximum(vv, SMALLEST)
    r = w - local * v - push * wide_float(psi_ref)
    z = sum_parts(parts) - (local / scale) * w - push * wide_float(first_ref)
    r_ref[...] = r
    z_ref[...] = z
    sums = [total(r * r), total(r * v), total(r * z), total(r * w)]
    sums += [total(z * v), total(z * w), total(z * z), total(w * w)]
    rows_ref[...] = pack([vv, vw, local] + sums, rows_ref.shape)


def final_kernel(entries, rows_ref, r_ref, z_ref, w_ref, v_ref, scal_ref, basis_ref, coef_ref):
    share = basis_ref.shape[2]
    mine = my_rows(share)
    vv, vw, local, rr, rv, rz, rw, zv, zw, zz, ww = (lane_of(rows_ref[...], i) for i in range(11))
    scal = first_row(scal_ref)
    scale = shrink(scal)
    inverse_scale = 1.0 / scale
    alpha_scaled = column_sum(vw) / entries
    off = local - alpha_scaled
    lift = off * inverse_scale
    square = column_sum(rr + off * (2.0 * rv + off * vv)) / entries
    beta_scaled = jnp.sqrt(jnp.maximum(square, 0.0) + scale * scale * EPSILON)
    inverse = 1.0 / beta_scaled
    mixed = column_sum(rz + lift * rw + off * (zv + lift * vw)) / entries
    alpha_3 = mixed * inverse * inverse
    r_v = column_sum(rv + off * vv) / entries
    z_v = column_sum(zv + lift * vw) / entries
    z_z = column_sum(zz + lift * (2.0 * zw + lift * ww)) / entries
    v_v = column_sum(vv) / entries
    beta_2 = beta_scaled * inverse_scale
    third = (z_z - 2.0 * alpha_3 * mixed + alpha_3 * alpha_3 * square) * inverse * inverse
    third += beta_2 * (beta_2 * v_v - 2.0 * inverse * (z_v - alpha_3 * r_v))
    beta_3 = jnp.sqrt(jnp.maximum(third, 0.0) + EPSILON)

    sector = here()
    row_of = lax.broadcasted_iota(jnp.int32, off.shape, 0)
    off_here = column_sum(jnp.where(row_of == sector, off, 0.0))
    v = v_ref[mine, :]
    v_wide = v.astype(jnp.float32)
    v_3 = (r_ref[mine, :] + off_here * v_wide) * inverse
    image = (z_ref[mine, :] + (off_here * inverse_scale) * w_ref[mine, :]) * inverse
    basis_ref[0, 0] = v
    basis_ref[1, 0] = v_3.astype(jnp.bfloat16)
    residual = image - alpha_3 * v_3 - beta_2 * v_wide
    basis_ref[2, 0] = (residual * (1.0 / beta_3)).astype(jnp.bfloat16)

    row = lax.broadcasted_iota(jnp.int32, coef_ref.shape, 0)
    column = lax.broadcasted_iota(jnp.int32, coef_ref.shape, 1)
    out = jnp.zeros(coef_ref.shape, jnp.float32)
    pairs = [(lane_of(scal, 0), lane_of(scal, 1)), (alpha_scaled * inverse_scale, beta_2), (alpha_3, beta_3)]
    for step, (a, b) in enumerate(pairs):
        out = jnp.where(column == step, jnp.where(row == 0, a, b), out)
    coef_ref[...] = out


def shards(wavefunction, env_left, env_right, channel_class):
    width = wavefunction.shape[1]
    ring = ("blk", "rep")
    parts = lax.axis_size("mpo")
    blocks = lax.axis_size("blk") * lax.axis_size("rep")
    entries = blocks * width * width
    permutes = routes(blocks)
    places, origins = slot_tables(permutes, blocks)
    slots = 1 + len(permutes)
    channels = channel_class.shape[0]
    psi, left, right = wavefunction[0], env_left[:, 0], env_right[:, 0]
    rows_shape = jax.ShapeDtypeStruct((blocks, 128), jnp.float32)
    scalars = jax.ShapeDtypeStruct((8, 128), jnp.float32)
    wide = jax.ShapeDtypeStruct((width, width), jnp.float32)
    narrow = jax.ShapeDtypeStruct((width, width), jnp.bfloat16)
    share_shape = jax.ShapeDtypeStruct((width // parts, width), jnp.bfloat16)
    lists = [pltpu.SMEM((channels + WIDE,), jnp.int32)] * 2

    def call(kernel, name, outs, args, scratch=(), share=0, limit=4, weight=0):
        flops = int(4 * channels * max(share, weight) * width**3)
        cost = pl.CostEstimate(flops=flops, bytes_accessed=4 * width * width, transcendentals=0)
        listed = outs if isinstance(outs, tuple) else (outs,)
        first = SMEM if share else VMEM
        return pl.pallas_call(
            kernel,
            out_shape=outs,
            in_specs=[first] + [VMEM] * (len(args) - 1),
            out_specs=tuple(VMEM for _ in listed) if isinstance(outs, tuple) else VMEM,
            scratch_shapes=list(scratch),
            compiler_params=pltpu.CompilerParams(vmem_limit_bytes=limit * MIB),
            cost_estimate=cost,
            name=name,
        )(*args)

    def sources(count):
        return pltpu.VMEM((count + 1, width, width), jnp.bfloat16)

    def own(scaled, block):
        return call(
            functools.partial(own_kernel, scaled, places),
            "own",
            (wide,) + (scalars,) * scaled,
            (channel_class, left, right, block),
            [sources(1)] + lists,
            0.2,
            16,
        )

    def rest(which, summed, first, others, rows=None):
        scaled, passes = len(summed) > 1, rows is not None
        outs = (wide if which == "others" else narrow,) + (scalars,) * scaled + (rows_shape,) * passes
        args = [channel_class, left, right, *summed] + first + others + [rows] * passes
        return call(
            functools.partial(rest_kernel, which, scaled, passes, len(first), slots, places),
            "rest",
            outs,
            args,
            [pltpu.VMEM((width, width), jnp.float32), sources(slots)] + lists,
            0.4 if which == "rest" else 0.2,
            16,
        )

    def shift(block, pairs):
        return lax.ppermute(block, ring, pairs)

    carried = carried_rounds(permutes, blocks)
    rounds = [(ring, pairs) for pairs in carried or []]
    for axis in () if carried else ("rep", "blk"):
        size = lax.axis_size(axis)
        bits = [1 << i for i in range(size.bit_length() - 1)]
        if sum(bits) == size - 1:
            rounds += [(axis, [(i, i ^ bit) for i in range(size)]) for bit in bits]
        else:
            rounds += [(axis, None)]

    def add_round(rows, axis, pairs):
        if pairs is None:
            return lax.psum(rows, axis)
        return rows + lax.ppermute(rows, axis, pairs)

    def spread(block, share, rows=None, after=None):
        piece = shift(share, permutes[0])
        if rows is not None and carried:
            piece, rows = call(
                functools.partial(unpack_kernel, origins[1]),
                "unpack",
                (share_shape, rows_shape),
                (piece, rows),
            )
            rows = add_round(rows, *rounds[0])
        elif rows is not None:
            for step in rounds[:-1]:
                rows = add_round(rows, *step)
            piece = call(pass_kernel, "hold", share_shape, (piece, rows))
        elif after is not None:
            piece = call(pass_kernel, "hold", share_shape, (piece, after), weight=0.5)
        if parts == 2:
            first = [piece, lax.ppermute(piece, "mpo", [(0, 1), (1, 0)])]
        else:
            first = [lax.all_gather(piece, "mpo", axis=0, tiled=True)]
        return first, [shift(block, pairs) for pairs in permutes[1:]], rows

    def gather_parts(t):
        if parts == 2:
            return [t, lax.ppermute(t, "mpo", [(0, 1), (1, 0)])]
        held = lax.all_gather(t, "mpo")
        return [held[i] for i in range(parts)]

    def exchange(rows):
        return lax.all_to_all(rows, ring, 0, 0, tiled=True)

    psi, share_0 = call(take_kernel, "take", (narrow, share_shape), (psi,), weight=2)
    first, others, _ = spread(psi, share_0, after=psi)
    summed = rest("others", own(True, psi), [], others)
    t, unit = rest("first", summed, first, [])
    rows_in_share = width // parts + (2 * TILE if carried else 0)
    w_1, share_1, rows = call(
        functools.partial(first_sums_kernel, width // parts),
        "sums",
        (narrow, jax.ShapeDtypeStruct((rows_in_share, width), jnp.bfloat16), rows_shape),
        (*gather_parts(t), psi, unit),
    )
    first, others, rows = spread(w_1, share_1, rows)
    t, unit, rows = rest("rest", own(True, w_1), first, others, rows)
    rows = add_round(rows, *rounds[-1])
    w_wide, w_2, share_2, v_2, scal = call(
        functools.partial(second_sums_kernel, entries),
        "sums",
        (wide, narrow, share_shape, narrow, scalars),
        (*gather_parts(t), rows, psi, w_1, unit),
    )
    first, others, _ = spread(w_2, share_2, after=w_2)
    summed = rest("others", own(False, w_2), [], others)
    (t,) = rest("first", summed, first, [])
    r, z, rows = call(
        third_sums_kernel,
        "sums",
        (wide, wide, rows_shape),
        (*gather_parts(t), psi, w_1, v_2, w_wide, scal),
        limit=8,
    )
    return call(
        functools.partial(final_kernel, entries),
        "final",
        (
            jax.ShapeDtypeStruct((STEPS, 1, width // parts, width), jnp.bfloat16),
            jax.ShapeDtypeStruct((2, STEPS), jnp.float32),
        ),
        (exchange(rows), r, z, w_wide, v_2, scal),
    )


def solution(mesh):
    return jax.shard_map(
        shards,
        mesh=mesh,
        in_specs=(
            P(("groups", "blk", "rep"), None, None),
            P("mpo", ("groups", "blk", "rep"), None, None),
            P("mpo", ("groups", "blk", "rep"), None, None),
            P("mpo"),
        ),
        out_specs=(P(None, ("groups", "blk", "rep"), "mpo", None), P("groups", None)),
        check_vma=False,
    )
```

```python
import functools

import jax
import jax.numpy as jnp
from jax import lax
from jax.experimental import pallas as pl
from jax.experimental.pallas import tpu as pltpu
from jax.sharding import PartitionSpec as P

NS = 4
STEPS = 3
OFFSETS = (0, NS + 1, NS - 1, -(NS + 1), -(NS - 1))
EPSILON = 1e-06
WIDE = 8
SMALLEST = 1e-30
TILE = 16
MIB = 1024 * 1024
VMEM = pl.BlockSpec(memory_space=pltpu.VMEM)
SMEM = pl.BlockSpec(memory_space=pltpu.SMEM)


def reaches(kind, sector, blocks):
    source = sector - OFFSETS[kind]
    spin = sector % NS
    inside = (source >= 0) & (source < blocks)
    if kind in (1, 4):
        return inside & (spin >= 1)
    if kind in (2, 3):
        return inside & (spin <= NS - 2)
    return inside


def routes(blocks):
    degree, edges = [0] * blocks, []
    for kind in (1, 2):
        for k in range(blocks):
            if reaches(kind, k, blocks):
                edges.append((k - OFFSETS[kind], k))
                degree[k - OFFSETS[kind]] += 1
                degree[k] += 1
    edges.sort(key=lambda edge: degree[edge[0]] + degree[edge[1]])
    partner = [{} for _ in range(blocks)]

    def lowest(block):
        return next(c for c in range(len(edges)) if c not in partner[block])

    for a, b in edges:
        here_free, there_free = lowest(a), lowest(b)
        if here_free in partner[b]:
            path, block, colour = [b], b, here_free
            while colour in partner[block]:
                block = partner[block][colour]
                path.append(block)
                colour = there_free if colour == here_free else here_free
            for block in path:
                moved = {}
                for old, new in ((here_free, there_free), (there_free, here_free)):
                    if old in partner[block]:
                        moved[new] = partner[block].pop(old)
                partner[block].update(moved)
        partner[a][here_free], partner[b][here_free] = b, a
    colours = sorted({c for held in partner for c in held})
    permutes = [[(held[c], k) for k, held in enumerate(partner) if c in held] for c in colours]
    return sorted(permutes, key=len, reverse=True)


def slot_tables(permutes, blocks):
    origins = [{k: k for k in range(blocks)}] + [{k: s for s, k in pairs} for pairs in permutes]
    places = []
    for kind in range(5):
        place = {}
        for slot, origin in enumerate(origins):
            for k, source in origin.items():
                if source == k - OFFSETS[kind] and reaches(kind, k, blocks):
                    place[k] = slot
        places.append(place)
    return places, origins


def carried_rounds(permutes, blocks):
    if not permutes or blocks % 4:
        return None
    rounds = [dict(permutes[0])] + [{k: k ^ bit for k in range(blocks)} for bit in (1, 2)]
    held = [{k} for k in range(blocks)]
    for pairs in rounds:
        if sorted(pairs.values()) != list(range(blocks)):
            return None
        if any(held[source] & held[k] for source, k in pairs.items()):
            return None
        grown = list(held)
        for source, k in pairs.items():
            grown[k] = held[k] | held[source]
        held = grown
    if any(len(rows) < blocks for rows in held):
        return None
    return [sorted(pairs.items()) for pairs in rounds[1:]]


def look_up(table, sector, default):
    out = jnp.int32(default)
    for k, value in table.items():
        if value != default:
            out = jnp.where(sector == k, jnp.int32(value), out)
    return out


def here():
    return lax.axis_index("blk") * lax.axis_size("rep") + lax.axis_index("rep")


def lane_of(rows, lane):
    return rows[:, lane : lane + 1]


def pack(values, shape):
    lanes = lax.broadcasted_iota(jnp.int32, shape, 1)
    out = jnp.zeros(shape, jnp.float32)
    for place, value in enumerate(values):
        out = jnp.where(lanes == place, value, out)
    return out


def total(x):
    return jnp.sum(jnp.sum(x, axis=0, keepdims=True), axis=1, keepdims=True)


def column_sum(x):
    return jnp.sum(x, axis=0, keepdims=True)


def peak(x):
    return jnp.max(jnp.max(jnp.abs(x), axis=0, keepdims=True), axis=1, keepdims=True)


def wide_float(ref):
    return ref[...].astype(jnp.float32)


def sum_parts(parts):
    w = wide_float(parts[0])
    for part in parts[1:]:
        w += wide_float(part)
    return w


def first_row(ref):
    return ref[0:1, :]


def list_channels(which, places, kinds_ref, order, slot_of, idle):
    sector = here()
    low, high = {"own": (0, 0), "rest": (1, idle), "first": (1, 1), "others": (2, idle)}[which]
    slots = []
    for place in places:
        kept = {k: slot for k, slot in place.items() if low <= slot <= high}
        slots.append(look_up(kept, sector, -1))
    count = jnp.int32(0)
    for b in range(kinds_ref.shape[0]):
        kind = kinds_ref[b]
        slot = slots[0]
        for c in range(1, 5):
            slot = jnp.where(kind == c, slots[c], slot)
        order[count] = jnp.int32(b)
        slot_of[count] = slot
        count += jnp.where(slot >= 0, 1, 0)
    for extra in range(WIDE):
        order[count + extra] = jnp.int32(0)
        slot_of[count + extra] = jnp.int32(idle)
    return count


def multiply_listed(count, left_ref, right_ref, source, acc, order, slot_of):
    def multiply(start, wide):
        held = [order[start + inner] for inner in range(wide)]
        pieces = [
            jnp.dot(
                left_ref[b], source[slot_of[start + inner]], preferred_element_type=jnp.float32
            ).astype(jnp.bfloat16)
            for inner, b in enumerate(held)
        ]
        acc[...] += lax.dot_general(
            jnp.concatenate(pieces, axis=1),
            jnp.concatenate([right_ref[b] for b in held], axis=1),
            (((1,), (1,)), ((), ())),
            preferred_element_type=jnp.float32,
        )

    def full(group, carry):
        multiply(group * WIDE, WIDE)
        return carry

    groups = (count + WIDE // 2 - 1) // WIDE
    lax.fori_loop(0, groups, full, 0)
    rest = count - groups * WIDE
    for low, wide in ((0, 2), (2, 4)):

        @pl.when((rest > low) & (rest <= wide))
        def _():
            multiply(groups * WIDE, wide)


def own_kernel(scaled, places, *refs):
    kinds_ref, left_ref, right_ref, block_ref, acc = refs[:5]
    source, order, slot_of = refs[-3:]
    count = list_channels("own", places, kinds_ref, order, slot_of, 1)
    if scaled:
        block = wide_float(block_ref)
        unit = jnp.maximum(peak(block), SMALLEST)
        refs[5][...] = jnp.broadcast_to(unit, refs[5].shape)
        source[0] = (block * (1.0 / unit)).astype(jnp.bfloat16)
    else:
        source[0] = block_ref[...]
    source[1] = jnp.zeros(source.shape[1:], jnp.bfloat16)
    acc[...] = jnp.zeros_like(acc)
    multiply_listed(count, left_ref, right_ref, source, acc, order, slot_of)


def rest_kernel(which, scaled, passes, shares, slots, places, *refs):
    kinds_ref, left_ref, right_ref, own_ref = refs[:4]
    refs = refs[4:]
    if scaled:
        met_ref, refs = refs[0], refs[1:]
    first, refs = refs[:shares], refs[shares:]
    count_others = 0 if which == "first" else slots - 2
    others, refs = refs[:count_others], refs[count_others:]
    if passes:
        rows_ref, refs = refs[0], refs[1:]
    t_ref, refs = refs[0], refs[1:]
    if scaled:
        unit_ref, refs = refs[0], refs[1:]
    if passes:
        refs[0][...] = rows_ref[...]
        refs = refs[1:]
    acc, source, order, slot_of = refs
    count = list_channels(which, places, kinds_ref, order, slot_of, slots)
    if scaled:
        met = lane_of(first_row(met_ref), 0)
        unit = met
        for block in (*first, *others):
            unit = jnp.maximum(unit, peak(wide_float(block)))
        unit_ref[...] = jnp.broadcast_to(unit, unit_ref.shape)
        inverse = 1.0 / unit

    def scale(block):
        return (wide_float(block) * inverse).astype(jnp.bfloat16) if scaled else block[...]

    for step, block in enumerate(first):
        share = source.shape[1] // shares
        at = 0 if shares == 1 else jnp.abs(step - lax.axis_index("mpo"))
        source[1, pl.ds(pl.multiple_of(at * share, share), share), :] = scale(block)
    for slot, block in enumerate(others, 2):
        source[slot] = scale(block)
    source[slots] = jnp.zeros(source.shape[1:], jnp.bfloat16)
    acc[...] = own_ref[...] * (met * inverse) if scaled else own_ref[...]
    multiply_listed(count, left_ref, right_ref, source, acc, order, slot_of)
    t_ref[...] = acc[...].astype(t_ref.dtype)


def pass_kernel(block_ref, rows_ref, out_ref):
    out_ref[...] = block_ref[...]


def unpack_kernel(origin, block_ref, rows_ref, out_ref, sums_ref):
    share = out_ref.shape[0]
    out_ref[...] = block_ref[0:share, :]
    terms = block_ref[share : share + 2 * TILE, :].astype(jnp.float32)
    sums = terms[0:TILE, 0:128] + terms[0:TILE, 128:256] + terms[TILE : 2 * TILE, 0:128]
    row = lax.broadcasted_iota(jnp.int32, rows_ref.shape, 0)
    source = look_up(origin, here(), 0)
    sums_ref[...] = jnp.where(row == source, first_row(sums), rows_ref[...])


def take_kernel(block_ref, copy_ref, share_ref):
    copy_ref[...] = block_ref[...]
    share_ref[...] = block_ref[my_rows(share_ref.shape[0]), :]


def my_rows(share):
    return pl.ds(pl.multiple_of(lax.axis_index("mpo") * share, share), share)


def first_sums_kernel(share, *refs):
    parts, (psi_ref, unit_ref, w_ref, share_ref, rows_ref) = refs[:-5], refs[-5:]
    w = sum_parts(parts)
    unit = lane_of(first_row(unit_ref), 0)
    w_ref[...] = (w * unit).astype(jnp.bfloat16)
    share_ref[0:share, :] = w_ref[my_rows(share), :]
    v = wide_float(psi_ref) * (1.0 / unit)
    a = total(v * w)
    d = total(v * v)
    local = a / jnp.maximum(d, SMALLEST)
    r = w - local * v
    values = [a, d, local, total(r * v), total(r * r), unit]
    if share_ref.shape[0] > share:
        sums = pack(values, (TILE, 128))
        high = sums.astype(jnp.bfloat16)
        rest = sums - high.astype(jnp.float32)
        middle = rest.astype(jnp.bfloat16)
        low = (rest - middle.astype(jnp.float32)).astype(jnp.bfloat16)
        blank = jnp.zeros((2 * TILE, share_ref.shape[1]), jnp.bfloat16)
        share_ref[share : share + 2 * TILE, :] = blank
        share_ref[share : share + TILE, 0:128] = high
        share_ref[share : share + TILE, 128:256] = middle
        share_ref[share + TILE : share + 2 * TILE, 0:128] = low
        sums = high.astype(jnp.float32) + middle.astype(jnp.float32) + low.astype(jnp.float32)
        sums = jnp.broadcast_to(first_row(sums), rows_ref.shape)
    else:
        sums = pack(values, rows_ref.shape)
    row = lax.broadcasted_iota(jnp.int32, rows_ref.shape, 0)
    rows_ref[...] = jnp.where(row == here(), sums, 0.0)


def shrink(scal):
    return 1.0 / (jnp.abs(lane_of(scal, 0)) + lane_of(scal, 1))


def second_sums_kernel(entries, *refs):
    parts, refs = refs[:-9], refs[-9:]
    rows_ref, psi_ref, first_ref, unit_ref, wide_ref, w_ref, share_ref, v_ref, scal_ref = refs
    rows = rows_ref[...]
    a, d, local, p, q, unit = (lane_of(rows, lane) for lane in range(6))
    beta_0 = jnp.sqrt(column_sum(unit * unit * d) / entries + EPSILON)
    start_inverse = 1.0 / beta_0
    gain = unit * start_inverse
    alpha = column_sum(gain * (gain * a)) / entries
    off = local - alpha
    square = column_sum(gain * (gain * (q + off * (2.0 * p + off * d))))
    beta = jnp.sqrt(jnp.maximum(square, 0.0) / entries + EPSILON)
    inverse = 1.0 / beta
    scal = pack([alpha, beta, start_inverse], scal_ref.shape)
    scal_ref[...] = scal
    image = wide_float(first_ref) * start_inverse
    v_ref[...] = ((image - (alpha * start_inverse) * wide_float(psi_ref)) * inverse).astype(jnp.bfloat16)
    lift = lane_of(first_row(unit_ref), 0) * start_inverse
    w = (sum_parts(parts) * lift - alpha * image) * (inverse * shrink(first_row(scal)))
    wide_ref[...] = w
    w_ref[...] = w.astype(jnp.bfloat16)
    share_ref[...] = w_ref[my_rows(share_ref.shape[0]), :]


def third_sums_kernel(*refs):
    parts, refs = refs[:-8], refs[-8:]
    psi_ref, first_ref, v_ref, w_ref, scal_ref, r_ref, z_ref, rows_ref = refs
    scal = first_row(scal_ref)
    scale = shrink(scal)
    push = scale * lane_of(scal, 1) * lane_of(scal, 2)
    v, w = wide_float(v_ref), w_ref[...]
    vv, vw = total(v * v), total(v * w)
    local = vw / jnp.maximum(vv, SMALLEST)
    r = w - local * v - push * wide_float(psi_ref)
    z = sum_parts(parts) - (local / scale) * w - push * wide_float(first_ref)
    r_ref[...] = r
    z_ref[...] = z
    sums = [total(r * r), total(r * v), total(r * z), total(r * w)]
    sums += [total(z * v), total(z * w), total(z * z), total(w * w)]
    rows_ref[...] = pack([vv, vw, local] + sums, rows_ref.shape)


def final_kernel(entries, rows_ref, r_ref, z_ref, w_ref, v_ref, scal_ref, basis_ref, coef_ref):
    share = basis_ref.shape[2]
    mine = my_rows(share)
    vv, vw, local, rr, rv, rz, rw, zv, zw, zz, ww = (lane_of(rows_ref[...], i) for i in range(11))
    scal = first_row(scal_ref)
    scale = shrink(scal)
    inverse_scale = 1.0 / scale
    alpha_scaled = column_sum(vw) / entries
    off = local - alpha_scaled
    lift = off * inverse_scale
    square = column_sum(rr + off * (2.0 * rv + off * vv)) / entries
    beta_scaled = jnp.sqrt(jnp.maximum(square, 0.0) + scale * scale * EPSILON)
    inverse = 1.0 / beta_scaled
    mixed = column_sum(rz + lift * rw + off * (zv + lift * vw)) / entries
    alpha_3 = mixed * inverse * inverse
    r_v = column_sum(rv + off * vv) / entries
    z_v = column_sum(zv + lift * vw) / entries
    z_z = column_sum(zz + lift * (2.0 * zw + lift * ww)) / entries
    v_v = column_sum(vv) / entries
    beta_2 = beta_scaled * inverse_scale
    third = (z_z - 2.0 * alpha_3 * mixed + alpha_3 * alpha_3 * square) * inverse * inverse
    third += beta_2 * (beta_2 * v_v - 2.0 * inverse * (z_v - alpha_3 * r_v))
    beta_3 = jnp.sqrt(jnp.maximum(third, 0.0) + EPSILON)

    sector = here()
    row_of = lax.broadcasted_iota(jnp.int32, off.shape, 0)
    off_here = column_sum(jnp.where(row_of == sector, off, 0.0))
    v = v_ref[mine, :]
    v_wide = v.astype(jnp.float32)
    v_3 = (r_ref[mine, :] + off_here * v_wide) * inverse
    image = (z_ref[mine, :] + (off_here * inverse_scale) * w_ref[mine, :]) * inverse
    basis_ref[0, 0] = v
    basis_ref[1, 0] = v_3.astype(jnp.bfloat16)
    residual = image - alpha_3 * v_3 - beta_2 * v_wide
    basis_ref[2, 0] = (residual * (1.0 / beta_3)).astype(jnp.bfloat16)

    row = lax.broadcasted_iota(jnp.int32, coef_ref.shape, 0)
    column = lax.broadcasted_iota(jnp.int32, coef_ref.shape, 1)
    out = jnp.zeros(coef_ref.shape, jnp.float32)
    pairs = [(lane_of(scal, 0), lane_of(scal, 1)), (alpha_scaled * inverse_scale, beta_2), (alpha_3, beta_3)]
    for step, (a, b) in enumerate(pairs):
        out = jnp.where(column == step, jnp.where(row == 0, a, b), out)
    coef_ref[...] = out


def shards(wavefunction, env_left, env_right, channel_class):
    width = wavefunction.shape[1]
    ring = ("blk", "rep")
    parts = lax.axis_size("mpo")
    blocks = lax.axis_size("blk") * lax.axis_size("rep")
    entries = blocks * width * width
    permutes = routes(blocks)
    places, origins = slot_tables(permutes, blocks)
    slots = 1 + len(permutes)
    channels = channel_class.shape[0]
    psi, left, right = wavefunction[0], env_left[:, 0], env_right[:, 0]
    rows_shape = jax.ShapeDtypeStruct((blocks, 128), jnp.float32)
    scalars = jax.ShapeDtypeStruct((8, 128), jnp.float32)
    wide = jax.ShapeDtypeStruct((width, width), jnp.float32)
    narrow = jax.ShapeDtypeStruct((width, width), jnp.bfloat16)
    share_shape = jax.ShapeDtypeStruct((width // parts, width), jnp.bfloat16)
    lists = [pltpu.SMEM((channels + WIDE,), jnp.int32)] * 2

    def call(kernel, name, outs, args, scratch=(), share=0, limit=4, weight=0):
        flops = int(4 * channels * max(share, weight) * width**3)
        cost = pl.CostEstimate(flops=flops, bytes_accessed=4 * width * width, transcendentals=0)
        listed = outs if isinstance(outs, tuple) else (outs,)
        first = SMEM if share else VMEM
        return pl.pallas_call(
            kernel,
            out_shape=outs,
            in_specs=[first] + [VMEM] * (len(args) - 1),
            out_specs=tuple(VMEM for _ in listed) if isinstance(outs, tuple) else VMEM,
            scratch_shapes=list(scratch),
            compiler_params=pltpu.CompilerParams(vmem_limit_bytes=limit * MIB),
            cost_estimate=cost,
            name=name,
        )(*args)

    def sources(count):
        return pltpu.VMEM((count + 1, width, width), jnp.bfloat16)

    def own(scaled, block):
        return call(
            functools.partial(own_kernel, scaled, places),
            "own",
            (wide,) + (scalars,) * scaled,
            (channel_class, left, right, block),
            [sources(1)] + lists,
            0.2,
            16,
        )

    def rest(which, summed, first, others, rows=None):
        scaled, passes = len(summed) > 1, rows is not None
        outs = (wide if which == "others" else narrow,) + (scalars,) * scaled + (rows_shape,) * passes
        args = [channel_class, left, right, *summed] + first + others + [rows] * passes
        return call(
            functools.partial(rest_kernel, which, scaled, passes, len(first), slots, places),
            "rest",
            outs,
            args,
            [pltpu.VMEM((width, width), jnp.float32), sources(slots)] + lists,
            0.4 if which == "rest" else 0.2,
            16,
        )

    def shift(block, pairs):
        return lax.ppermute(block, ring, pairs)

    carried = carried_rounds(permutes, blocks)
    rounds = [(ring, pairs) for pairs in carried or []]
    for axis in () if carried else ("rep", "blk"):
        size = lax.axis_size(axis)
        bits = [1 << i for i in range(size.bit_length() - 1)]
        if sum(bits) == size - 1:
            rounds += [(axis, [(i, i ^ bit) for i in range(size)]) for bit in bits]
        else:
            rounds += [(axis, None)]

    def add_round(rows, axis, pairs):
        if pairs is None:
            return lax.psum(rows, axis)
        return rows + lax.ppermute(rows, axis, pairs)

    def spread(block, share, rows=None, after=None):
        piece = shift(share, permutes[0])
        if rows is not None and carried:
            piece, rows = call(
                functools.partial(unpack_kernel, origins[1]),
                "unpack",
                (share_shape, rows_shape),
                (piece, rows),
            )
            rows = add_round(rows, *rounds[0])
        elif rows is not None:
            for step in rounds[:-1]:
                rows = add_round(rows, *step)
            piece = call(pass_kernel, "hold", share_shape, (piece, rows))
        elif after is not None:
            piece = call(pass_kernel, "hold", share_shape, (piece, after), weight=0.5)
        if parts == 2:
            first = [piece, lax.ppermute(piece, "mpo", [(0, 1), (1, 0)])]
        else:
            first = [lax.all_gather(piece, "mpo", axis=0, tiled=True)]
        return first, [shift(block, pairs) for pairs in permutes[1:]], rows

    def gather_parts(t):
        if parts == 2:
            return [t, lax.ppermute(t, "mpo", [(0, 1), (1, 0)])]
        held = lax.all_gather(t, "mpo")
        return [held[i] for i in range(parts)]

    def exchange(rows):
        return lax.all_to_all(rows, ring, 0, 0, tiled=True)

    psi, share_0 = call(take_kernel, "take", (narrow, share_shape), (psi,), weight=2)
    first, others, _ = spread(psi, share_0, after=psi)
    summed = rest("others", own(True, psi), [], others)
    t, unit = rest("first", summed, first, [])
    rows_in_share = width // parts + (2 * TILE if carried else 0)
    w_1, share_1, rows = call(
        functools.partial(first_sums_kernel, width // parts),
        "sums",
        (narrow, jax.ShapeDtypeStruct((rows_in_share, width), jnp.bfloat16), rows_shape),
        (*gather_parts(t), psi, unit),
    )
    first, others, rows = spread(w_1, share_1, rows)
    t, unit, rows = rest("rest", own(True, w_1), first, others, rows)
    rows = add_round(rows, *rounds[-1])
    w_wide, w_2, share_2, v_2, scal = call(
        functools.partial(second_sums_kernel, entries),
        "sums",
        (wide, narrow, share_shape, narrow, scalars),
        (*gather_parts(t), rows, psi, w_1, unit),
    )
    first, others, _ = spread(w_2, share_2)
    (t,) = rest("rest", own(False, w_2), first, others)
    r, z, rows = call(
        third_sums_kernel,
        "sums",
        (wide, wide, rows_shape),
        (*gather_parts(t), psi, w_1, v_2, w_wide, scal),
        limit=8,
    )
    return call(
        functools.partial(final_kernel, entries),
        "final",
        (
            jax.ShapeDtypeStruct((STEPS, 1, width // parts, width), jnp.bfloat16),
            jax.ShapeDtypeStruct((2, STEPS), jnp.float32),
        ),
        (exchange(rows), r, z, w_wide, v_2, scal),
    )


def solution(mesh):
    return jax.shard_map(
        shards,
        mesh=mesh,
        in_specs=(
            P(("groups", "blk", "rep"), None, None),
            P("mpo", ("groups", "blk", "rep"), None, None),
            P("mpo", ("groups", "blk", "rep"), None, None),
            P("mpo"),
        ),
        out_specs=(P(None, ("groups", "blk", "rep"), "mpo", None), P("groups", None)),
        check_vma=False,
    )
```

```python
import functools

import jax
import jax.numpy as jnp
from jax import lax
from jax.experimental import pallas as pl
from jax.experimental.pallas import tpu as pltpu
from jax.sharding import PartitionSpec as P

NS = 4
STEPS = 3
OFFSETS = (0, NS + 1, NS - 1, -(NS + 1), -(NS - 1))
EPSILON = 1e-06
WIDE, WIDEST = 8, 12
SMALLEST = 1e-30
TILE = 16
MIB = 1024 * 1024
VMEM = pl.BlockSpec(memory_space=pltpu.VMEM)
SMEM = pl.BlockSpec(memory_space=pltpu.SMEM)


def reaches(kind, sector, blocks):
    source = sector - OFFSETS[kind]
    spin = sector % NS
    inside = (source >= 0) & (source < blocks)
    if kind in (1, 4):
        return inside & (spin >= 1)
    if kind in (2, 3):
        return inside & (spin <= NS - 2)
    return inside


def routes(blocks):
    degree, edges = [0] * blocks, []
    for kind in (1, 2):
        for k in range(blocks):
            if reaches(kind, k, blocks):
                edges.append((k - OFFSETS[kind], k))
                degree[k - OFFSETS[kind]] += 1
                degree[k] += 1
    edges.sort(key=lambda edge: degree[edge[0]] + degree[edge[1]])
    partner = [{} for _ in range(blocks)]

    def lowest(block):
        return next(c for c in range(len(edges)) if c not in partner[block])

    for a, b in edges:
        here_free, there_free = lowest(a), lowest(b)
        if here_free in partner[b]:
            path, block, colour = [b], b, here_free
            while colour in partner[block]:
                block = partner[block][colour]
                path.append(block)
                colour = there_free if colour == here_free else here_free
            for block in path:
                moved = {}
                for old, new in ((here_free, there_free), (there_free, here_free)):
                    if old in partner[block]:
                        moved[new] = partner[block].pop(old)
                partner[block].update(moved)
        partner[a][here_free], partner[b][here_free] = b, a
    colours = sorted({c for held in partner for c in held})
    permutes = [[(held[c], k) for k, held in enumerate(partner) if c in held] for c in colours]
    return sorted(permutes, key=len, reverse=True)


def slot_tables(permutes, blocks):
    origins = [{k: k for k in range(blocks)}] + [{k: s for s, k in pairs} for pairs in permutes]
    places = []
    for kind in range(5):
        place = {}
        for slot, origin in enumerate(origins):
            for k, source in origin.items():
                if source == k - OFFSETS[kind] and reaches(kind, k, blocks):
                    place[k] = slot
        places.append(place)
    return places, origins


def carried_rounds(permutes, blocks):
    if not permutes or blocks % 4:
        return None
    rounds = [dict(permutes[0])] + [{k: k ^ bit for k in range(blocks)} for bit in (1, 2)]
    held = [{k} for k in range(blocks)]
    for pairs in rounds:
        if sorted(pairs.values()) != list(range(blocks)):
            return None
        if any(held[source] & held[k] for source, k in pairs.items()):
            return None
        grown = list(held)
        for source, k in pairs.items():
            grown[k] = held[k] | held[source]
        held = grown
    if any(len(rows) < blocks for rows in held):
        return None
    return [sorted(pairs.items()) for pairs in rounds[1:]]


def look_up(table, sector, default):
    out = jnp.int32(default)
    for k, value in table.items():
        if value != default:
            out = jnp.where(sector == k, jnp.int32(value), out)
    return out


def here():
    return lax.axis_index("blk") * lax.axis_size("rep") + lax.axis_index("rep")


def lane_of(rows, lane):
    return rows[:, lane : lane + 1]


def pack(values, shape):
    lanes = lax.broadcasted_iota(jnp.int32, shape, 1)
    out = jnp.zeros(shape, jnp.float32)
    for place, value in enumerate(values):
        out = jnp.where(lanes == place, value, out)
    return out


def total(x):
    return jnp.sum(jnp.sum(x, axis=0, keepdims=True), axis=1, keepdims=True)


def column_sum(x):
    return jnp.sum(x, axis=0, keepdims=True)


def peak(x):
    return jnp.max(jnp.max(jnp.abs(x), axis=0, keepdims=True), axis=1, keepdims=True)


def wide_float(ref):
    return ref[...].astype(jnp.float32)


def sum_parts(parts):
    w = wide_float(parts[0])
    for part in parts[1:]:
        w += wide_float(part)
    return w


def first_row(ref):
    return ref[0:1, :]


def list_channels(which, places, kinds_ref, order, slot_of, idle):
    sector = here()
    low, high = {"own": (0, 0), "rest": (1, idle), "first": (1, 1), "others": (2, idle)}[which]
    slots = []
    for place in places:
        kept = {k: slot for k, slot in place.items() if low <= slot <= high}
        slots.append(look_up(kept, sector, -1))
    count = jnp.int32(0)
    for b in range(kinds_ref.shape[0]):
        kind = kinds_ref[b]
        slot = slots[0]
        for c in range(1, 5):
            slot = jnp.where(kind == c, slots[c], slot)
        order[count] = jnp.int32(b)
        slot_of[count] = slot
        count += jnp.where(slot >= 0, 1, 0)
    for extra in range(WIDEST):
        order[count + extra] = jnp.int32(0)
        slot_of[count + extra] = jnp.int32(idle)
    return count


def multiply_listed(count, size, left_ref, right_ref, source, acc, order, slot_of):
    def multiply(start, wide):
        held = [order[start + inner] for inner in range(wide)]
        pieces = [
            jnp.dot(
                left_ref[b], source[slot_of[start + inner]], preferred_element_type=jnp.float32
            ).astype(jnp.bfloat16)
            for inner, b in enumerate(held)
        ]
        acc[...] += lax.dot_general(
            jnp.concatenate(pieces, axis=1),
            jnp.concatenate([right_ref[b] for b in held], axis=1),
            (((1,), (1,)), ((), ())),
            preferred_element_type=jnp.float32,
        )

    def full(group, carry):
        multiply(group * size, size)
        return carry

    smaller = [wide for wide in (2, 4, WIDE) if wide < size]
    groups = (count + size - 1 - smaller[-1]) // size
    lax.fori_loop(0, groups, full, 0)
    rest = count - groups * size
    for low, wide in zip([0] + smaller, smaller):

        @pl.when((rest > low) & (rest <= wide))
        def _():
            multiply(groups * size, wide)


def own_kernel(scaled, places, *refs):
    kinds_ref, left_ref, right_ref, block_ref, acc = refs[:5]
    source, order, slot_of = refs[-3:]
    count = list_channels("own", places, kinds_ref, order, slot_of, 1)
    if scaled:
        block = wide_float(block_ref)
        unit = jnp.maximum(peak(block), SMALLEST)
        refs[5][...] = jnp.broadcast_to(unit, refs[5].shape)
        source[0] = (block * (1.0 / unit)).astype(jnp.bfloat16)
    else:
        source[0] = block_ref[...]
    source[1] = jnp.zeros(source.shape[1:], jnp.bfloat16)
    acc[...] = jnp.zeros_like(acc)
    multiply_listed(count, WIDE, left_ref, right_ref, source, acc, order, slot_of)


def rest_kernel(which, scaled, passes, shares, slots, places, *refs):
    kinds_ref, left_ref, right_ref, own_ref = refs[:4]
    refs = refs[4:]
    if scaled:
        met_ref, refs = refs[0], refs[1:]
    first, refs = refs[:shares], refs[shares:]
    count_others = 0 if which == "first" else slots - 2
    others, refs = refs[:count_others], refs[count_others:]
    if passes:
        rows_ref, refs = refs[0], refs[1:]
    t_ref, refs = refs[0], refs[1:]
    if scaled:
        unit_ref, refs = refs[0], refs[1:]
    if passes:
        refs[0][...] = rows_ref[...]
        refs = refs[1:]
    acc, source, order, slot_of = refs
    count = list_channels(which, places, kinds_ref, order, slot_of, slots)
    if scaled:
        met = lane_of(first_row(met_ref), 0)
        unit = met
        for block in (*first, *others):
            unit = jnp.maximum(unit, peak(wide_float(block)))
        unit_ref[...] = jnp.broadcast_to(unit, unit_ref.shape)
        inverse = 1.0 / unit

    def scale(block):
        return (wide_float(block) * inverse).astype(jnp.bfloat16) if scaled else block[...]

    for step, block in enumerate(first):
        share = source.shape[1] // shares
        at = 0 if shares == 1 else jnp.abs(step - lax.axis_index("mpo"))
        source[1, pl.ds(pl.multiple_of(at * share, share), share), :] = scale(block)
    for slot, block in enumerate(others, 2):
        source[slot] = scale(block)
    source[slots] = jnp.zeros(source.shape[1:], jnp.bfloat16)
    acc[...] = own_ref[...] * (met * inverse) if scaled else own_ref[...]
    multiply_listed(count, WIDEST if which == "rest" else WIDE, left_ref, right_ref, source, acc, order, slot_of)
    t_ref[...] = acc[...].astype(t_ref.dtype)


def pass_kernel(block_ref, rows_ref, out_ref):
    out_ref[...] = block_ref[...]


def unpack_kernel(origin, block_ref, rows_ref, out_ref, sums_ref):
    share = out_ref.shape[0]
    out_ref[...] = block_ref[0:share, :]
    terms = block_ref[share : share + 2 * TILE, :].astype(jnp.float32)
    sums = terms[0:TILE, 0:128] + terms[0:TILE, 128:256] + terms[TILE : 2 * TILE, 0:128]
    row = lax.broadcasted_iota(jnp.int32, rows_ref.shape, 0)
    source = look_up(origin, here(), 0)
    sums_ref[...] = jnp.where(row == source, first_row(sums), rows_ref[...])


def take_kernel(block_ref, copy_ref, share_ref):
    copy_ref[...] = block_ref[...]
    share_ref[...] = block_ref[my_rows(share_ref.shape[0]), :]


def my_rows(share):
    return pl.ds(pl.multiple_of(lax.axis_index("mpo") * share, share), share)


def first_sums_kernel(share, *refs):
    parts, (psi_ref, unit_ref, w_ref, share_ref, rows_ref) = refs[:-5], refs[-5:]
    w = sum_parts(parts)
    unit = lane_of(first_row(unit_ref), 0)
    w_ref[...] = (w * unit).astype(jnp.bfloat16)
    share_ref[0:share, :] = w_ref[my_rows(share), :]
    v = wide_float(psi_ref) * (1.0 / unit)
    a = total(v * w)
    d = total(v * v)
    local = a / jnp.maximum(d, SMALLEST)
    r = w - local * v
    values = [a, d, local, total(r * v), total(r * r), unit]
    if share_ref.shape[0] > share:
        sums = pack(values, (TILE, 128))
        high = sums.astype(jnp.bfloat16)
        rest = sums - high.astype(jnp.float32)
        middle = rest.astype(jnp.bfloat16)
        low = (rest - middle.astype(jnp.float32)).astype(jnp.bfloat16)
        blank = jnp.zeros((2 * TILE, share_ref.shape[1]), jnp.bfloat16)
        share_ref[share : share + 2 * TILE, :] = blank
        share_ref[share : share + TILE, 0:128] = high
        share_ref[share : share + TILE, 128:256] = middle
        share_ref[share + TILE : share + 2 * TILE, 0:128] = low
        sums = high.astype(jnp.float32) + middle.astype(jnp.float32) + low.astype(jnp.float32)
        sums = jnp.broadcast_to(first_row(sums), rows_ref.shape)
    else:
        sums = pack(values, rows_ref.shape)
    row = lax.broadcasted_iota(jnp.int32, rows_ref.shape, 0)
    rows_ref[...] = jnp.where(row == here(), sums, 0.0)


def shrink(scal):
    return 1.0 / (jnp.abs(lane_of(scal, 0)) + lane_of(scal, 1))


def second_sums_kernel(entries, *refs):
    parts, refs = refs[:-9], refs[-9:]
    rows_ref, psi_ref, first_ref, unit_ref, wide_ref, w_ref, share_ref, v_ref, scal_ref = refs
    rows = rows_ref[...]
    a, d, local, p, q, unit = (lane_of(rows, lane) for lane in range(6))
    beta_0 = jnp.sqrt(column_sum(unit * unit * d) / entries + EPSILON)
    start_inverse = 1.0 / beta_0
    gain = unit * start_inverse
    alpha = column_sum(gain * (gain * a)) / entries
    off = local - alpha
    square = column_sum(gain * (gain * (q + off * (2.0 * p + off * d))))
    beta = jnp.sqrt(jnp.maximum(square, 0.0) / entries + EPSILON)
    inverse = 1.0 / beta
    scal = pack([alpha, beta, start_inverse], scal_ref.shape)
    scal_ref[...] = scal
    image = wide_float(first_ref) * start_inverse
    v_ref[...] = ((image - (alpha * start_inverse) * wide_float(psi_ref)) * inverse).astype(jnp.bfloat16)
    lift = lane_of(first_row(unit_ref), 0) * start_inverse
    w = (sum_parts(parts) * lift - alpha * image) * (inverse * shrink(first_row(scal)))
    wide_ref[...] = w
    w_ref[...] = w.astype(jnp.bfloat16)
    share_ref[...] = w_ref[my_rows(share_ref.shape[0]), :]


def third_sums_kernel(*refs):
    parts, refs = refs[:-8], refs[-8:]
    psi_ref, first_ref, v_ref, w_ref, scal_ref, r_ref, z_ref, rows_ref = refs
    scal = first_row(scal_ref)
    scale = shrink(scal)
    push = scale * lane_of(scal, 1) * lane_of(scal, 2)
    v, w = wide_float(v_ref), w_ref[...]
    vv, vw = total(v * v), total(v * w)
    local = vw / jnp.maximum(vv, SMALLEST)
    r = w - local * v - push * wide_float(psi_ref)
    z = sum_parts(parts) - (local / scale) * w - push * wide_float(first_ref)
    r_ref[...] = r
    z_ref[...] = z
    sums = [total(r * r), total(r * v), total(r * z), total(r * w)]
    sums += [total(z * v), total(z * w), total(z * z), total(w * w)]
    rows_ref[...] = pack([vv, vw, local] + sums, rows_ref.shape)


def final_kernel(entries, rows_ref, r_ref, z_ref, w_ref, v_ref, scal_ref, basis_ref, coef_ref):
    share = basis_ref.shape[2]
    mine = my_rows(share)
    vv, vw, local, rr, rv, rz, rw, zv, zw, zz, ww = (lane_of(rows_ref[...], i) for i in range(11))
    scal = first_row(scal_ref)
    scale = shrink(scal)
    inverse_scale = 1.0 / scale
    alpha_scaled = column_sum(vw) / entries
    off = local - alpha_scaled
    lift = off * inverse_scale
    square = column_sum(rr + off * (2.0 * rv + off * vv)) / entries
    beta_scaled = jnp.sqrt(jnp.maximum(square, 0.0) + scale * scale * EPSILON)
    inverse = 1.0 / beta_scaled
    mixed = column_sum(rz + lift * rw + off * (zv + lift * vw)) / entries
    alpha_3 = mixed * inverse * inverse
    r_v = column_sum(rv + off * vv) / entries
    z_v = column_sum(zv + lift * vw) / entries
    z_z = column_sum(zz + lift * (2.0 * zw + lift * ww)) / entries
    v_v = column_sum(vv) / entries
    beta_2 = beta_scaled * inverse_scale
    third = (z_z - 2.0 * alpha_3 * mixed + alpha_3 * alpha_3 * square) * inverse * inverse
    third += beta_2 * (beta_2 * v_v - 2.0 * inverse * (z_v - alpha_3 * r_v))
    beta_3 = jnp.sqrt(jnp.maximum(third, 0.0) + EPSILON)

    sector = here()
    row_of = lax.broadcasted_iota(jnp.int32, off.shape, 0)
    off_here = column_sum(jnp.where(row_of == sector, off, 0.0))
    v = v_ref[mine, :]
    v_wide = v.astype(jnp.float32)
    v_3 = (r_ref[mine, :] + off_here * v_wide) * inverse
    image = (z_ref[mine, :] + (off_here * inverse_scale) * w_ref[mine, :]) * inverse
    basis_ref[0, 0] = v
    basis_ref[1, 0] = v_3.astype(jnp.bfloat16)
    residual = image - alpha_3 * v_3 - beta_2 * v_wide
    basis_ref[2, 0] = (residual * (1.0 / beta_3)).astype(jnp.bfloat16)

    row = lax.broadcasted_iota(jnp.int32, coef_ref.shape, 0)
    column = lax.broadcasted_iota(jnp.int32, coef_ref.shape, 1)
    out = jnp.zeros(coef_ref.shape, jnp.float32)
    pairs = [(lane_of(scal, 0), lane_of(scal, 1)), (alpha_scaled * inverse_scale, beta_2), (alpha_3, beta_3)]
    for step, (a, b) in enumerate(pairs):
        out = jnp.where(column == step, jnp.where(row == 0, a, b), out)
    coef_ref[...] = out


def shards(wavefunction, env_left, env_right, channel_class):
    width = wavefunction.shape[1]
    ring = ("blk", "rep")
    parts = lax.axis_size("mpo")
    blocks = lax.axis_size("blk") * lax.axis_size("rep")
    entries = blocks * width * width
    permutes = routes(blocks)
    places, origins = slot_tables(permutes, blocks)
    slots = 1 + len(permutes)
    channels = channel_class.shape[0]
    psi, left, right = wavefunction[0], env_left[:, 0], env_right[:, 0]
    rows_shape = jax.ShapeDtypeStruct((blocks, 128), jnp.float32)
    scalars = jax.ShapeDtypeStruct((8, 128), jnp.float32)
    wide = jax.ShapeDtypeStruct((width, width), jnp.float32)
    narrow = jax.ShapeDtypeStruct((width, width), jnp.bfloat16)
    share_shape = jax.ShapeDtypeStruct((width // parts, width), jnp.bfloat16)
    lists = [pltpu.SMEM((channels + WIDEST,), jnp.int32)] * 2

    def call(kernel, name, outs, args, scratch=(), share=0, limit=4, weight=0):
        flops = int(4 * channels * max(share, weight) * width**3)
        cost = pl.CostEstimate(flops=flops, bytes_accessed=4 * width * width, transcendentals=0)
        listed = outs if isinstance(outs, tuple) else (outs,)
        first = SMEM if share else VMEM
        return pl.pallas_call(
            kernel,
            out_shape=outs,
            in_specs=[first] + [VMEM] * (len(args) - 1),
            out_specs=tuple(VMEM for _ in listed) if isinstance(outs, tuple) else VMEM,
            scratch_shapes=list(scratch),
            compiler_params=pltpu.CompilerParams(vmem_limit_bytes=limit * MIB),
            cost_estimate=cost,
            name=name,
        )(*args)

    def sources(count):
        return pltpu.VMEM((count + 1, width, width), jnp.bfloat16)

    def own(scaled, block):
        return call(
            functools.partial(own_kernel, scaled, places),
            "own",
            (wide,) + (scalars,) * scaled,
            (channel_class, left, right, block),
            [sources(1)] + lists,
            0.2,
            16,
        )

    def rest(which, summed, first, others, rows=None):
        scaled, passes = len(summed) > 1, rows is not None
        outs = (wide if which == "others" else narrow,) + (scalars,) * scaled + (rows_shape,) * passes
        args = [channel_class, left, right, *summed] + first + others + [rows] * passes
        return call(
            functools.partial(rest_kernel, which, scaled, passes, len(first), slots, places),
            "rest",
            outs,
            args,
            [pltpu.VMEM((width, width), jnp.float32), sources(slots)] + lists,
            0.4 if which == "rest" else 0.2,
            16,
        )

    def shift(block, pairs):
        return lax.ppermute(block, ring, pairs)

    carried = carried_rounds(permutes, blocks)
    rounds = [(ring, pairs) for pairs in carried or []]
    for axis in () if carried else ("rep", "blk"):
        size = lax.axis_size(axis)
        bits = [1 << i for i in range(size.bit_length() - 1)]
        if sum(bits) == size - 1:
            rounds += [(axis, [(i, i ^ bit) for i in range(size)]) for bit in bits]
        else:
            rounds += [(axis, None)]

    def add_round(rows, axis, pairs):
        if pairs is None:
            return lax.psum(rows, axis)
        return rows + lax.ppermute(rows, axis, pairs)

    def spread(block, share, rows=None, after=None):
        piece = shift(share, permutes[0])
        if rows is not None and carried:
            piece, rows = call(
                functools.partial(unpack_kernel, origins[1]),
                "unpack",
                (share_shape, rows_shape),
                (piece, rows),
            )
            rows = add_round(rows, *rounds[0])
        elif rows is not None:
            for step in rounds[:-1]:
                rows = add_round(rows, *step)
            piece = call(pass_kernel, "hold", share_shape, (piece, rows))
        elif after is not None:
            piece = call(pass_kernel, "hold", share_shape, (piece, after), weight=0.5)
        if parts == 2:
            first = [piece, lax.ppermute(piece, "mpo", [(0, 1), (1, 0)])]
        else:
            first = [lax.all_gather(piece, "mpo", axis=0, tiled=True)]
        return first, [shift(block, pairs) for pairs in permutes[1:]], rows

    def gather_parts(t):
        if parts == 2:
            return [t, lax.ppermute(t, "mpo", [(0, 1), (1, 0)])]
        held = lax.all_gather(t, "mpo")
        return [held[i] for i in range(parts)]

    def exchange(rows):
        return lax.all_to_all(rows, ring, 0, 0, tiled=True)

    psi, share_0 = call(take_kernel, "take", (narrow, share_shape), (psi,), weight=2)
    first, others, _ = spread(psi, share_0, after=psi)
    summed = rest("others", own(True, psi), [], others)
    t, unit = rest("first", summed, first, [])
    rows_in_share = width // parts + (2 * TILE if carried else 0)
    w_1, share_1, rows = call(
        functools.partial(first_sums_kernel, width // parts),
        "sums",
        (narrow, jax.ShapeDtypeStruct((rows_in_share, width), jnp.bfloat16), rows_shape),
        (*gather_parts(t), psi, unit),
    )
    first, others, rows = spread(w_1, share_1, rows)
    t, unit, rows = rest("rest", own(True, w_1), first, others, rows)
    rows = add_round(rows, *rounds[-1])
    w_wide, w_2, share_2, v_2, scal = call(
        functools.partial(second_sums_kernel, entries),
        "sums",
        (wide, narrow, share_shape, narrow, scalars),
        (*gather_parts(t), rows, psi, w_1, unit),
    )
    first, others, _ = spread(w_2, share_2)
    (t,) = rest("rest", own(False, w_2), first, others)
    r, z, rows = call(
        third_sums_kernel,
        "sums",
        (wide, wide, rows_shape),
        (*gather_parts(t), psi, w_1, v_2, w_wide, scal),
        limit=8,
    )
    return call(
        functools.partial(final_kernel, entries),
        "final",
        (
            jax.ShapeDtypeStruct((STEPS, 1, width // parts, width), jnp.bfloat16),
            jax.ShapeDtypeStruct((2, STEPS), jnp.float32),
        ),
        (exchange(rows), r, z, w_wide, v_2, scal),
    )


def solution(mesh):
    return jax.shard_map(
        shards,
        mesh=mesh,
        in_specs=(
            P(("groups", "blk", "rep"), None, None),
            P("mpo", ("groups", "blk", "rep"), None, None),
            P("mpo", ("groups", "blk", "rep"), None, None),
            P("mpo"),
        ),
        out_specs=(P(None, ("groups", "blk", "rep"), "mpo", None), P("groups", None)),
        check_vma=False,
    )
```

```python
import functools

import jax
import jax.numpy as jnp
from jax import lax
from jax.experimental import pallas as pl
from jax.experimental.pallas import tpu as pltpu
from jax.sharding import PartitionSpec as P

NS = 4
STEPS = 3
OFFSETS = (0, NS + 1, NS - 1, -(NS + 1), -(NS - 1))
EPSILON = 1e-06
WIDE, WIDEST = 8, 16
SMALLEST = 1e-30
TILE = 16
MIB = 1024 * 1024
VMEM = pl.BlockSpec(memory_space=pltpu.VMEM)
SMEM = pl.BlockSpec(memory_space=pltpu.SMEM)


def reaches(kind, sector, blocks):
    source = sector - OFFSETS[kind]
    spin = sector % NS
    inside = (source >= 0) & (source < blocks)
    if kind in (1, 4):
        return inside & (spin >= 1)
    if kind in (2, 3):
        return inside & (spin <= NS - 2)
    return inside


def routes(blocks):
    degree, edges = [0] * blocks, []
    for kind in (1, 2):
        for k in range(blocks):
            if reaches(kind, k, blocks):
                edges.append((k - OFFSETS[kind], k))
                degree[k - OFFSETS[kind]] += 1
                degree[k] += 1
    edges.sort(key=lambda edge: degree[edge[0]] + degree[edge[1]])
    partner = [{} for _ in range(blocks)]

    def lowest(block):
        return next(c for c in range(len(edges)) if c not in partner[block])

    for a, b in edges:
        here_free, there_free = lowest(a), lowest(b)
        if here_free in partner[b]:
            path, block, colour = [b], b, here_free
            while colour in partner[block]:
                block = partner[block][colour]
                path.append(block)
                colour = there_free if colour == here_free else here_free
            for block in path:
                moved = {}
                for old, new in ((here_free, there_free), (there_free, here_free)):
                    if old in partner[block]:
                        moved[new] = partner[block].pop(old)
                partner[block].update(moved)
        partner[a][here_free], partner[b][here_free] = b, a
    colours = sorted({c for held in partner for c in held})
    permutes = [[(held[c], k) for k, held in enumerate(partner) if c in held] for c in colours]
    return sorted(permutes, key=len, reverse=True)


def slot_tables(permutes, blocks):
    origins = [{k: k for k in range(blocks)}] + [{k: s for s, k in pairs} for pairs in permutes]
    places = []
    for kind in range(5):
        place = {}
        for slot, origin in enumerate(origins):
            for k, source in origin.items():
                if source == k - OFFSETS[kind] and reaches(kind, k, blocks):
                    place[k] = slot
        places.append(place)
    return places, origins


def carried_rounds(permutes, blocks):
    if not permutes or blocks % 4:
        return None
    rounds = [dict(permutes[0])] + [{k: k ^ bit for k in range(blocks)} for bit in (1, 2)]
    held = [{k} for k in range(blocks)]
    for pairs in rounds:
        if sorted(pairs.values()) != list(range(blocks)):
            return None
        if any(held[source] & held[k] for source, k in pairs.items()):
            return None
        grown = list(held)
        for source, k in pairs.items():
            grown[k] = held[k] | held[source]
        held = grown
    if any(len(rows) < blocks for rows in held):
        return None
    return [sorted(pairs.items()) for pairs in rounds[1:]]


def look_up(table, sector, default):
    out = jnp.int32(default)
    for k, value in table.items():
        if value != default:
            out = jnp.where(sector == k, jnp.int32(value), out)
    return out


def here():
    return lax.axis_index("blk") * lax.axis_size("rep") + lax.axis_index("rep")


def lane_of(rows, lane):
    return rows[:, lane : lane + 1]


def pack(values, shape):
    lanes = lax.broadcasted_iota(jnp.int32, shape, 1)
    out = jnp.zeros(shape, jnp.float32)
    for place, value in enumerate(values):
        out = jnp.where(lanes == place, value, out)
    return out


def total(x):
    return jnp.sum(jnp.sum(x, axis=0, keepdims=True), axis=1, keepdims=True)


def column_sum(x):
    return jnp.sum(x, axis=0, keepdims=True)


def peak(x):
    return jnp.max(jnp.max(jnp.abs(x), axis=0, keepdims=True), axis=1, keepdims=True)


def wide_float(ref):
    return ref[...].astype(jnp.float32)


def sum_parts(parts):
    w = wide_float(parts[0])
    for part in parts[1:]:
        w += wide_float(part)
    return w


def first_row(ref):
    return ref[0:1, :]


def list_channels(which, places, kinds_ref, order, slot_of, idle):
    sector = here()
    low, high = {"own": (0, 0), "rest": (1, idle), "first": (1, 1), "others": (2, idle)}[which]
    slots = []
    for place in places:
        kept = {k: slot for k, slot in place.items() if low <= slot <= high}
        slots.append(look_up(kept, sector, -1))
    count = jnp.int32(0)
    for b in range(kinds_ref.shape[0]):
        kind = kinds_ref[b]
        slot = slots[0]
        for c in range(1, 5):
            slot = jnp.where(kind == c, slots[c], slot)
        order[count] = jnp.int32(b)
        slot_of[count] = slot
        count += jnp.where(slot >= 0, 1, 0)
    for extra in range(WIDEST):
        order[count + extra] = jnp.int32(0)
        slot_of[count + extra] = jnp.int32(idle)
    return count


def multiply_listed(count, size, left_ref, right_ref, source, acc, order, slot_of):
    def multiply(start, wide):
        held = [order[start + inner] for inner in range(wide)]
        pieces = [
            jnp.dot(
                left_ref[b], source[slot_of[start + inner]], preferred_element_type=jnp.float32
            ).astype(jnp.bfloat16)
            for inner, b in enumerate(held)
        ]
        acc[...] += lax.dot_general(
            jnp.concatenate(pieces, axis=1),
            jnp.concatenate([right_ref[b] for b in held], axis=1),
            (((1,), (1,)), ((), ())),
            preferred_element_type=jnp.float32,
        )

    def full(group, carry):
        multiply(group * size, size)
        return carry

    smaller = [wide for wide in (2, 4, 8, 12) if wide < size]
    groups = (count + size - 1 - smaller[-1]) // size
    lax.fori_loop(0, groups, full, 0)
    rest = count - groups * size
    for low, wide in zip([0] + smaller, smaller):

        @pl.when((rest > low) & (rest <= wide))
        def _():
            multiply(groups * size, wide)


def own_kernel(scaled, places, *refs):
    kinds_ref, left_ref, right_ref, block_ref, acc = refs[:5]
    source, order, slot_of = refs[-3:]
    count = list_channels("own", places, kinds_ref, order, slot_of, 1)
    if scaled:
        block = wide_float(block_ref)
        unit = jnp.maximum(peak(block), SMALLEST)
        refs[5][...] = jnp.broadcast_to(unit, refs[5].shape)
        source[0] = (block * (1.0 / unit)).astype(jnp.bfloat16)
    else:
        source[0] = block_ref[...]
    source[1] = jnp.zeros(source.shape[1:], jnp.bfloat16)
    acc[...] = jnp.zeros_like(acc)
    multiply_listed(count, WIDE, left_ref, right_ref, source, acc, order, slot_of)


def rest_kernel(which, scaled, passes, shares, slots, places, *refs):
    kinds_ref, left_ref, right_ref, own_ref = refs[:4]
    refs = refs[4:]
    if scaled:
        met_ref, refs = refs[0], refs[1:]
    first, refs = refs[:shares], refs[shares:]
    count_others = 0 if which == "first" else slots - 2
    others, refs = refs[:count_others], refs[count_others:]
    if passes:
        rows_ref, refs = refs[0], refs[1:]
    t_ref, refs = refs[0], refs[1:]
    if scaled:
        unit_ref, refs = refs[0], refs[1:]
    if passes:
        refs[0][...] = rows_ref[...]
        refs = refs[1:]
    acc, source, order, slot_of = refs
    count = list_channels(which, places, kinds_ref, order, slot_of, slots)
    if scaled:
        met = lane_of(first_row(met_ref), 0)
        unit = met
        for block in (*first, *others):
            unit = jnp.maximum(unit, peak(wide_float(block)))
        unit_ref[...] = jnp.broadcast_to(unit, unit_ref.shape)
        inverse = 1.0 / unit

    def scale(block):
        return (wide_float(block) * inverse).astype(jnp.bfloat16) if scaled else block[...]

    for step, block in enumerate(first):
        share = source.shape[1] // shares
        at = 0 if shares == 1 else jnp.abs(step - lax.axis_index("mpo"))
        source[1, pl.ds(pl.multiple_of(at * share, share), share), :] = scale(block)
    for slot, block in enumerate(others, 2):
        source[slot] = scale(block)
    source[slots] = jnp.zeros(source.shape[1:], jnp.bfloat16)
    acc[...] = own_ref[...] * (met * inverse) if scaled else own_ref[...]
    multiply_listed(count, WIDEST if which == "rest" else WIDE, left_ref, right_ref, source, acc, order, slot_of)
    t_ref[...] = acc[...].astype(t_ref.dtype)


def pass_kernel(block_ref, rows_ref, out_ref):
    out_ref[...] = block_ref[...]


def unpack_kernel(origin, block_ref, rows_ref, out_ref, sums_ref):
    share = out_ref.shape[0]
    out_ref[...] = block_ref[0:share, :]
    terms = block_ref[share : share + 2 * TILE, :].astype(jnp.float32)
    sums = terms[0:TILE, 0:128] + terms[0:TILE, 128:256] + terms[TILE : 2 * TILE, 0:128]
    row = lax.broadcasted_iota(jnp.int32, rows_ref.shape, 0)
    source = look_up(origin, here(), 0)
    sums_ref[...] = jnp.where(row == source, first_row(sums), rows_ref[...])


def take_kernel(block_ref, copy_ref, share_ref):
    copy_ref[...] = block_ref[...]
    share_ref[...] = block_ref[my_rows(share_ref.shape[0]), :]


def my_rows(share):
    return pl.ds(pl.multiple_of(lax.axis_index("mpo") * share, share), share)


def first_sums_kernel(share, *refs):
    parts, (psi_ref, unit_ref, w_ref, share_ref, rows_ref) = refs[:-5], refs[-5:]
    w = sum_parts(parts)
    unit = lane_of(first_row(unit_ref), 0)
    w_ref[...] = (w * unit).astype(jnp.bfloat16)
    share_ref[0:share, :] = w_ref[my_rows(share), :]
    v = wide_float(psi_ref) * (1.0 / unit)
    a = total(v * w)
    d = total(v * v)
    local = a / jnp.maximum(d, SMALLEST)
    r = w - local * v
    values = [a, d, local, total(r * v), total(r * r), unit]
    if share_ref.shape[0] > share:
        sums = pack(values, (TILE, 128))
        high = sums.astype(jnp.bfloat16)
        rest = sums - high.astype(jnp.float32)
        middle = rest.astype(jnp.bfloat16)
        low = (rest - middle.astype(jnp.float32)).astype(jnp.bfloat16)
        blank = jnp.zeros((2 * TILE, share_ref.shape[1]), jnp.bfloat16)
        share_ref[share : share + 2 * TILE, :] = blank
        share_ref[share : share + TILE, 0:128] = high
        share_ref[share : share + TILE, 128:256] = middle
        share_ref[share + TILE : share + 2 * TILE, 0:128] = low
        sums = high.astype(jnp.float32) + middle.astype(jnp.float32) + low.astype(jnp.float32)
        sums = jnp.broadcast_to(first_row(sums), rows_ref.shape)
    else:
        sums = pack(values, rows_ref.shape)
    row = lax.broadcasted_iota(jnp.int32, rows_ref.shape, 0)
    rows_ref[...] = jnp.where(row == here(), sums, 0.0)


def shrink(scal):
    return 1.0 / (jnp.abs(lane_of(scal, 0)) + lane_of(scal, 1))


def second_sums_kernel(entries, *refs):
    parts, refs = refs[:-9], refs[-9:]
    rows_ref, psi_ref, first_ref, unit_ref, wide_ref, w_ref, share_ref, v_ref, scal_ref = refs
    rows = rows_ref[...]
    a, d, local, p, q, unit = (lane_of(rows, lane) for lane in range(6))
    beta_0 = jnp.sqrt(column_sum(unit * unit * d) / entries + EPSILON)
    start_inverse = 1.0 / beta_0
    gain = unit * start_inverse
    alpha = column_sum(gain * (gain * a)) / entries
    off = local - alpha
    square = column_sum(gain * (gain * (q + off * (2.0 * p + off * d))))
    beta = jnp.sqrt(jnp.maximum(square, 0.0) / entries + EPSILON)
    inverse = 1.0 / beta
    scal = pack([alpha, beta, start_inverse], scal_ref.shape)
    scal_ref[...] = scal
    image = wide_float(first_ref) * start_inverse
    v_ref[...] = ((image - (alpha * start_inverse) * wide_float(psi_ref)) * inverse).astype(jnp.bfloat16)
    lift = lane_of(first_row(unit_ref), 0) * start_inverse
    w = (sum_parts(parts) * lift - alpha * image) * (inverse * shrink(first_row(scal)))
    wide_ref[...] = w
    w_ref[...] = w.astype(jnp.bfloat16)
    share_ref[...] = w_ref[my_rows(share_ref.shape[0]), :]


def third_sums_kernel(*refs):
    parts, refs = refs[:-8], refs[-8:]
    psi_ref, first_ref, v_ref, w_ref, scal_ref, r_ref, z_ref, rows_ref = refs
    scal = first_row(scal_ref)
    scale = shrink(scal)
    push = scale * lane_of(scal, 1) * lane_of(scal, 2)
    v, w = wide_float(v_ref), w_ref[...]
    vv, vw = total(v * v), total(v * w)
    local = vw / jnp.maximum(vv, SMALLEST)
    r = w - local * v - push * wide_float(psi_ref)
    z = sum_parts(parts) - (local / scale) * w - push * wide_float(first_ref)
    r_ref[...] = r
    z_ref[...] = z
    sums = [total(r * r), total(r * v), total(r * z), total(r * w)]
    sums += [total(z * v), total(z * w), total(z * z), total(w * w)]
    rows_ref[...] = pack([vv, vw, local] + sums, rows_ref.shape)


def final_kernel(entries, rows_ref, r_ref, z_ref, w_ref, v_ref, scal_ref, basis_ref, coef_ref):
    share = basis_ref.shape[2]
    mine = my_rows(share)
    vv, vw, local, rr, rv, rz, rw, zv, zw, zz, ww = (lane_of(rows_ref[...], i) for i in range(11))
    scal = first_row(scal_ref)
    scale = shrink(scal)
    inverse_scale = 1.0 / scale
    alpha_scaled = column_sum(vw) / entries
    off = local - alpha_scaled
    lift = off * inverse_scale
    square = column_sum(rr + off * (2.0 * rv + off * vv)) / entries
    beta_scaled = jnp.sqrt(jnp.maximum(square, 0.0) + scale * scale * EPSILON)
    inverse = 1.0 / beta_scaled
    mixed = column_sum(rz + lift * rw + off * (zv + lift * vw)) / entries
    alpha_3 = mixed * inverse * inverse
    r_v = column_sum(rv + off * vv) / entries
    z_v = column_sum(zv + lift * vw) / entries
    z_z = column_sum(zz + lift * (2.0 * zw + lift * ww)) / entries
    v_v = column_sum(vv) / entries
    beta_2 = beta_scaled * inverse_scale
    third = (z_z - 2.0 * alpha_3 * mixed + alpha_3 * alpha_3 * square) * inverse * inverse
    third += beta_2 * (beta_2 * v_v - 2.0 * inverse * (z_v - alpha_3 * r_v))
    beta_3 = jnp.sqrt(jnp.maximum(third, 0.0) + EPSILON)

    sector = here()
    row_of = lax.broadcasted_iota(jnp.int32, off.shape, 0)
    off_here = column_sum(jnp.where(row_of == sector, off, 0.0))
    v = v_ref[mine, :]
    v_wide = v.astype(jnp.float32)
    v_3 = (r_ref[mine, :] + off_here * v_wide) * inverse
    image = (z_ref[mine, :] + (off_here * inverse_scale) * w_ref[mine, :]) * inverse
    basis_ref[0, 0] = v
    basis_ref[1, 0] = v_3.astype(jnp.bfloat16)
    residual = image - alpha_3 * v_3 - beta_2 * v_wide
    basis_ref[2, 0] = (residual * (1.0 / beta_3)).astype(jnp.bfloat16)

    row = lax.broadcasted_iota(jnp.int32, coef_ref.shape, 0)
    column = lax.broadcasted_iota(jnp.int32, coef_ref.shape, 1)
    out = jnp.zeros(coef_ref.shape, jnp.float32)
    pairs = [(lane_of(scal, 0), lane_of(scal, 1)), (alpha_scaled * inverse_scale, beta_2), (alpha_3, beta_3)]
    for step, (a, b) in enumerate(pairs):
        out = jnp.where(column == step, jnp.where(row == 0, a, b), out)
    coef_ref[...] = out


def shards(wavefunction, env_left, env_right, channel_class):
    width = wavefunction.shape[1]
    ring = ("blk", "rep")
    parts = lax.axis_size("mpo")
    blocks = lax.axis_size("blk") * lax.axis_size("rep")
    entries = blocks * width * width
    permutes = routes(blocks)
    places, origins = slot_tables(permutes, blocks)
    slots = 1 + len(permutes)
    channels = channel_class.shape[0]
    psi, left, right = wavefunction[0], env_left[:, 0], env_right[:, 0]
    rows_shape = jax.ShapeDtypeStruct((blocks, 128), jnp.float32)
    scalars = jax.ShapeDtypeStruct((8, 128), jnp.float32)
    wide = jax.ShapeDtypeStruct((width, width), jnp.float32)
    narrow = jax.ShapeDtypeStruct((width, width), jnp.bfloat16)
    share_shape = jax.ShapeDtypeStruct((width // parts, width), jnp.bfloat16)
    lists = [pltpu.SMEM((channels + WIDEST,), jnp.int32)] * 2

    def call(kernel, name, outs, args, scratch=(), share=0, limit=4, weight=0):
        flops = int(4 * channels * max(share, weight) * width**3)
        cost = pl.CostEstimate(flops=flops, bytes_accessed=4 * width * width, transcendentals=0)
        listed = outs if isinstance(outs, tuple) else (outs,)
        first = SMEM if share else VMEM
        return pl.pallas_call(
            kernel,
            out_shape=outs,
            in_specs=[first] + [VMEM] * (len(args) - 1),
            out_specs=tuple(VMEM for _ in listed) if isinstance(outs, tuple) else VMEM,
            scratch_shapes=list(scratch),
            compiler_params=pltpu.CompilerParams(vmem_limit_bytes=limit * MIB),
            cost_estimate=cost,
            name=name,
        )(*args)

    def sources(count):
        return pltpu.VMEM((count + 1, width, width), jnp.bfloat16)

    def own(scaled, block):
        return call(
            functools.partial(own_kernel, scaled, places),
            "own",
            (wide,) + (scalars,) * scaled,
            (channel_class, left, right, block),
            [sources(1)] + lists,
            0.2,
            16,
        )

    def rest(which, summed, first, others, rows=None):
        scaled, passes = len(summed) > 1, rows is not None
        outs = (wide if which == "others" else narrow,) + (scalars,) * scaled + (rows_shape,) * passes
        args = [channel_class, left, right, *summed] + first + others + [rows] * passes
        return call(
            functools.partial(rest_kernel, which, scaled, passes, len(first), slots, places),
            "rest",
            outs,
            args,
            [pltpu.VMEM((width, width), jnp.float32), sources(slots)] + lists,
            0.4 if which == "rest" else 0.2,
            16,
        )

    def shift(block, pairs):
        return lax.ppermute(block, ring, pairs)

    carried = carried_rounds(permutes, blocks)
    rounds = [(ring, pairs) for pairs in carried or []]
    for axis in () if carried else ("rep", "blk"):
        size = lax.axis_size(axis)
        bits = [1 << i for i in range(size.bit_length() - 1)]
        if sum(bits) == size - 1:
            rounds += [(axis, [(i, i ^ bit) for i in range(size)]) for bit in bits]
        else:
            rounds += [(axis, None)]

    def add_round(rows, axis, pairs):
        if pairs is None:
            return lax.psum(rows, axis)
        return rows + lax.ppermute(rows, axis, pairs)

    def spread(block, share, rows=None, after=None):
        piece = shift(share, permutes[0])
        if rows is not None and carried:
            piece, rows = call(
                functools.partial(unpack_kernel, origins[1]),
                "unpack",
                (share_shape, rows_shape),
                (piece, rows),
            )
            rows = add_round(rows, *rounds[0])
        elif rows is not None:
            for step in rounds[:-1]:
                rows = add_round(rows, *step)
            piece = call(pass_kernel, "hold", share_shape, (piece, rows))
        elif after is not None:
            piece = call(pass_kernel, "hold", share_shape, (piece, after), weight=0.5)
        if parts == 2:
            first = [piece, lax.ppermute(piece, "mpo", [(0, 1), (1, 0)])]
        else:
            first = [lax.all_gather(piece, "mpo", axis=0, tiled=True)]
        return first, [shift(block, pairs) for pairs in permutes[1:]], rows

    def gather_parts(t):
        if parts == 2:
            return [t, lax.ppermute(t, "mpo", [(0, 1), (1, 0)])]
        held = lax.all_gather(t, "mpo")
        return [held[i] for i in range(parts)]

    def exchange(rows):
        return lax.all_to_all(rows, ring, 0, 0, tiled=True)

    psi, share_0 = call(take_kernel, "take", (narrow, share_shape), (psi,), weight=2)
    first, others, _ = spread(psi, share_0, after=psi)
    summed = rest("others", own(True, psi), [], others)
    t, unit = rest("first", summed, first, [])
    rows_in_share = width // parts + (2 * TILE if carried else 0)
    w_1, share_1, rows = call(
        functools.partial(first_sums_kernel, width // parts),
        "sums",
        (narrow, jax.ShapeDtypeStruct((rows_in_share, width), jnp.bfloat16), rows_shape),
        (*gather_parts(t), psi, unit),
    )
    first, others, rows = spread(w_1, share_1, rows)
    t, unit, rows = rest("rest", own(True, w_1), first, others, rows)
    rows = add_round(rows, *rounds[-1])
    w_wide, w_2, share_2, v_2, scal = call(
        functools.partial(second_sums_kernel, entries),
        "sums",
        (wide, narrow, share_shape, narrow, scalars),
        (*gather_parts(t), rows, psi, w_1, unit),
    )
    first, others, _ = spread(w_2, share_2)
    (t,) = rest("rest", own(False, w_2), first, others)
    r, z, rows = call(
        third_sums_kernel,
        "sums",
        (wide, wide, rows_shape),
        (*gather_parts(t), psi, w_1, v_2, w_wide, scal),
        limit=8,
    )
    return call(
        functools.partial(final_kernel, entries),
        "final",
        (
            jax.ShapeDtypeStruct((STEPS, 1, width // parts, width), jnp.bfloat16),
            jax.ShapeDtypeStruct((2, STEPS), jnp.float32),
        ),
        (exchange(rows), r, z, w_wide, v_2, scal),
    )


def solution(mesh):
    return jax.shard_map(
        shards,
        mesh=mesh,
        in_specs=(
            P(("groups", "blk", "rep"), None, None),
            P("mpo", ("groups", "blk", "rep"), None, None),
            P("mpo", ("groups", "blk", "rep"), None, None),
            P("mpo"),
        ),
        out_specs=(P(None, ("groups", "blk", "rep"), "mpo", None), P("groups", None)),
        check_vma=False,
    )
```
